32 devices in a mesh: dp: 16 (over z, x, core), seq: 2 (over y).
Axes of the slice: x: 2, y: 2, z: 4, core: 2. Of those that a mesh axis runs over, the one named last changes fastest.
Arguments:
- tokens: bfloat16 [16, 1024, 1024], P('dp', 'seq'), may hold values from -6 to 6
- cotangent: bfloat16 [16, 1024, 1024], P('dp', 'seq'), may hold values from -6 to 6
- prefix: int32 [16], P('dp'), may hold values from 102 to 512, as said below
- attention_gain: float32 [1024], P(('dp', 'seq')), may hold values from 0.5 to 1.5
- query_weight: float32 [1024, 1024], P(('dp', 'seq')), may hold values from -0.375 to 0.375
- key_weight: float32 [1024, 128], P(('dp', 'seq')), may hold values from -0.1875 to 0.1875
- value_weight: float32 [1024, 128], P(('dp', 'seq')), may hold values from -0.1875 to 0.1875
- projection_weight: float32 [1024, 1024], P(None, ('dp', 'seq')), may hold values from -0.75 to 0.75
- feedforward_gain: float32 [1024], P(('dp', 'seq')), may hold values from 0.5 to 1.5
- up_weight: float32 [1024, 4096], P(('dp', 'seq')), may hold values from -0.1875 to 0.1875
- down_weight: float32 [4096, 1024], P(('dp', 'seq')), may hold values from -0.09375 to 0.09375
Outputs:
- layer_output: bfloat16 [16, 1024, 1024], P('dp', 'seq')
- input_grad: float32 [16, 1024, 1024], P('dp', 'seq')
- attention_gain_grad: float32 [1024], P(('dp', 'seq'))
- query_grad: float32 [1024, 1024], P(('dp', 'seq'))
- key_grad: float32 [1024, 128], P(('dp', 'seq'))
- value_grad: float32 [1024, 128], P(('dp', 'seq'))
- projection_grad: float32 [1024, 1024], P(None, ('dp', 'seq'))
- feedforward_gain_grad: float32 [1024], P(('dp', 'seq'))
- up_grad: float32 [1024, 4096], P(('dp', 'seq'))
- down_grad: float32 [4096, 1024], P(('dp', 'seq'))
The draws below stay inside these ranges and needn't reach their ends.
Inputs may be any that keep to these rules, and one draw needn't show every extreme that they name: `prefix`: some sequence has exactly 102 such positions and some exactly 512.
All inputs are finite; a program needn't handle non-finite values.
Results may differ from the reference program's by a relative error of at most 0.014.
The reference program's roundings to bfloat16 on the way count: a program that leaves them out, or rounds other values in their place, can miss the bound.
Values may be sent and summed in bfloat16 or wider, within the bound.
A program may use at most 192 MiB of HBM per device.

```python
import math
import jax
import jax.numpy as jnp
from jax import lax

D = 1024
H = 8
DH = 128
FF = 4096
SEQ_LEN = 1024
SEQS = 16


def draw_prefix(key, part):
    lowest = SEQ_LEN // 10
    highest = SEQ_LEN // 2
    drawn = jax.random.randint(key, (SEQS,), lowest, highest + 1)
    return drawn.at[0].set(highest).at[SEQS - 1].set(lowest).astype(jnp.int32)


def level_of(rng, shape, cuts, least, high):
    def one(position, parts):
        heights = jax.random.uniform(jax.random.fold_in(jax.random.fold_in(rng, 6), position), (parts,), jnp.float32, least / len(cuts), high / len(cuts))
        return jnp.repeat(jnp.exp(heights), shape[position] // parts).reshape((-1,) + (1,) * (len(shape) - position - 1))

    factor_of = one(*cuts[0])
    for cut in cuts[1:]:
        factor_of = factor_of * one(*cut)
    return factor_of


def centred(key, dims, width, reach, pieces=(), kind=jnp.bfloat16):
    values = jax.random.normal(key, dims, jnp.float32) * width
    if len(pieces) > 0:
        values = level_of(key, dims, pieces, -0.22, 0.18) * values
    return jnp.clip(values, min=-reach, max=reach).astype(kind)


def setup_inputs(seed: int = 0) -> dict:
    keys = jax.random.split(jax.random.key(seed), 12)
    tokens = centred(keys[0], (SEQS, SEQ_LEN, D), 1.0, 6.0, ((0, 16), (1, 2)))
    cotangent = centred(keys[1], (SEQS, SEQ_LEN, D), 1.0, 6.0, ((0, 16), (1, 2)))
    prefix = draw_prefix(jax.random.fold_in(keys[11], 71), 0)
    attention_gain = jnp.clip(1.0 + 0.1 * jax.random.normal(keys[3], (D,), jnp.float32), 0.5, 1.5)
    query_weight = centred(keys[4], (D, H * DH), (D // 4) ** -0.5, 0.375, ((0, 32),), jnp.float32)
    key_weight = centred(keys[5], (D, DH), D ** -0.5, 0.1875, ((0, 32),), jnp.float32)
    value_weight = centred(keys[6], (D, DH), D ** -0.5, 0.1875, ((0, 32),), jnp.float32)
    projection_weight = centred(keys[7], (H * DH, D), (H * DH // 16) ** -0.5, 0.75, ((1, 32),), jnp.float32)
    feedforward_gain = jnp.clip(1.0 + 0.1 * jax.random.normal(keys[8], (D,), jnp.float32), 0.5, 1.5)
    up_weight = centred(keys[9], (D, FF), D ** -0.5, 0.1875, ((0, 32),), jnp.float32)
    down_weight = centred(keys[10], (FF, D), FF ** -0.5, 0.09375, ((0, 32),), jnp.float32)
    return {"tokens": tokens, "cotangent": cotangent, "prefix": prefix, "attention_gain": attention_gain, "query_weight": query_weight, "key_weight": key_weight, "value_weight": value_weight, "projection_weight": projection_weight, "feedforward_gain": feedforward_gain, "up_weight": up_weight, "down_weight": down_weight}


epsilon = 1e-06
masked_score = -10000.0

@jax.custom_vjp
def low(v):
    return lax.optimization_barrier(v.astype(jnp.bfloat16)).astype(jnp.float32)

@jax.custom_vjp
def low_back(v):
    return v

def low_keep(v):
    return (low(v), None)

def low_pass(kept, grad):
    return (grad,)

def back_keep(v):
    return (v, None)

def back_low(kept, grad):
    return (low(grad),)
low.defvjp(low_keep, low_pass)
low_back.defvjp(back_keep, back_low)

def product(left, right):
    return jnp.dot(left, right, precision=lax.Precision.HIGHEST, preferred_element_type=jnp.float32)

def root_norm(values, gain):
    factor = lax.rsqrt(lax.optimization_barrier(jnp.mean(values * values, axis=-1, keepdims=True)) + epsilon)
    return values * factor * gain

def smooth_gate(values):
    return jax.nn.gelu(values, approximate=True)

def attend(queries, key_rows, value_rows, prefix_len):
    length = key_rows.shape[0]
    block_len = min(64, length)
    block_count = length // block_len
    score_scale = DH ** (-0.5)
    key_pos = jnp.arange(length, dtype=jnp.int32)
    limit = prefix_len.astype(jnp.int32)

    def score_block(query_block, first):
        positions = (first.astype(jnp.int32) + jnp.arange(block_len, dtype=jnp.int32)).astype(jnp.int32)
        scores = jnp.einsum('qhd,kd->qhk', query_block, key_rows, precision=lax.Precision.HIGHEST)
        scores = low_back(scores * score_scale)
        visible = (key_pos[None, :] <= positions[:, None]) | (key_pos[None, :] < limit)
        scores = jnp.where(visible[:, None, :], scores, jnp.full_like(scores, masked_score))
        chances = jax.nn.softmax(scores, axis=-1)
        return jnp.einsum('qhk,kd->qhd', low(chances), value_rows, precision=lax.Precision.HIGHEST)
    query_blocks = queries.reshape(block_count, block_len, H, DH)
    firsts = (jnp.arange(block_count, dtype=jnp.int32) * block_len).astype(jnp.int32)
    outputs = []
    checked = jax.checkpoint(score_block)
    for index in range(block_count):
        outputs.append(checked(query_blocks[index], firsts[index]))
    mixed = jnp.stack(outputs, axis=0)
    return mixed.reshape(length, H * DH)

def decoder_layer(inputs, prefix_len, weights):
    gain_one, query_weight, key_weight, value_weight, projection_weight, gain_two, up_weight, down_weight = weights
    normed = low(root_norm(inputs, low(gain_one)))
    queries = low_back(low(product(normed, low(query_weight))))
    key_rows = low_back(low(product(normed, low(key_weight))))
    value_rows = low_back(low(product(normed, low(value_weight))))
    mixed = low_back(low(attend(queries.reshape(-1, H, DH), key_rows, value_rows, prefix_len)))
    hidden = inputs + low_back(product(mixed, low(projection_weight)))
    normed_two = low(root_norm(hidden, low(gain_two)))
    before = low_back(product(normed_two, low(up_weight)))
    active = low(smooth_gate(before))
    return hidden + low_back(product(active, low(down_weight)))

def reference(tokens, cotangent, prefix, attention_gain, query_weight, key_weight, value_weight, projection_weight, feedforward_gain, up_weight, down_weight):
    weights = tuple((member.astype(jnp.float32) for member in (attention_gain, query_weight, key_weight, value_weight, projection_weight, feedforward_gain, up_weight, down_weight)))
    group_size = math.gcd(SEQS, max(1, 4096 // SEQ_LEN))
    rounds = SEQS // group_size
    inputs = tokens.astype(jnp.float32).reshape(rounds, group_size, SEQ_LEN, D)
    cotangents = cotangent.astype(jnp.float32).reshape(rounds, group_size, SEQ_LEN, D)
    limits = prefix.astype(jnp.int32).reshape(rounds, group_size)

    def advance(totals, members):
        input_part, cot_part, limit_part = members
        limit_int = limit_part.astype(jnp.int32)

        def forward(input_in, weight_in):
            return jax.vmap(decoder_layer, in_axes=(0, 0, None))(input_in, limit_int, weight_in)
        result, pullback = jax.vjp(forward, input_part, weights)
        grad_input, grad_weights = pullback(cot_part.astype(result.dtype))
        totals = jax.tree.map(lambda left, right: left + right.astype(left.dtype), totals, grad_weights)
        return (totals, (result.astype(jnp.bfloat16), grad_input.astype(jnp.float32)))
    initial = jax.tree.map(lambda member: jnp.zeros(member.shape, jnp.float32), weights)
    totals, (result, grad_input) = lax.scan(advance, initial, (inputs, cotangents, limits))
    return (result.reshape(SEQS, SEQ_LEN, D), grad_input.reshape(SEQS, SEQ_LEN, D), totals[0], totals[1], totals[2], totals[3], totals[4], totals[5], totals[6], totals[7])
```

```python
import functools
import jax
import jax.numpy as jnp
from jax import lax
from jax.experimental import pallas as pl
from jax.experimental.pallas import tpu as pltpu
from jax.sharding import PartitionSpec as P

H = 8
DH = 128
BF = jnp.bfloat16
F32 = jnp.float32
MESH = pl.DeviceIdType.MESH
VMEM_LIMIT = 61 * 2**20
GELU_C = 0.7978845608028654
GELU_A = 0.044715

epsilon = 1e-06
masked_score = -10000.0


def dot(left, right, left_dim, right_dim):
    return lax.dot_general(
        left, right, (((left_dim,), (right_dim,)), ((), ())), preferred_element_type=F32
    )


class Place:
    def __init__(self, send_sems, recv_sems, local_sems):
        dp = lax.axis_index("dp")
        self.y = lax.axis_index("seq")
        self.c = lax.rem(dp, 2)
        self.x = lax.rem(lax.div(dp, 2), 2)
        self.z = lax.div(dp, 4)
        self.send_sems, self.recv_sems, self.local_sems = send_sems, recv_sems, local_sems
        self.sent, self.n_local = [], 0
        self.xn = self.at(self.z, 1 - self.x, self.c, self.y)
        self.yn = self.at(self.z, self.x, self.c, 1 - self.y)
        self.cn = self.at(self.z, self.x, 1 - self.c, self.y)

    def at(self, z, x, c, y):
        return ((z * 2 + x) * 2 + c, y)

    def z_to(self, step):
        return lax.rem(self.z + step, 4)

    def zn(self, step):
        return self.at(self.z_to(step), self.x, self.c, self.y)

    def greet(self):
        barrier = pltpu.get_barrier_semaphore()
        for device in (self.cn, self.xn, self.yn, self.zn(1), self.zn(2), self.zn(3)):
            pl.semaphore_signal(barrier, inc=1, device_id=device, device_id_type=MESH)
        pl.semaphore_wait(barrier, 6)

    def send(self, src, dst, recv, device):
        copy = pltpu.make_async_remote_copy(
            src_ref=src,
            dst_ref=dst,
            send_sem=self.send_sems.at[len(self.sent)],
            recv_sem=self.recv_sems.at[recv],
            device_id=device,
            device_id_type=MESH,
        )
        copy.start()
        self.sent.append(copy)

    def arrived(self, dst, recv):
        pltpu.make_async_remote_copy(
            src_ref=dst,
            dst_ref=dst,
            send_sem=self.send_sems.at[0],
            recv_sem=self.recv_sems.at[recv],
            device_id=self.cn,
            device_id_type=MESH,
        ).wait_recv()

    def move(self, src, dst):
        copy = pltpu.make_async_copy(src, dst, self.local_sems.at[self.n_local])
        self.n_local += 1
        copy.start()
        return copy

    def finish(self):
        for copy in self.sent:
            copy.wait_send()


def gelu_parts(u):
    square = u * u
    t = jnp.tanh(GELU_C * u * (1.0 + GELU_A * square))
    half = 0.5 * (1.0 + t)
    slope = half + (0.5 * GELU_C) * u * (1.0 - t * t) * (1.0 + (3.0 * GELU_A) * square)
    return u * half, slope


PIECES = 10
STEPS = 8


def forward_kernel(
    prefix_ref, x_hbm, gy_hbm, wq_ref, wk_ref, wv_ref, wg_ref, wo_ref, w1_ref, w2_ref,
    out_hbm, w2_hbm, w1_hbm, wa_hbm, wot_hbm, gain_hbm, n1_hbm, q_hbm, kv_hbm, a_hbm, hidden_hbm,
    n2_hbm, slope_hbm, p_hbm, down_hbm,
    wa, wot, w1, w2, x, gy, n1, q, kv, a, hidden, n2, z, slope, p, bias, gain, down_out, down_in, out,
    send_sems, recv_sems, local_sems,
):
    me = Place(send_sems, recv_sems, local_sems)
    rows, width = x.shape
    load_x = me.move(x_hbm, x)
    load_gy = me.move(gy_hbm, gy)
    views = [wa, wot] + [w1.at[j] for j in range(4)] + [w2.at[k] for k in range(4)]
    saves = []

    def s0(i):
        for step in (1, 2, 3):
            mine = views[i].at[me.z, me.x, me.c, me.y]
            me.send(mine, mine, i * STEPS + step - 1, me.zn(step))

    def s1(i):
        for step in (1, 2, 3):
            me.arrived(views[i].at[me.z_to(4 - step), me.x, me.c, me.y], i * STEPS + step - 1)
        column = views[i].at[:, me.x, me.c, me.y]
        me.send(column, column, i * STEPS + 3, me.xn)
        me.send(column, column, i * STEPS + 4, me.yn)

    def s2(i):
        half = views[i].shape[4] // 2
        low, high = pl.ds(0, half), pl.ds(half, half)
        me.arrived(views[i].at[:, 1 - me.x, me.c, me.y], i * STEPS + 3)
        part = views[i].at[:, 1 - me.x, me.c, me.y, low]
        me.send(part, part, i * STEPS + 5, me.yn)
        me.arrived(views[i].at[:, me.x, me.c, 1 - me.y], i * STEPS + 4)
        part = views[i].at[:, me.x, me.c, 1 - me.y, high]
        me.send(part, part, i * STEPS + 6, me.xn)

    def s3(i):
        half = views[i].shape[4] // 2
        low, high = pl.ds(0, half), pl.ds(half, half)
        me.arrived(views[i].at[:, 1 - me.x, me.c, 1 - me.y, low], i * STEPS + 5)
        me.arrived(views[i].at[:, 1 - me.x, me.c, 1 - me.y, high], i * STEPS + 6)
        plane = views[i].at[:, :, me.c]
        me.send(plane, plane, i * STEPS + 7, me.cn)

    def s4(i):
        me.arrived(views[i].at[:, :, 1 - me.c], i * STEPS + 7)
        if i == 0:
            saves.append(me.move(wa, wa_hbm))
        elif i == 1:
            saves.append(me.move(wot, wot_hbm))
        elif i < 6:
            saves.append(me.move(w1.at[i - 2], w1_hbm.at[i - 2]))
        else:
            k = i - 6
            saves.append(me.move(w2.at[k], w2_hbm.at[:, :, :, :, :, pl.ds(256 * k, 256)]))

    done = set()

    def run(step, i):
        if 0 <= i < PIECES and (step, i) not in done:
            done.add((step, i))
            step(i)

    def poll(k):
        for step, i in ((s0, k + 3), (s1, k + 1), (s2, k), (s3, k - 1), (s4, k - 2)):
            run(step, i)

    own = (me.z, me.x, me.c, me.y)
    wa[(*own, slice(None), pl.ds(0, 1024))] = wq_ref[...].astype(BF)
    wa[(*own, slice(None), pl.ds(1024, 128))] = wk_ref[...].astype(BF)
    wa[(*own, slice(None), pl.ds(1152, 128))] = wv_ref[...].astype(BF)
    wa[(*own, slice(None), pl.ds(1280, 128))] = wg_ref[...]
    wot[own] = wo_ref[...]
    me.greet()
    run(s0, 0)
    run(s0, 1)
    for j in range(4):
        w1[(j, *own)] = w1_ref[:, pl.ds(1024 * j, 1024)].astype(BF)
    run(s0, 2)
    for k in range(4):
        w2[(k, *own)] = w2_ref[:, pl.ds(256 * k, 256)].astype(BF)

    first = me.y * rows

    @pl.loop(0, rows // 64)
    def _(t):
        at = pl.multiple_of(t * 64, 64)
        query_pos = first + at + lax.broadcasted_iota(jnp.int32, (64, 2 * rows), 0)
        key_pos = lax.broadcasted_iota(jnp.int32, (64, 2 * rows), 1)
        visible = (key_pos <= query_pos) | (key_pos < prefix_ref[0])
        bias[pl.ds(at, 64), :] = jnp.where(visible, 0.0, -1e30)

    run(s1, 0)
    load_x.wait()
    load_gy.wait()
    poll(0)
    poll(1)
    run(s4, 0)

    for kind in (0, 1):
        for zi in range(4):
            for xi in range(2):
                tile = jnp.zeros((16, 128), F32)
                for ci in range(2):
                    for yi in range(2):
                        tile += wa[zi, xi, ci, yi, pl.ds(16 * kind, 16), pl.ds(1280, 128)].astype(F32)
                gain[kind, :, pl.ds(128 * (2 * zi + xi), 128)] = tile[:8]
    saves.append(me.move(gain, gain_hbm))

    @pl.loop(0, rows // 64)
    def _(t):
        r = pl.ds(pl.multiple_of(t * 64, 64), 64)
        values = x[r, :].astype(F32)
        factor = lax.rsqrt(jnp.mean(values * values, axis=-1, keepdims=True) + epsilon)
        n1[r, :] = (values * factor * gain[0, 0:1, :]).astype(BF)

    kv[me.y] = dot(
        n1[...], wa[:, :, :, :, :, pl.ds(1024, 256)].reshape(width, 256), 1, 0
    ).astype(BF)
    mine = kv.at[me.y]
    me.send(mine, mine, PIECES * STEPS, me.yn)

    @pl.loop(0, 2)
    def _(i):
        cols = pl.ds(pl.multiple_of(i * 512, 512), 512)
        q[:, cols] = dot(n1[...], wa[:, :, :, :, :, cols].reshape(width, 512), 1, 0).astype(BF)

    saves.append(me.move(n1, n1_hbm))
    saves.append(me.move(q, q_hbm))
    me.arrived(kv.at[1 - me.y], PIECES * STEPS)
    saves.append(me.move(kv, kv_hbm))
    length = 2 * rows
    to_log2 = (DH ** -0.5) * 1.4426950408889634

    def heads(g):
        @pl.loop(0, 2)
        def _(hh):
            cols = pl.ds(pl.multiple_of((2 * g + hh) * DH, DH), DH)
            keys = kv[:, :, pl.ds(0, DH)].reshape(length, DH)
            vals = kv[:, :, pl.ds(DH, DH)].reshape(length, DH)
            for t in range(rows // 256):
                r = pl.ds(256 * t, 256)
                s = dot(q[r, cols], keys, 1, 1) * to_log2 + bias[r, :]
                e = jnp.exp2(s - jnp.max(s, axis=-1, keepdims=True))
                chances = (e * (1.0 / jnp.sum(e, axis=-1, keepdims=True))).astype(BF)
                p[g % 2, pl.ds(pl.multiple_of(hh * rows + 256 * t, 256), 256), :] = chances
                a[r, cols] = dot(chances, vals, 1, 0).astype(BF)

    p_saves = []
    for g in range(4):
        if g >= 2:
            p_saves[g - 2].wait()
        heads(g)
        p_saves.append(me.move(p.at[g % 2], p_hbm.at[g]))
        if g in (0, 2):
            poll(2 + g // 2)
    saves.extend(p_saves[2:])
    saves.append(me.move(a, a_hbm))

    for i in range(2):
        cols = pl.ds(512 * i, 512)
        weight = wot[pl.ds(2 * i, 2)].reshape(512, width)
        hidden[:, cols] = x[:, cols].astype(F32) + dot(a[...], weight, 1, 1)
    poll(4)

    @pl.loop(0, rows // 64)
    def _(t):
        r = pl.ds(pl.multiple_of(t * 64, 64), 64)
        values = hidden[r, :]
        factor = lax.rsqrt(jnp.mean(values * values, axis=-1, keepdims=True) + epsilon)
        n2[r, :] = (values * factor * gain[1, 0:1, :]).astype(BF)

    saves.append(me.move(hidden, hidden_hbm))
    saves.append(me.move(n2, n2_hbm))

    def up(j):
        @pl.loop(0, 2)
        def _(i):
            cols = pl.ds(pl.multiple_of(i * 512, 512), 512)
            to = pl.ds(pl.multiple_of(j * 1024 + i * 512, 512), 512)
            u = dot(n2[...], w1[j, :, :, :, :, :, cols].reshape(width, 512), 1, 0)
            active, steep = gelu_parts(u)
            z[:, to] = active.astype(BF)
            slope[:, to] = steep.astype(BF)

    up(0)
    poll(5)
    up(1)
    poll(6)
    up(2)
    poll(7)
    up(3)
    saves.append(me.move(slope, slope_hbm))

    @pl.loop(0, 8)
    def _(t):
        cols = pl.ds(pl.multiple_of((2 * t + 1 - me.c) * 256, 256), 256)
        down_out[t] = dot(z[:, cols], gy[...], 0, 0).astype(BF)

    me.send(down_out, down_in, PIECES * STEPS + 1, me.cn)
    poll(8)

    def down(k):
        cols = pl.ds(256 * k, 256)
        for t in range(2):
            r = pl.ds(256 * t, 256)
            y = dot(z[r, :], w2[k].reshape(4096, 256), 1, 0)
            out[r, cols] = (hidden[r, cols] + y).astype(BF)

    down(0)
    me.arrived(down_in, PIECES * STEPS + 1)

    @pl.loop(0, 8)
    def _(t):
        cols = pl.ds(pl.multiple_of((2 * t + me.c) * 256, 256), 256)
        down_in[t] = (dot(z[:, cols], gy[...], 0, 0) + down_in[t].astype(F32)).astype(BF)

    saves.append(me.move(down_in, down_hbm))
    poll(9)
    down(1)
    poll(10)
    down(2)
    poll(11)
    down(3)
    saves.append(me.move(out, out_hbm))
    for copy in saves:
        copy.wait()
    me.finish()


def backward_kernel(
    x_hbm, gy_hbm, gain_hbm, w2_hbm, w1_hbm, wa_hbm, wot_hbm, n1_hbm, q_hbm, kv_hbm, a_hbm, hidden_hbm,
    n2_hbm, slope_hbm, p_hbm, down_hbm,
    grad_x_hbm, g2_ref, g1_ref, go_ref, ga_ref,
    gy, n2, hidden, gn, a, q, kv, gain, wbuf, gu, wkv, att, sums, kvsum, kvout, kvin,
    down, pup, pproj, patt, pair_up, pair_att, dx2, dy2, dx1, dy1, dxa, dya, x2, y2, x1, y1, xa, ya, z2, z1, za,
    send_sems, recv_sems, local_sems,
):
    me = Place(send_sems, recv_sems, local_sems)
    rows, width = gy.shape
    length = 2 * rows
    load_down = [
        me.move(down_hbm.at[:, :, :, :, pl.ds(256 * k, 256)], down.at[:, :, :, :, pl.ds(256 * k, 256)])
        for k in range(4)
    ]
    load_gy = me.move(gy_hbm, gy)
    load_w2 = [me.move(w2_hbm.at[j], wbuf.at[j]) for j in range(2)]
    load_slope = [me.move(slope_hbm.at[:, pl.ds(1024 * j, 1024)], gu.at[j]) for j in range(2)]
    load_n2 = me.move(n2_hbm, n2)
    load_w1 = [me.move(w1_hbm.at[j], wbuf.at[2 + j]) for j in range(2)]
    load_rest = [
        me.move(src, dst)
        for src, dst in (
            (hidden_hbm, hidden), (gain_hbm, gain), (a_hbm, a), (q_hbm, q), (kv_hbm, kv),
            (wa_hbm.at[:, pl.ds(1024, 256)], wkv),
        )
    ]

    def partial(i, zi, xi, yi, r):
        if i < 4:
            return down.at[zi, xi, yi, r, pl.ds(256 * i, 256)]
        if i < 8:
            return pup.at[i - 4, zi, xi, me.c, yi, r]
        return (pproj if i == 8 else patt).at[zi, xi, me.c, yi, r]

    def group(i, two, one, att_ref):
        return two.at[i] if i < 4 else one.at[i - 4] if i < 9 else att_ref

    def half_of(i):
        return 64 if i < 4 else 16

    every = slice(None)

    def t0(i):
        source = pup.at[i - 4] if i < 8 else pproj if i == 8 else patt
        to = pair_up.at[i - 4] if i < 9 else pair_att
        me.send(source.at[:, :, 1 - me.c], to, i * STEPS, me.cn)

    def t1(i):
        half = half_of(i)
        low, high = pl.ds(0, half), pl.ds(half, half)
        if i < 4:
            load_down[i].wait()
        else:
            source = pup.at[i - 4] if i < 8 else pproj if i == 8 else patt
            to = pair_up.at[i - 4] if i < 9 else pair_att
            me.arrived(to, i * STEPS)

            @pl.loop(0, 4)
            def _(zi):
                for xi in range(2):
                    source[zi, xi, me.c] = source[zi, xi, me.c] + to[zi, xi]

        me.send(partial(i, every, 1 - me.x, 1 - me.y, low), group(i, dy2, dy1, dya), i * STEPS + 1, me.yn)
        me.send(partial(i, every, 1 - me.x, 1 - me.y, high), group(i, dx2, dx1, dxa), i * STEPS + 2, me.xn)

    def t2(i):
        half = half_of(i)
        for came, recv, xi, yi, r, device, to, out_recv in (
            (group(i, dy2, dy1, dya), 1, 1 - me.x, me.y, pl.ds(0, half), me.xn, group(i, x2, x1, xa), 3),
            (group(i, dx2, dx1, dxa), 2, me.x, 1 - me.y, pl.ds(half, half), me.yn, group(i, y2, y1, ya), 4),
        ):
            me.arrived(came, i * STEPS + recv)
            for zi in range(4):
                mine = partial(i, zi, xi, yi, r)
                mine[...] = mine[...] + came[zi]
            me.send(partial(i, every, xi, yi, pl.ds(0, 2 * half)), to, i * STEPS + out_recv, device)

    def t3(i):
        half = half_of(i)
        whole = pl.ds(0, 2 * half)
        from_x, from_y = group(i, x2, x1, xa), group(i, y2, y1, ya)
        me.arrived(from_x, i * STEPS + 3)
        me.arrived(from_y, i * STEPS + 4)
        for zi in range(4):
            mine = partial(i, zi, me.x, me.y, whole)
            total = mine[...].astype(F32) + from_x[zi].astype(F32) + from_y[zi].astype(F32)
            mine[...] = total.astype(BF)
        for step in (1, 2, 3):
            to = group(i, z2, z1, za).at[step - 1]
            me.send(partial(i, me.z_to(step), me.x, me.y, whole), to, i * STEPS + 4 + step, me.zn(step))

    def t4(i):
        came = group(i, z2, z1, za)
        total = partial(i, me.z, me.x, me.y, pl.ds(0, 2 * half_of(i)))[...].astype(F32)
        for step in (1, 2, 3):
            me.arrived(came.at[step - 1], i * STEPS + 4 + step)
            total += came[step - 1].astype(F32)
        if i < 4:
            g2_ref[:, pl.ds(256 * i, 256)] = total
        elif i < 8:
            g1_ref[:, pl.ds(1024 * (i - 4), 1024)] = total
        elif i == 8:
            go_ref[...] = total
        else:
            ga_ref[...] = total

    def poll(k):
        for step, i in ((t1, k + 1), (t2, k), (t3, k - 1), (t4, k - 2)):
            if 0 <= i < PIECES:
                step(i)

    me.greet()
    poll(-1)

    def feed_forward(j):
        slot = j % 2
        load_w2[j].wait()
        load_slope[j].wait()
        for i in range(2):
            cols = pl.ds(512 * i, 512)
            grad_active = dot(gy[...], wbuf[slot, cols, :], 1, 1)
            gu[slot, :, cols] = (grad_active * gu[slot, :, cols].astype(F32)).astype(BF)
        if j < 2:
            load_w2.append(me.move(w2_hbm.at[j + 2], wbuf.at[slot]))
        elif j == 2:
            load_w2.append(me.move(wot_hbm, wbuf.at[0]))
        else:
            load_w2.append(me.move(p_hbm.at[1], wbuf.at[1]))
        for i in range(2):
            term = dot(n2[:, pl.ds(512 * i, 512)], gu[slot], 0, 0)
            pup[j, pl.ds(2 * i, 2)] = term.reshape(2, 2, 2, 2, 32, 1024).astype(BF)
        t0(4 + j)
        load_w1[j].wait()
        for i in range(2):
            cols = pl.ds(512 * i, 512)
            term = dot(gu[slot], wbuf[2 + slot, cols, :], 1, 1)
            if j == 0:
                gn[:, cols] = term
            else:
                gn[:, cols] = gn[:, cols] + term
        if j < 2:
            load_slope.append(me.move(slope_hbm.at[:, pl.ds(1024 * (j + 2), 1024)], gu.at[slot]))
            load_w1.append(me.move(w1_hbm.at[j + 2], wbuf.at[2 + slot]))
        else:
            load_w1.append(me.move(p_hbm.at[(0, 2)[j - 2]], wbuf.at[2 + slot]))

    load_gy.wait()
    load_n2.wait()
    feed_forward(0)
    poll(0)
    feed_forward(1)
    poll(1)
    feed_forward(2)
    poll(2)
    feed_forward(3)
    load_x = me.move(x_hbm, n2)
    for copy in load_rest:
        copy.wait()

    sums[...] = jnp.zeros_like(sums)

    @pl.loop(0, rows // 64)
    def _(t):
        r = pl.ds(pl.multiple_of(t * 64, 64), 64)
        grad, values = gn[r, :], hidden[r, :]
        factor = lax.rsqrt(jnp.mean(values * values, axis=-1, keepdims=True) + epsilon)
        scaled = grad * gain[1, 0:1, :]
        middle = jnp.mean(scaled * values, axis=-1, keepdims=True)
        total = gy[r, :].astype(F32) + factor * scaled - values * (factor * factor * factor * middle)
        sums[1] += jnp.sum((grad * values * factor).reshape(8, 8, width), axis=0)
        gn[r, :] = total
        gy[r, :] = total.astype(BF)

    for i in range(2):
        term = dot(gy[:, pl.ds(512 * i, 512)], a[...], 0, 0)
        pproj[pl.ds(2 * i, 2)] = term.reshape(2, 2, 2, 2, 32, width).astype(BF)
    t0(8)
    load_w2[4].wait()
    for i in range(2):
        cols = pl.ds(512 * i, 512)
        att[:, cols] = dot(gy[...], wbuf[0, :, cols], 1, 0).astype(BF)
    load_p3 = me.move(p_hbm.at[3], wbuf.at[0])
    load_n1 = me.move(n1_hbm, gy)
    poll(3)
    kvsum[...] = jnp.zeros_like(kvsum)
    scale = DH ** -0.5

    def heads(g):
        slot = (2, 1, 3, 0)[g]

        @pl.loop(0, 2)
        def _(hh):
            cols = pl.ds(pl.multiple_of((2 * g + hh) * DH, DH), DH)
            keys = kv[:, :, pl.ds(0, DH)].reshape(length, DH)
            vals = kv[:, :, pl.ds(DH, DH)].reshape(length, DH)
            for t in range(rows // 256):
                r = pl.ds(256 * t, 256)
                grad = att[r, cols]
                chances = wbuf[slot, pl.ds(pl.multiple_of(hh * rows + 256 * t, 256), 256), :]
                grad_chances = dot(grad, vals, 1, 1)
                wide = chances.astype(F32)
                center = jnp.sum(wide * grad_chances, axis=-1, keepdims=True)
                grad_scores = (wide * (grad_chances - center)).astype(BF)
                kvsum[0] += dot(q[r, cols], grad_scores, 0, 0)
                kvsum[1] += dot(grad, chances, 0, 0)
                att[r, cols] = (dot(grad_scores, keys, 1, 0) * scale).astype(BF)

    for g, load in enumerate((load_w1[4], load_w2[5], load_w1[5], load_p3)):
        load.wait()
        heads(g)
        if g == 0:
            load_wq = me.move(wa_hbm.at[:, pl.ds(0, 1024)], wbuf.at[2])
        if g in (1, 3):
            poll(4 + g // 2)
    for half in (0, 1):
        cols = pl.ds(half * rows, rows)
        kvout[half, :, pl.ds(0, DH)] = (kvsum[0, :, cols] * scale).T.astype(BF)
        kvout[half, :, pl.ds(DH, DH)] = kvsum[1, :, cols].T.astype(BF)
    me.send(kvout.at[1 - me.y], kvin, PIECES * STEPS, me.yn)
    load_n1.wait()
    for i in range(2):
        term = dot(gy[:, pl.ds(512 * i, 512)], att[...], 0, 0)
        patt[pl.ds(2 * i, 2), :, :, :, :, pl.ds(0, 1024)] = term.reshape(2, 2, 2, 2, 32, width).astype(BF)
    me.arrived(kvin, PIECES * STEPS)
    kvin[...] = kvin[...] + kvout[me.y]
    for i in range(2):
        term = dot(gy[:, pl.ds(512 * i, 512)], kvin[...], 0, 0)
        patt[pl.ds(2 * i, 2), :, :, :, :, pl.ds(1024, 256)] = term.reshape(2, 2, 2, 2, 32, 256).astype(BF)
    load_wq.wait()
    for i in range(2):
        cols = pl.ds(512 * i, 512)
        hidden[:, cols] = dot(att[...], wbuf[2, cols, :], 1, 1) + dot(kvin[...], wkv[cols, :], 1, 1)
    load_x.wait()

    @pl.loop(0, rows // 64)
    def _(t):
        r = pl.ds(pl.multiple_of(t * 64, 64), 64)
        grad, values = hidden[r, :], n2[r, :].astype(F32)
        factor = lax.rsqrt(jnp.mean(values * values, axis=-1, keepdims=True) + epsilon)
        scaled = grad * gain[0, 0:1, :]
        middle = jnp.mean(scaled * values, axis=-1, keepdims=True)
        sums[0] += jnp.sum((grad * values * factor).reshape(8, 8, width), axis=0)
        gn[r, :] = gn[r, :] + factor * scaled - values * (factor * factor * factor * middle)

    save_x = me.move(gn, grad_x_hbm)
    for kind in (0, 1):
        row = jnp.sum(sums[kind], axis=0, keepdims=True)
        for zi in range(4):
            for xi in range(2):
                lanes = slice(128 * (2 * zi + xi), 128 * (2 * zi + xi) + 128)
                tile = jnp.broadcast_to(row[:, lanes], (16, 128)).astype(BF)
                for ci in range(2):
                    for yi in range(2):
                        patt[zi, xi, ci, yi, pl.ds(16 * kind, 16), pl.ds(1280, 128)] = tile
    t0(9)
    for k in range(6, 12):
        poll(k)
    save_x.wait()
    me.finish()


def on_grid(
    tokens, cotangent, prefix, attention_gain, query_weight, key_weight, value_weight, projection_weight,
    feedforward_gain, up_weight, down_weight,
):
    rows, width = tokens.shape[1:]
    vmem, hbm = pl.BlockSpec(memory_space=pltpu.VMEM), pl.BlockSpec(memory_space=pl.ANY)
    smem = pl.BlockSpec(memory_space=pltpu.SMEM)
    x, gy = tokens.reshape(rows, width), cotangent.reshape(rows, width)
    place = lax.axis_index("dp") * 2 + lax.axis_index("seq")
    lane = 32 * lax.rem(place, 4)
    gains = jnp.zeros((2, 16, 128), BF)
    both = jnp.stack([attention_gain, feedforward_gain]).astype(BF)
    gains = lax.dynamic_update_slice(
        gains, jnp.broadcast_to(both[:, None, :], (2, 16, 32)), (0, 0, lane)
    ).reshape(32, 128)
    projection_t = projection_weight.T.astype(BF)
    sds = jax.ShapeDtypeStruct
    grid = (4, 2, 2, 2)
    n_sems = PIECES * STEPS + 2
    length = 2 * rows
    out = pl.pallas_call(
        forward_kernel,
        out_shape=(
            sds((rows, width), BF),
            sds((*grid, 128, 1024), BF),
            sds((4, *grid, 32, 1024), BF),
            sds((*grid, 32, 1408), BF),
            sds((*grid, 32, 1024), BF),
            sds((2, 8, width), F32),
            sds((rows, width), BF),
            sds((rows, width), BF),
            sds((2, rows, 256), BF),
            sds((rows, width), BF),
            sds((rows, width), F32),
            sds((rows, width), BF),
            sds((rows, 4096), BF),
            sds((4, 2 * rows, length), BF),
            sds((8, 256, width), BF),
        ),
        in_specs=[smem, hbm, hbm] + [vmem] * 7,
        out_specs=[hbm] * 15,
        scratch_shapes=[
            pltpu.VMEM((*grid, 32, 1408), BF),
            pltpu.VMEM((*grid, 32, 1024), BF),
            pltpu.VMEM((4, *grid, 32, 1024), BF),
            pltpu.VMEM((4, *grid, 128, 256), BF),
            pltpu.VMEM((rows, width), BF),
            pltpu.VMEM((rows, width), BF),
            pltpu.VMEM((rows, width), BF),
            pltpu.VMEM((rows, width), BF),
            pltpu.VMEM((2, rows, 256), BF),
            pltpu.VMEM((rows, width), BF),
            pltpu.VMEM((rows, width), F32),
            pltpu.VMEM((rows, width), BF),
            pltpu.VMEM((rows, 4096), BF),
            pltpu.VMEM((rows, 4096), BF),
            pltpu.VMEM((2, 2 * rows, length), BF),
            pltpu.VMEM((rows, length), F32),
            pltpu.VMEM((2, 8, width), F32),
            pltpu.VMEM((8, 256, width), BF),
            pltpu.VMEM((8, 256, width), BF),
            pltpu.VMEM((rows, width), BF),
            pltpu.SemaphoreType.DMA((n_sems,)),
            pltpu.SemaphoreType.DMA((n_sems,)),
            pltpu.SemaphoreType.DMA((40,)),
        ],
        compiler_params=pltpu.CompilerParams(
            collective_id=0, has_side_effects=True, vmem_limit_bytes=VMEM_LIMIT
        ),
    )(
        prefix, x, gy, query_weight, key_weight, value_weight, gains, projection_t, up_weight, down_weight
    )
    layer_output, w2, w1, wa, wot, gain, n1, q, kv, a, hidden, n2, slope, p, down = out
    four = lambda pieces, r, cols: pltpu.VMEM((pieces, 4, r, cols), BF)
    grad_x, g2, g1, go, ga = pl.pallas_call(
        backward_kernel,
        out_shape=(
            sds((rows, width), F32),
            sds((128, 1024), F32),
            sds((32, 4096), F32),
            sds((32, 1024), F32),
            sds((32, 1408), F32),
        ),
        in_specs=[hbm] * 16,
        out_specs=[hbm] + [vmem] * 4,
        scratch_shapes=[
            pltpu.VMEM((rows, width), BF),
            pltpu.VMEM((rows, width), BF),
            pltpu.VMEM((rows, width), F32),
            pltpu.VMEM((rows, width), F32),
            pltpu.VMEM((rows, width), BF),
            pltpu.VMEM((rows, width), BF),
            pltpu.VMEM((2, rows, 256), BF),
            pltpu.VMEM((2, 8, width), F32),
            pltpu.VMEM((4, 1024, 1024), BF),
            pltpu.VMEM((2, rows, 1024), BF),
            pltpu.VMEM((width, 256), BF),
            pltpu.VMEM((rows, width), BF),
            pltpu.VMEM((2, 8, width), F32),
            pltpu.VMEM((2, DH, length), F32),
            pltpu.VMEM((2, rows, 256), BF),
            pltpu.VMEM((rows, 256), BF),
            pltpu.VMEM((4, 2, 2, 128, 1024), BF),
            pltpu.VMEM((4, *grid, 32, 1024), BF),
            pltpu.VMEM((*grid, 32, 1024), BF),
            pltpu.VMEM((*grid, 32, 1408), BF),
            pltpu.VMEM((5, 4, 2, 2, 32, 1024), BF),
            pltpu.VMEM((4, 2, 2, 32, 1408), BF),
            four(4, 64, 256), four(4, 64, 256), four(5, 16, 1024), four(5, 16, 1024),
            pltpu.VMEM((4, 16, 1408), BF), pltpu.VMEM((4, 16, 1408), BF),
            four(4, 128, 256), four(4, 128, 256), four(5, 32, 1024), four(5, 32, 1024),
            pltpu.VMEM((4, 32, 1408), BF), pltpu.VMEM((4, 32, 1408), BF),
            pltpu.VMEM((4, 3, 128, 256), BF), pltpu.VMEM((5, 3, 32, 1024), BF), pltpu.VMEM((3, 32, 1408), BF),
            pltpu.SemaphoreType.DMA((n_sems,)),
            pltpu.SemaphoreType.DMA((n_sems,)),
            pltpu.SemaphoreType.DMA((40,)),
        ],
        compiler_params=pltpu.CompilerParams(
            collective_id=1, has_side_effects=True, vmem_limit_bytes=VMEM_LIMIT
        ),
    )(
        x, gy, gain, w2.reshape(4, 1024, 1024), w1.reshape(4, 1024, 1024), wa.reshape(1024, 1408), wot.reshape(1024, 1024),
        n1, q, kv, a, hidden, n2, slope, p, down.reshape(4, 2, 2, 128, 1024),
    )
    gain_grads = lax.dynamic_slice(ga[:, 1280:].reshape(2, 16, 128)[:, 0], (0, lane), (2, 32))
    return (
        layer_output.reshape(tokens.shape),
        grad_x.reshape(tokens.shape),
        gain_grads[0],
        ga[:, :1024],
        ga[:, 1024:1152],
        ga[:, 1152:1280],
        go.T,
        gain_grads[1],
        g1,
        g2,
    )


def root_norm(values, gain):
    factor = lax.rsqrt(jnp.mean(values * values, axis=-1, keepdims=True) + epsilon)
    return values * factor * gain


def smooth_gate(values):
    return jax.nn.gelu(values, approximate=True)


def product(left, right):
    return jnp.dot(left, right, preferred_element_type=jnp.float32)


def inner_rows(left, right):
    return lax.dot_general(
        left, right, (((0,), (0,)), ((), ())), preferred_element_type=jnp.float32
    )


def outer_rows(left, right):
    return lax.dot_general(
        left, right, (((1,), (1,)), ((), ())), preferred_element_type=jnp.float32
    )


def local(
    tokens,
    cotangent,
    prefix,
    attention_gain,
    query_weight,
    key_weight,
    value_weight,
    projection_weight,
    feedforward_gain,
    up_weight,
    down_weight,
):
    seqs_here, span_len, model_width = tokens.shape
    length = span_len * lax.axis_size("seq")
    row_count = seqs_here * span_len
    block_len = min(64, span_len)
    block_count = span_len // block_len
    score_scale = DH ** (-0.5)
    gain_low = attention_gain.astype(jnp.bfloat16)
    query_low = query_weight.astype(jnp.bfloat16)
    key_low = key_weight.astype(jnp.bfloat16)
    value_low = value_weight.astype(jnp.bfloat16)
    projection_low = projection_weight.astype(jnp.bfloat16)
    second_low = feedforward_gain.astype(jnp.bfloat16)
    up_low = up_weight.astype(jnp.bfloat16)
    down_low = down_weight.astype(jnp.bfloat16)
    gathered = (
        lax.all_gather(gain_low, ("dp", "seq"), axis=0, tiled=True),
        lax.all_gather(query_low, ("dp", "seq"), axis=0, tiled=True),
        lax.all_gather(key_low, ("dp", "seq"), axis=0, tiled=True),
        lax.all_gather(value_low, ("dp", "seq"), axis=0, tiled=True),
        lax.all_gather(projection_low, ("dp", "seq"), axis=1, tiled=True),
        lax.all_gather(second_low, ("dp", "seq"), axis=0, tiled=True),
        lax.all_gather(up_low, ("dp", "seq"), axis=0, tiled=True),
        lax.all_gather(down_low, ("dp", "seq"), axis=0, tiled=True),
    )
    gain_one, query_full, key_full, value_full, projection_full, gain_two, up_full, down_full = (
        gathered
    )
    inputs = tokens.reshape(row_count, model_width).astype(jnp.float32)
    gain_first = gain_one.astype(jnp.float32)
    normed = root_norm(inputs, gain_first).astype(jnp.bfloat16)
    queries = product(normed, query_full).astype(jnp.bfloat16)
    pair_weight = jnp.concatenate([key_full, value_full], axis=1)
    pair_rows = product(normed, pair_weight).astype(jnp.bfloat16)
    key_own = pair_rows[:, :DH].reshape(seqs_here, span_len, DH)
    value_own = pair_rows[:, DH:].reshape(seqs_here, span_len, DH)
    key_all, value_all = (
        lax.all_gather(key_own, "seq", axis=1, tiled=True),
        lax.all_gather(value_own, "seq", axis=1, tiled=True),
    )
    query_pos = lax.axis_index("seq") * span_len + jnp.arange(span_len, dtype=jnp.int32)
    pos_blocks = query_pos.reshape(block_count, block_len)
    key_pos = jnp.arange(length, dtype=jnp.int32)

    def masked_scores(query_block, key_rows, positions, prefix_len):
        flat = query_block.reshape(block_len * H, DH)
        scores = (outer_rows(flat, key_rows) * score_scale).reshape(block_len, H, length)
        visible = (key_pos[None, :] <= positions[:, None]) | (key_pos[None, :] < prefix_len)
        return jnp.where(visible[:, None, :], scores, masked_score)

    def forward_sequence(members):
        query_blocks, key_rows, value_rows, prefix_len = members

        def forward_block(pieces):
            query_block, positions = pieces
            scores = masked_scores(query_block, key_rows, positions, prefix_len)
            maxima = jnp.max(scores, axis=-1, keepdims=True)
            exponent = jnp.exp(scores - maxima)
            totals = jnp.sum(exponent, axis=-1, keepdims=True)
            chances = (exponent / totals).astype(jnp.bfloat16)
            mixed = product(chances.reshape(block_len * H, length), value_rows)
            return (
                mixed.reshape(block_len, H * DH).astype(jnp.bfloat16),
                (maxima + jnp.log(totals))[..., 0],
            )

        return lax.map(forward_block, (query_blocks, pos_blocks))

    query_seq = queries.reshape(seqs_here, block_count, block_len, H, DH)
    attended, log_totals = lax.map(forward_sequence, (query_seq, key_all, value_all, prefix))
    attended = attended.reshape(row_count, H * DH)
    hidden = inputs + product(attended, projection_full)
    gain_second = gain_two.astype(jnp.float32)
    normed_two = root_norm(hidden, gain_second).astype(jnp.bfloat16)
    before = product(normed_two, up_full)
    active = smooth_gate(before).astype(jnp.bfloat16)
    layer_output = (hidden + product(active, down_full)).astype(jnp.bfloat16)
    gathered = (
        lax.all_gather(gain_low, ("dp", "seq"), axis=0, tiled=True),
        lax.all_gather(query_low, ("dp", "seq"), axis=0, tiled=True),
        lax.all_gather(key_low, ("dp", "seq"), axis=0, tiled=True),
        lax.all_gather(value_low, ("dp", "seq"), axis=0, tiled=True),
        lax.all_gather(projection_low, ("dp", "seq"), axis=1, tiled=True),
        lax.all_gather(second_low, ("dp", "seq"), axis=0, tiled=True),
        lax.all_gather(up_low, ("dp", "seq"), axis=0, tiled=True),
        lax.all_gather(down_low, ("dp", "seq"), axis=0, tiled=True),
    )
    gain_one, query_full, key_full, value_full, projection_full, gain_two, up_full, down_full = (
        gathered
    )
    gain_first = gain_one.astype(jnp.float32)
    gain_second = gain_two.astype(jnp.float32)
    pair_weight = jnp.concatenate([key_full, value_full], axis=1)
    grad_out = cotangent.reshape(row_count, model_width)
    grad_start = grad_out.astype(jnp.float32)
    down_grad = inner_rows(active, grad_out)
    grad_active = outer_rows(grad_out, down_full)
    _, gate_pull = jax.vjp(smooth_gate, before)
    grad_before = gate_pull(grad_active)[0].astype(jnp.bfloat16)
    up_grad = inner_rows(normed_two, grad_before)
    grad_normed_two = outer_rows(grad_before, up_full)
    _, second_pull = jax.vjp(root_norm, hidden, gain_second)
    grad_hidden_norm, feedforward_gain_grad = second_pull(grad_normed_two)
    grad_hidden = grad_start + grad_hidden_norm
    grad_branch = grad_hidden.astype(jnp.bfloat16)
    projection_grad = inner_rows(attended, grad_branch)
    grad_attended = outer_rows(grad_branch, projection_full).astype(jnp.bfloat16)
    key_all, value_all = (
        lax.all_gather(key_own, "seq", axis=1, tiled=True),
        lax.all_gather(value_own, "seq", axis=1, tiled=True),
    )
    grad_seq = grad_attended.reshape(seqs_here, block_count, block_len, H, DH)

    def backward_sequence(members):
        query_blocks, grad_blocks, total_blocks, key_rows, value_rows, prefix_len = members

        def backward_block(carry, pieces):
            key_sum, value_sum = carry
            query_block, grad_block, total_block, positions = pieces
            scores = masked_scores(query_block, key_rows, positions, prefix_len)
            chances = jnp.exp(scores - total_block[..., None])
            chance_low = chances.astype(jnp.bfloat16).reshape(block_len * H, length)
            grad_rows = grad_block.reshape(block_len * H, DH)
            query_rows = query_block.reshape(block_len * H, DH)
            grad_chances = outer_rows(grad_rows, value_rows).reshape(block_len, H, length)
            center = jnp.sum(chances * grad_chances, axis=-1, keepdims=True)
            grad_scores = (
                (chances * (grad_chances - center))
                .astype(jnp.bfloat16)
                .reshape(block_len * H, length)
            )
            grad_query = (product(grad_scores, key_rows) * score_scale).astype(jnp.bfloat16)
            key_sum = key_sum + inner_rows(grad_scores, query_rows) * score_scale
            value_sum = value_sum + inner_rows(chance_low, grad_rows)
            return ((key_sum, value_sum), grad_query.reshape(block_len, H * DH))

        empty_sum = jnp.zeros((length, DH), jnp.float32)
        (key_sum, value_sum), grad_queries = lax.scan(
            backward_block,
            (empty_sum, empty_sum),
            (query_blocks, grad_blocks, total_blocks, pos_blocks),
        )
        return (key_sum, value_sum, grad_queries)

    key_terms, value_terms, grad_queries = lax.map(
        backward_sequence, (query_seq, grad_seq, log_totals, key_all, value_all, prefix)
    )
    grad_keys, grad_values = (
        lax.psum_scatter(
            key_terms.astype(jnp.bfloat16), "seq", scatter_dimension=1, tiled=True
        ).astype(jnp.float32),
        lax.psum_scatter(
            value_terms.astype(jnp.bfloat16), "seq", scatter_dimension=1, tiled=True
        ).astype(jnp.float32),
    )
    grad_pair = jnp.concatenate(
        [grad_keys.reshape(row_count, DH), grad_values.reshape(row_count, DH)], axis=1
    ).astype(jnp.bfloat16)
    grad_query_rows = grad_queries.reshape(row_count, H * DH)
    query_grad = inner_rows(normed, grad_query_rows)
    pair_grad = inner_rows(normed, grad_pair)
    key_grad = pair_grad[:, :DH]
    value_grad = pair_grad[:, DH:]
    grad_normed = outer_rows(grad_query_rows, query_full) + outer_rows(grad_pair, pair_weight)
    _, first_pull = jax.vjp(root_norm, inputs, gain_first)
    grad_inputs_norm, attention_gain_grad = first_pull(grad_normed)
    input_grad = (grad_hidden + grad_inputs_norm).reshape(seqs_here, span_len, model_width)
    layer_output = layer_output.reshape(seqs_here, span_len, model_width)
    summed = (
        lax.psum_scatter(attention_gain_grad, ("dp", "seq"), scatter_dimension=0, tiled=True),
        lax.psum_scatter(query_grad, ("dp", "seq"), scatter_dimension=0, tiled=True),
        lax.psum_scatter(key_grad, ("dp", "seq"), scatter_dimension=0, tiled=True),
        lax.psum_scatter(value_grad, ("dp", "seq"), scatter_dimension=0, tiled=True),
        lax.psum_scatter(projection_grad, ("dp", "seq"), scatter_dimension=1, tiled=True),
        lax.psum_scatter(feedforward_gain_grad, ("dp", "seq"), scatter_dimension=0, tiled=True),
        lax.psum_scatter(up_grad, ("dp", "seq"), scatter_dimension=0, tiled=True),
        lax.psum_scatter(down_grad, ("dp", "seq"), scatter_dimension=0, tiled=True),
    )
    return (
        layer_output,
        input_grad,
        summed[0],
        summed[1],
        summed[2],
        summed[3],
        summed[4],
        summed[5],
        summed[6],
        summed[7],
    )


def fits(mesh, tokens, up_weight):
    return (
        mesh.shape["dp"] == 16
        and mesh.shape["seq"] == 2
        and tokens.shape == (16, 1024, 1024)
        and up_weight.shape == (1024, 4096)
    )


def solution(mesh):
    def layer(*args):
        return sharded(mesh, on_grid if fits(mesh, args[0], args[9]) else local)(*args)

    return layer


def sharded(mesh, part):
    return jax.shard_map(
        part,
        mesh=mesh,
        in_specs=(
            P("dp", "seq", None),
            P("dp", "seq", None),
            P("dp"),
            P(("dp", "seq")),
            P(("dp", "seq"), None),
            P(("dp", "seq"), None),
            P(("dp", "seq"), None),
            P(None, ("dp", "seq")),
            P(("dp", "seq")),
            P(("dp", "seq"), None),
            P(("dp", "seq"), None),
        ),
        out_specs=(
            P("dp", "seq", None),
            P("dp", "seq", None),
            P(("dp", "seq")),
            P(("dp", "seq"), None),
            P(("dp", "seq"), None),
            P(("dp", "seq"), None),
            P(None, ("dp", "seq")),
            P(("dp", "seq")),
            P(("dp", "seq"), None),
            P(("dp", "seq"), None),
        ),
        check_vma=False,
    )
```

```python
import functools
import jax
import jax.numpy as jnp
from jax import lax
from jax.experimental import pallas as pl
from jax.experimental.pallas import tpu as pltpu
from jax.sharding import PartitionSpec as P

H = 8
DH = 128
BF = jnp.bfloat16
F32 = jnp.float32
MESH = pl.DeviceIdType.MESH
VMEM_LIMIT = 61 * 2**20
GELU_C = 0.7978845608028654
GELU_A = 0.044715

epsilon = 1e-06
masked_score = -10000.0


def dot(left, right, left_dim, right_dim):
    return lax.dot_general(
        left, right, (((left_dim,), (right_dim,)), ((), ())), preferred_element_type=F32
    )


class Place:
    def __init__(self, send_sems, recv_sems, local_sems):
        dp = lax.axis_index("dp")
        self.y = lax.axis_index("seq")
        self.c = lax.rem(dp, 2)
        self.x = lax.rem(lax.div(dp, 2), 2)
        self.z = lax.div(dp, 4)
        self.send_sems, self.recv_sems, self.local_sems = send_sems, recv_sems, local_sems
        self.n_local = 0
        self.xn = self.at(self.z, 1 - self.x, self.c, self.y)
        self.yn = self.at(self.z, self.x, self.c, 1 - self.y)
        self.cn = self.at(self.z, self.x, 1 - self.c, self.y)

    def at(self, z, x, c, y):
        return ((z * 2 + x) * 2 + c, y)

    def z_to(self, step):
        return lax.rem(self.z + step, 4)

    def zn(self, step):
        return self.at(self.z_to(step), self.x, self.c, self.y)

    def greet(self):
        barrier = pltpu.get_barrier_semaphore()
        for device in (self.cn, self.xn, self.yn, self.zn(1), self.zn(2), self.zn(3)):
            pl.semaphore_signal(barrier, inc=1, device_id=device, device_id_type=MESH)
        pl.semaphore_wait(barrier, 6)

    def send(self, src, dst, recv, device, group):
        pltpu.make_async_remote_copy(
            src_ref=src,
            dst_ref=dst,
            send_sem=self.send_sems.at[group],
            recv_sem=self.recv_sems.at[recv],
            device_id=device,
            device_id_type=MESH,
        ).start()

    def wait(self, like, sem):
        pltpu.make_async_copy(like, like, sem).wait()

    def arrived(self, like, recv):
        self.wait(like, self.recv_sems.at[recv])

    def left(self, like, group):
        self.wait(like, self.send_sems.at[group])

    def move(self, src, dst):
        copy = pltpu.make_async_copy(src, dst, self.local_sems.at[self.n_local])
        self.n_local += 1
        copy.start()
        return copy


class Steps:
    def __init__(self, order):
        self.order, self.done = list(order), set()

    def next(self, count=1):
        for _ in range(count):
            if self.order and self.order[0][2]():
                step, i, _ready = self.order.pop(0)
                step(i)
                self.done.add((step, i))

    def until(self, step, i):
        while (step, i) not in self.done:
            self.next()

    def rest(self):
        while self.order:
            self.next()


def gelu_parts(u):
    square = u * u
    t = jnp.tanh(GELU_C * u * (1.0 + GELU_A * square))
    half = 0.5 * (1.0 + t)
    slope = half + (0.5 * GELU_C) * u * (1.0 - t * t) * (1.0 + (3.0 * GELU_A) * square)
    return u * half, slope


PIECES = 10
RECVS = 11
SENDS = 3


def cut(rows, cols):
    if rows < 128:
        first, second = (pl.ds(0, rows), pl.ds(0, cols - 128)), (pl.ds(0, rows), pl.ds(cols - 128, 128))
        halves = (pl.ds(0, rows // 2), first[1]), (pl.ds(rows // 2, rows // 2), first[1])
    else:
        edge = rows - rows // 8
        first, second = (pl.ds(0, edge), pl.ds(0, cols)), (pl.ds(edge, rows // 8), pl.ds(0, cols))
        halves = (pl.ds(0, 64), first[1]), (pl.ds(64, edge - 64), first[1])
    return first, second, halves


def forward_kernel(
    prefix_ref, x_hbm, gy_hbm, wq_ref, wk_ref, wv_ref, wg_ref, wo_ref, w1_ref, w2_ref,
    out_hbm, w2_hbm, w1_hbm, wa_hbm, wot_hbm, gain_hbm, n1_hbm, q_hbm, kv_hbm, a_hbm, hidden_hbm,
    n2_hbm, slope_hbm, p_hbm, down_hbm,
    wa, wot, w1, w2, x, gy, n1, q, kv, a, hidden, n2, z, slope, p, bias, gain, down_out, down_in, out,
    send_sems, recv_sems, local_sems,
):
    me = Place(send_sems, recv_sems, local_sems)
    rows, width = x.shape
    load_x = me.move(x_hbm, x)
    load_gy = me.move(gy_hbm, gy)
    views = [wa, wot] + [w1.at[j] for j in range(4)] + [w2.at[k] for k in range(4)]
    saves = []

    every = slice(None)
    own = (me.z, me.x, me.c, me.y)

    def pass_on(i, at, recv, device, group):
        view = views[i].at[at]
        me.send(view, view, i * RECVS + recv, device, i * SENDS + group)

    def came(i, at, recv):
        me.arrived(views[i].at[at], i * RECVS + recv)

    def s0(i):
        first, second, _ = cut(*views[i].shape[4:])
        for step in (1, 3, 2):
            pass_on(i, own + first, step - 1, me.zn(step), 0)
        pass_on(i, own + first, 3, me.xn, 1)
        pass_on(i, own + first, 4, me.yn, 1)
        pass_on(i, own + second, 5, me.xn, 0)
        pass_on(i, own + second, 6, me.yn, 0)

    def s1(i):
        first, second, _ = cut(*views[i].shape[4:])
        for step in (1, 3, 2):
            at = (me.z_to(4 - step), me.x, me.c, me.y) + first
            came(i, at, step - 1)
            pass_on(i, at, 3, me.xn, 1)
            pass_on(i, at, 4, me.yn, 1)
        from_x, from_y = (me.z, 1 - me.x, me.c, me.y) + second, (me.z, me.x, me.c, 1 - me.y) + second
        came(i, from_x, 5)
        came(i, from_y, 6)
        if i % 2:
            pass_on(i, from_y, 7, me.xn, 0)
        else:
            pass_on(i, from_x, 7, me.yn, 0)

    def s2(i):
        first, second, (low, high) = cut(*views[i].shape[4:])
        came(i, (every, 1 - me.x, me.c, me.y) + first, 3)
        pass_on(i, (every, 1 - me.x, me.c, me.y) + low, 9, me.yn, 1)
        came(i, (every, me.x, me.c, 1 - me.y) + first, 4)
        pass_on(i, (every, me.x, me.c, 1 - me.y) + high, 9, me.xn, 1)
        came(i, (me.z, 1 - me.x, me.c, 1 - me.y) + second, 7)
        for step in (1, 3, 2):
            pass_on(i, (me.z, every, me.c, every) + second, 8, me.zn(step), 1)

    def s3(i):
        first, second, _ = cut(*views[i].shape[4:])
        came(i, (every, 1 - me.x, me.c, 1 - me.y) + first, 9)
        came(i, (pl.ds(0, 3), every, me.c, every) + second, 8)
        pass_on(i, (every, every, me.c), 10, me.cn, 2)

    def s4(i):
        came(i, (every, every, 1 - me.c), 10)
        if i == 0:
            saves.append(me.move(wa, wa_hbm))
        elif i == 1:
            saves.append(me.move(wot, wot_hbm))
        elif i < 6:
            saves.append(me.move(w1.at[i - 2], w1_hbm.at[i - 2]))
        else:
            k = i - 6
            saves.append(me.move(w2.at[k], w2_hbm.at[:, :, :, :, :, pl.ds(256 * k, 256)]))

    def order():
        yield s0, 0
        for k in range(-1, PIECES + 3):
            for step, i in ((s1, k + 1), (s0, k + 2), (s2, k), (s3, k - 1), (s4, k - 2)):
                if 0 <= i < PIECES:
                    yield step, i

    steps = Steps((step, i, lambda: True) for step, i in order())

    wa[(*own, every, pl.ds(0, 1024))] = wq_ref[...].astype(BF)
    wa[(*own, every, pl.ds(1024, 128))] = wk_ref[...].astype(BF)
    wa[(*own, every, pl.ds(1152, 128))] = wv_ref[...].astype(BF)
    wa[(*own, every, pl.ds(1280, 128))] = wg_ref[...]
    wot[own] = wo_ref[...]
    me.greet()
    steps.next()
    for j in range(4):
        w1[(j, *own)] = w1_ref[:, pl.ds(1024 * j, 1024)].astype(BF)
    for k in range(4):
        w2[(k, *own)] = w2_ref[:, pl.ds(256 * k, 256)].astype(BF)
    steps.next(2)

    first_pos = me.y * rows

    @pl.loop(0, rows // 64)
    def _(t):
        at = pl.multiple_of(t * 64, 64)
        query_pos = first_pos + at + lax.broadcasted_iota(jnp.int32, (64, 2 * rows), 0)
        key_pos = lax.broadcasted_iota(jnp.int32, (64, 2 * rows), 1)
        visible = (key_pos <= query_pos) | (key_pos < prefix_ref[0])
        bias[pl.ds(at, 64), :] = jnp.where(visible, 0.0, -1e30)

    load_x.wait()
    load_gy.wait()
    steps.until(s4, 0)

    for kind in (0, 1):
        for zi in range(4):
            for xi in range(2):
                tile = jnp.zeros((16, 128), F32)
                for ci in range(2):
                    for yi in range(2):
                        tile += wa[zi, xi, ci, yi, pl.ds(16 * kind, 16), pl.ds(1280, 128)].astype(F32)
                gain[kind, :, pl.ds(128 * (2 * zi + xi), 128)] = tile[:8]
    saves.append(me.move(gain, gain_hbm))

    @pl.loop(0, rows // 64)
    def _(t):
        r = pl.ds(pl.multiple_of(t * 64, 64), 64)
        values = x[r, :].astype(F32)
        factor = lax.rsqrt(jnp.mean(values * values, axis=-1, keepdims=True) + epsilon)
        n1[r, :] = (values * factor * gain[0, 0:1, :]).astype(BF)

    kv[me.y] = dot(
        n1[...], wa[:, :, :, :, :, pl.ds(1024, 256)].reshape(width, 256), 1, 0
    ).astype(BF)
    me.send(kv.at[me.y], kv.at[me.y], PIECES * RECVS, me.yn, PIECES * SENDS)
    for i in range(2):
        steps.next()
        cols = pl.ds(512 * i, 512)
        q[:, cols] = dot(n1[...], wa[:, :, :, :, :, cols].reshape(width, 512), 1, 0).astype(BF)

    saves.append(me.move(n1, n1_hbm))
    saves.append(me.move(q, q_hbm))
    steps.next()
    me.arrived(kv.at[1 - me.y], PIECES * RECVS)
    saves.append(me.move(kv, kv_hbm))
    length = 2 * rows
    to_log2 = (DH ** -0.5) * 1.4426950408889634

    def head(h):
        cols = pl.ds(h * DH, DH)
        keys = kv[:, :, pl.ds(0, DH)].reshape(length, DH)
        vals = kv[:, :, pl.ds(DH, DH)].reshape(length, DH)
        for t in range(rows // 256):
            r = pl.ds(256 * t, 256)
            s = dot(q[r, cols], keys, 1, 1) * to_log2 + bias[r, :]
            e = jnp.exp2(s - jnp.max(s, axis=-1, keepdims=True))
            chances = (e * (1.0 / jnp.sum(e, axis=-1, keepdims=True))).astype(BF)
            p[(h // 2) % 2, pl.ds((h % 2) * rows + 256 * t, 256), :] = chances
            a[r, cols] = dot(chances, vals, 1, 0).astype(BF)

    p_saves = []
    for h in range(H):
        if h >= 4 and h % 2 == 0:
            p_saves[h // 2 - 2].wait()
        head(h)
        if h % 2:
            p_saves.append(me.move(p.at[(h // 2) % 2], p_hbm.at[h // 2]))
        steps.next()
    saves.extend(p_saves[2:])
    saves.append(me.move(a, a_hbm))
    steps.until(s4, 1)
    for i in range(2):
        cols = pl.ds(512 * i, 512)
        weight = wot[pl.ds(2 * i, 2)].reshape(512, width)
        hidden[:, cols] = x[:, cols].astype(F32) + dot(a[...], weight, 1, 1)
        steps.next()

    @pl.loop(0, rows // 64)
    def _(t):
        r = pl.ds(pl.multiple_of(t * 64, 64), 64)
        values = hidden[r, :]
        factor = lax.rsqrt(jnp.mean(values * values, axis=-1, keepdims=True) + epsilon)
        n2[r, :] = (values * factor * gain[1, 0:1, :]).astype(BF)

    saves.append(me.move(hidden, hidden_hbm))
    saves.append(me.move(n2, n2_hbm))
    steps.next()
    for j in range(4):
        steps.until(s4, 2 + j)
        for i in range(2):
            cols, to = pl.ds(512 * i, 512), pl.ds(1024 * j + 512 * i, 512)
            u = dot(n2[...], w1[j, :, :, :, :, :, cols].reshape(width, 512), 1, 0)
            active, steep = gelu_parts(u)
            z[:, to] = active.astype(BF)
            slope[:, to] = steep.astype(BF)
            steps.next()
    saves.append(me.move(slope, slope_hbm))

    for half in range(2):
        @pl.loop(4 * half, 4 * half + 4)
        def _(t):
            cols = pl.ds(pl.multiple_of((2 * t + 1 - me.c) * 256, 256), 256)
            down_out[t] = dot(z[:, cols], gy[...], 0, 0).astype(BF)

        steps.next(2)
    me.send(down_out, down_in, PIECES * RECVS + 1, me.cn, PIECES * SENDS + 1)

    def down(k):
        cols = pl.ds(256 * k, 256)
        for t in range(2):
            r = pl.ds(256 * t, 256)
            y = dot(z[r, :], w2[k].reshape(4096, 256), 1, 0)
            out[r, cols] = (hidden[r, cols] + y).astype(BF)

    steps.until(s4, 6)
    down(0)
    steps.next(2)
    me.arrived(down_in, PIECES * RECVS + 1)
    for half in range(2):
        @pl.loop(4 * half, 4 * half + 4)
        def _(t):
            cols = pl.ds(pl.multiple_of((2 * t + me.c) * 256, 256), 256)
            down_in[t] = (dot(z[:, cols], gy[...], 0, 0) + down_in[t].astype(F32)).astype(BF)

        steps.next(2)
    saves.append(me.move(down_in, down_hbm))
    for k in (1, 2, 3):
        steps.until(s4, 6 + k)
        down(k)
    steps.rest()
    saves.append(me.move(out, out_hbm))
    for copy in saves:
        copy.wait()
    for i in range(PIECES):
        me.left(views[i].at[pl.ds(0, 3), me.x, me.c, me.y], i * SENDS)
        me.left(views[i].at[pl.ds(0, 3), :, me.c], i * SENDS + 1)
        me.left(views[i].at[:, :, me.c], i * SENDS + 2)
    me.left(kv.at[me.y], PIECES * SENDS)
    me.left(down_out, PIECES * SENDS + 1)


def backward_kernel(
    x_hbm, gy_hbm, gain_hbm, w2_hbm, w1_hbm, wa_hbm, wot_hbm, n1_hbm, q_hbm, kv_hbm, a_hbm, hidden_hbm,
    n2_hbm, slope_hbm, p_hbm, down_hbm,
    grad_x_hbm, g2_ref, g1_ref, go_ref, ga_ref,
    gy, n2, hidden, gn, a, q, kv, gain, wbuf, gu, wkv, att, sums, kvsum, kvout, kvin,
    down, pup, pproj, patt, pair_up, pair_att, diag2, diag1, diaga, side2, side1, sidea, line2, line1, linea,
    plane2, plane1, planea,
    send_sems, recv_sems, local_sems,
):
    me = Place(send_sems, recv_sems, local_sems)
    rows, width = gy.shape
    length = 2 * rows
    load_down = [
        me.move(down_hbm.at[:, :, :, :, pl.ds(256 * k, 256)], down.at[:, :, :, :, pl.ds(256 * k, 256)])
        for k in range(4)
    ]
    load_gy = me.move(gy_hbm, gy)
    load_w2 = [me.move(w2_hbm.at[j], wbuf.at[j]) for j in range(2)]
    load_slope = [me.move(slope_hbm.at[:, pl.ds(1024 * j, 1024)], gu.at[j]) for j in range(2)]
    load_n2 = me.move(n2_hbm, n2)
    load_w1 = [me.move(w1_hbm.at[j], wbuf.at[2 + j]) for j in range(2)]
    load_rest = [
        me.move(src, dst)
        for src, dst in (
            (hidden_hbm, hidden), (gain_hbm, gain), (a_hbm, a), (q_hbm, q), (kv_hbm, kv),
            (wa_hbm.at[:, pl.ds(1024, 256)], wkv),
        )
    ]

    def source(i):
        return pup.at[i - 4] if i < 8 else pproj if i == 8 else patt

    def pair(i):
        return pair_up.at[i - 4] if i < 9 else pair_att

    def part(i, zi, xi, yi, at):
        if i < 4:
            return down.at[zi, xi, yi, at[0], pl.ds(256 * i + at[1].start, at[1].size)]
        return source(i).at[(zi, xi, me.c, yi) + at]

    def group(i, two, one, last):
        return two.at[i] if i < 4 else one.at[i - 4] if i < 9 else last

    def cut_of(i):
        return cut(*((128, 256) if i < 4 else (32, 1024) if i < 9 else (32, 1408)))

    every = slice(None)
    given = set(range(4))

    def send(src, dst, i, recv, device, to):
        me.send(src, dst, i * RECVS + recv, device, i * SENDS + to)

    def came(like, i, recv):
        me.arrived(like, i * RECVS + recv)

    def t0(i):
        send(source(i).at[:, :, 1 - me.c], pair(i), i, 0, me.cn, 2)
        given.add(i)

    def t1(i):
        first, second, (low, high) = cut_of(i)
        diag, plane = group(i, diag2, diag1, diaga), group(i, plane2, plane1, planea)
        if i < 4:
            load_down[i].wait()
        else:
            total, term = source(i), pair(i)
            came(term, i, 0)

            @pl.loop(0, 4)
            def _(zi):
                for xi in range(2):
                    total[zi, xi, me.c] = total[zi, xi, me.c] + term[zi, xi]

        send(part(i, every, 1 - me.x, 1 - me.y, low), diag.at[(every,) + low], i, 1, me.yn, 1)
        send(part(i, every, 1 - me.x, 1 - me.y, high), diag.at[(every,) + high], i, 1, me.xn, 1)
        for step in (1, 3, 2):
            send(part(i, me.z_to(step), every, every, second), plane.at[step - 1], i, 2, me.zn(step), 1)

    def t2(i):
        first, second, (low, high) = cut_of(i)
        diag, plane = group(i, diag2, diag1, diaga), group(i, plane2, plane1, planea)
        side = group(i, side2, side1, sidea)
        came(diag.at[(every,) + first], i, 1)
        for step in (1, 3, 2, 0):
            zi = me.z_to(step)
            for xi, yi, half in ((1 - me.x, me.y, low), (me.x, 1 - me.y, high)):
                mine = part(i, zi, xi, yi, half)
                mine[...] = mine[...] + diag[(zi,) + half]
            recv = 2 + step if step else 6
            send(part(i, zi, 1 - me.x, me.y, first), side.at[(0, zi) + first], i, recv, me.xn, 1)
            send(part(i, zi, me.x, 1 - me.y, first), side.at[(1, zi) + first], i, recv, me.yn, 1)
        came(plane, i, 2)
        for xi in range(2):
            for yi in range(2):
                mine = part(i, me.z, xi, yi, second)
                total = mine[...].astype(F32)
                for step in range(3):
                    total += plane[step, xi, yi].astype(F32)
                mine[...] = total.astype(BF)
        send(
            part(i, me.z, 1 - me.x, 1 - me.y, second), diag.at[(me.z,) + second], i, 7,
            me.xn if i % 2 else me.yn, 0,
        )

    def t3(i):
        first, second, _ = cut_of(i)
        diag, side = group(i, diag2, diag1, diaga), group(i, side2, side1, sidea)
        line = group(i, line2, line1, linea)
        for step in (1, 3, 2):
            zi = me.z_to(step)
            came(side.at[(every, zi) + first], i, 2 + step)
            mine = part(i, zi, me.x, me.y, first)
            total = mine[...].astype(F32) + side[(0, zi) + first].astype(F32) + side[(1, zi) + first].astype(F32)
            mine[...] = total.astype(BF)
            send(mine, line.at[(step - 1,) + first], i, 8, me.zn(step), 0)
        came(diag.at[(me.z,) + second], i, 7)
        mine = part(i, me.z, *((me.x, 1 - me.y) if i % 2 else (1 - me.x, me.y)), second)
        mine[...] = mine[...] + diag[(me.z,) + second]
        send(part(i, me.z, 1 - me.x, me.y, second), side.at[(0, me.z) + second], i, 9, me.xn, 0)
        send(part(i, me.z, me.x, 1 - me.y, second), side.at[(1, me.z) + second], i, 9, me.yn, 0)

    def t4(i):
        first, second, _ = cut_of(i)
        side, line = group(i, side2, side1, sidea), group(i, line2, line1, linea)
        came(side.at[(every, me.z) + first], i, 6)
        came(line.at[(every,) + first], i, 8)
        came(side.at[(every, me.z) + second], i, 9)
        out, shift = (
            (g2_ref, 256 * i) if i < 4 else (g1_ref, 1024 * (i - 4)) if i < 8 else (go_ref, 0) if i == 8 else (ga_ref, 0)
        )
        for at in (first, second):
            total = part(i, me.z, me.x, me.y, at)[...].astype(F32)
            total += side[(0, me.z) + at].astype(F32) + side[(1, me.z) + at].astype(F32)
            if at is first:
                for step in range(3):
                    total += line[(step,) + first].astype(F32)
            out[at[0], pl.ds(shift + at[1].start, at[1].size)] = total

    def order():
        yield t1, 0
        for k in range(PIECES + 2):
            for step, i in ((t1, k + 1), (t2, k), (t3, k - 1), (t4, k - 2)):
                if 0 <= i < PIECES:
                    yield step, i

    steps = Steps((step, i, lambda step=step, i=i: step is not t1 or i in given) for step, i in order())
    me.greet()
    steps.next()

    def feed_forward(j):
        slot = j % 2
        load_w2[j].wait()
        load_slope[j].wait()
        for i in range(2):
            cols = pl.ds(512 * i, 512)
            grad_active = dot(gy[...], wbuf[slot, cols, :], 1, 1)
            gu[slot, :, cols] = (grad_active * gu[slot, :, cols].astype(F32)).astype(BF)
        steps.next()
        if j < 2:
            load_w2.append(me.move(w2_hbm.at[j + 2], wbuf.at[slot]))
        elif j == 2:
            load_w2.append(me.move(wot_hbm, wbuf.at[0]))
        else:
            load_w2.append(me.move(p_hbm.at[1], wbuf.at[1]))
        for i in range(2):
            term = dot(n2[:, pl.ds(512 * i, 512)], gu[slot], 0, 0)
            pup[j, pl.ds(2 * i, 2)] = term.reshape(2, 2, 2, 2, 32, 1024).astype(BF)
        t0(4 + j)
        steps.next()
        load_w1[j].wait()
        for i in range(2):
            cols = pl.ds(512 * i, 512)
            term = dot(gu[slot], wbuf[2 + slot, cols, :], 1, 1)
            if j == 0:
                gn[:, cols] = term
            else:
                gn[:, cols] = gn[:, cols] + term
        if j < 2:
            load_slope.append(me.move(slope_hbm.at[:, pl.ds(1024 * (j + 2), 1024)], gu.at[slot]))
            load_w1.append(me.move(w1_hbm.at[j + 2], wbuf.at[2 + slot]))
        else:
            load_w1.append(me.move(p_hbm.at[(0, 2)[j - 2]], wbuf.at[2 + slot]))
        steps.next()

    load_gy.wait()
    load_n2.wait()
    for j in range(4):
        feed_forward(j)
    load_x = me.move(x_hbm, n2)
    for copy in load_rest:
        copy.wait()

    sums[...] = jnp.zeros_like(sums)

    @pl.loop(0, rows // 64)
    def _(t):
        r = pl.ds(pl.multiple_of(t * 64, 64), 64)
        grad, values = gn[r, :], hidden[r, :]
        factor = lax.rsqrt(jnp.mean(values * values, axis=-1, keepdims=True) + epsilon)
        scaled = grad * gain[1, 0:1, :]
        middle = jnp.mean(scaled * values, axis=-1, keepdims=True)
        total = gy[r, :].astype(F32) + factor * scaled - values * (factor * factor * factor * middle)
        sums[1] += jnp.sum((grad * values * factor).reshape(8, 8, width), axis=0)
        gn[r, :] = total
        gy[r, :] = total.astype(BF)

    for i in range(2):
        term = dot(gy[:, pl.ds(512 * i, 512)], a[...], 0, 0)
        pproj[pl.ds(2 * i, 2)] = term.reshape(2, 2, 2, 2, 32, width).astype(BF)
    t0(8)
    steps.next()
    load_w2[4].wait()
    for i in range(2):
        cols = pl.ds(512 * i, 512)
        att[:, cols] = dot(gy[...], wbuf[0, :, cols], 1, 0).astype(BF)
    load_p3 = me.move(p_hbm.at[3], wbuf.at[0])
    load_n1 = me.move(n1_hbm, gy)
    steps.next()
    kvsum[...] = jnp.zeros_like(kvsum)
    scale = DH ** -0.5

    def head(h):
        slot = (2, 1, 3, 0)[h // 2]
        cols = pl.ds(h * DH, DH)
        keys = kv[:, :, pl.ds(0, DH)].reshape(length, DH)
        vals = kv[:, :, pl.ds(DH, DH)].reshape(length, DH)
        for t in range(rows // 256):
            r = pl.ds(256 * t, 256)
            grad = att[r, cols]
            chances = wbuf[slot, pl.ds((h % 2) * rows + 256 * t, 256), :]
            grad_chances = dot(grad, vals, 1, 1)
            wide = chances.astype(F32)
            center = jnp.sum(wide * grad_chances, axis=-1, keepdims=True)
            grad_scores = (wide * (grad_chances - center)).astype(BF)
            kvsum[0] += dot(q[r, cols], grad_scores, 0, 0)
            kvsum[1] += dot(grad, chances, 0, 0)
            att[r, cols] = (dot(grad_scores, keys, 1, 0) * scale).astype(BF)

    load_p = (load_w1[4], load_w2[5], load_w1[5], load_p3)
    for h in range(H):
        if h % 2 == 0:
            load_p[h // 2].wait()
        head(h)
        if h == 1:
            load_wq = me.move(wa_hbm.at[:, pl.ds(0, 1024)], wbuf.at[2])
        steps.next()
    for half in (0, 1):
        cols = pl.ds(half * rows, rows)
        kvout[half, :, pl.ds(0, DH)] = (kvsum[0, :, cols] * scale).T.astype(BF)
        kvout[half, :, pl.ds(DH, DH)] = kvsum[1, :, cols].T.astype(BF)
    me.send(kvout.at[1 - me.y], kvin, PIECES * RECVS, me.yn, PIECES * SENDS)
    load_n1.wait()
    for i in range(2):
        term = dot(gy[:, pl.ds(512 * i, 512)], att[...], 0, 0)
        patt[pl.ds(2 * i, 2), :, :, :, :, pl.ds(0, 1024)] = term.reshape(2, 2, 2, 2, 32, width).astype(BF)
    steps.next()
    me.arrived(kvin, PIECES * RECVS)
    kvin[...] = kvin[...] + kvout[me.y]
    for i in range(2):
        term = dot(gy[:, pl.ds(512 * i, 512)], kvin[...], 0, 0)
        patt[pl.ds(2 * i, 2), :, :, :, :, pl.ds(1024, 256)] = term.reshape(2, 2, 2, 2, 32, 256).astype(BF)
    load_wq.wait()
    for i in range(2):
        cols = pl.ds(512 * i, 512)
        hidden[:, cols] = dot(att[...], wbuf[2, cols, :], 1, 1) + dot(kvin[...], wkv[cols, :], 1, 1)
        steps.next()
    load_x.wait()

    @pl.loop(0, rows // 64)
    def _(t):
        r = pl.ds(pl.multiple_of(t * 64, 64), 64)
        grad, values = hidden[r, :], n2[r, :].astype(F32)
        factor = lax.rsqrt(jnp.mean(values * values, axis=-1, keepdims=True) + epsilon)
        scaled = grad * gain[0, 0:1, :]
        middle = jnp.mean(scaled * values, axis=-1, keepdims=True)
        sums[0] += jnp.sum((grad * values * factor).reshape(8, 8, width), axis=0)
        gn[r, :] = gn[r, :] + factor * scaled - values * (factor * factor * factor * middle)

    save_x = me.move(gn, grad_x_hbm)
    for kind in (0, 1):
        row = jnp.sum(sums[kind], axis=0, keepdims=True)
        for zi in range(4):
            for xi in range(2):
                lanes = slice(128 * (2 * zi + xi), 128 * (2 * zi + xi) + 128)
                tile = jnp.broadcast_to(row[:, lanes], (16, 128)).astype(BF)
                for ci in range(2):
                    for yi in range(2):
                        patt[zi, xi, ci, yi, pl.ds(16 * kind, 16), pl.ds(1280, 128)] = tile
    t0(9)
    steps.rest()
    save_x.wait()
    for i in range(PIECES):
        if i < 4:
            at = (every, pl.ds(256 * i, 256))
            me.left(down.at[(pl.ds(0, 3), 0, 0) + at], i * SENDS)
            me.left(down.at[(pl.ds(0, 3), every, every) + at], i * SENDS + 1)
        else:
            me.left(source(i).at[pl.ds(0, 3), 0, 0, 0], i * SENDS)
            me.left(source(i).at[pl.ds(0, 3), :, 0], i * SENDS + 1)
            me.left(source(i).at[:, :, 0], i * SENDS + 2)
    me.left(kvin, PIECES * SENDS)


def on_grid(
    tokens, cotangent, prefix, attention_gain, query_weight, key_weight, value_weight, projection_weight,
    feedforward_gain, up_weight, down_weight,
):
    rows, width = tokens.shape[1:]
    vmem, hbm = pl.BlockSpec(memory_space=pltpu.VMEM), pl.BlockSpec(memory_space=pl.ANY)
    smem = pl.BlockSpec(memory_space=pltpu.SMEM)
    x, gy = tokens.reshape(rows, width), cotangent.reshape(rows, width)
    place = lax.axis_index("dp") * 2 + lax.axis_index("seq")
    lane = 32 * lax.rem(place, 4)
    gains = jnp.zeros((2, 16, 128), BF)
    both = jnp.stack([attention_gain, feedforward_gain]).astype(BF)
    gains = lax.dynamic_update_slice(
        gains, jnp.broadcast_to(both[:, None, :], (2, 16, 32)), (0, 0, lane)
    ).reshape(32, 128)
    projection_t = projection_weight.T.astype(BF)
    sds = jax.ShapeDtypeStruct
    grid = (4, 2, 2, 2)
    send_sems, recv_sems = (pltpu.SemaphoreType.DMA((PIECES * n + 2,)) for n in (SENDS, RECVS))
    length = 2 * rows
    out = pl.pallas_call(
        forward_kernel,
        out_shape=(
            sds((rows, width), BF),
            sds((*grid, 128, 1024), BF),
            sds((4, *grid, 32, 1024), BF),
            sds((*grid, 32, 1408), BF),
            sds((*grid, 32, 1024), BF),
            sds((2, 8, width), F32),
            sds((rows, width), BF),
            sds((rows, width), BF),
            sds((2, rows, 256), BF),
            sds((rows, width), BF),
            sds((rows, width), F32),
            sds((rows, width), BF),
            sds((rows, 4096), BF),
            sds((4, 2 * rows, length), BF),
            sds((8, 256, width), BF),
        ),
        in_specs=[smem, hbm, hbm] + [vmem] * 7,
        out_specs=[hbm] * 15,
        scratch_shapes=[
            pltpu.VMEM((*grid, 32, 1408), BF),
            pltpu.VMEM((*grid, 32, 1024), BF),
            pltpu.VMEM((4, *grid, 32, 1024), BF),
            pltpu.VMEM((4, *grid, 128, 256), BF),
            pltpu.VMEM((rows, width), BF),
            pltpu.VMEM((rows, width), BF),
            pltpu.VMEM((rows, width), BF),
            pltpu.VMEM((rows, width), BF),
            pltpu.VMEM((2, rows, 256), BF),
            pltpu.VMEM((rows, width), BF),
            pltpu.VMEM((rows, width), F32),
            pltpu.VMEM((rows, width), BF),
            pltpu.VMEM((rows, 4096), BF),
            pltpu.VMEM((rows, 4096), BF),
            pltpu.VMEM((2, 2 * rows, length), BF),
            pltpu.VMEM((rows, length), F32),
            pltpu.VMEM((2, 8, width), F32),
            pltpu.VMEM((8, 256, width), BF),
            pltpu.VMEM((8, 256, width), BF),
            pltpu.VMEM((rows, width), BF),
            send_sems,
            recv_sems,
            pltpu.SemaphoreType.DMA((40,)),
        ],
        compiler_params=pltpu.CompilerParams(
            collective_id=0, has_side_effects=True, vmem_limit_bytes=VMEM_LIMIT
        ),
    )(
        prefix, x, gy, query_weight, key_weight, value_weight, gains, projection_t, up_weight, down_weight
    )
    layer_output, w2, w1, wa, wot, gain, n1, q, kv, a, hidden, n2, slope, p, down = out
    grad_x, g2, g1, go, ga = pl.pallas_call(
        backward_kernel,
        out_shape=(
            sds((rows, width), F32),
            sds((128, 1024), F32),
            sds((32, 4096), F32),
            sds((32, 1024), F32),
            sds((32, 1408), F32),
        ),
        in_specs=[hbm] * 16,
        out_specs=[hbm] + [vmem] * 4,
        scratch_shapes=[
            pltpu.VMEM((rows, width), BF),
            pltpu.VMEM((rows, width), BF),
            pltpu.VMEM((rows, width), F32),
            pltpu.VMEM((rows, width), F32),
            pltpu.VMEM((rows, width), BF),
            pltpu.VMEM((rows, width), BF),
            pltpu.VMEM((2, rows, 256), BF),
            pltpu.VMEM((2, 8, width), F32),
            pltpu.VMEM((4, 1024, 1024), BF),
            pltpu.VMEM((2, rows, 1024), BF),
            pltpu.VMEM((width, 256), BF),
            pltpu.VMEM((rows, width), BF),
            pltpu.VMEM((2, 8, width), F32),
            pltpu.VMEM((2, DH, length), F32),
            pltpu.VMEM((2, rows, 256), BF),
            pltpu.VMEM((rows, 256), BF),
            pltpu.VMEM((4, 2, 2, 128, 1024), BF),
            pltpu.VMEM((4, *grid, 32, 1024), BF),
            pltpu.VMEM((*grid, 32, 1024), BF),
            pltpu.VMEM((*grid, 32, 1408), BF),
            pltpu.VMEM((5, 4, 2, 2, 32, 1024), BF),
            pltpu.VMEM((4, 2, 2, 32, 1408), BF),
            pltpu.VMEM((4, 4, 128, 256), BF), pltpu.VMEM((5, 4, 32, 1024), BF), pltpu.VMEM((4, 32, 1408), BF),
            pltpu.VMEM((4, 2, 4, 128, 256), BF), pltpu.VMEM((5, 2, 4, 32, 1024), BF), pltpu.VMEM((2, 4, 32, 1408), BF),
            pltpu.VMEM((4, 3, 128, 256), BF), pltpu.VMEM((5, 3, 32, 1024), BF), pltpu.VMEM((3, 32, 1408), BF),
            pltpu.VMEM((4, 3, 2, 2, 16, 256), BF), pltpu.VMEM((5, 3, 2, 2, 32, 128), BF), pltpu.VMEM((3, 2, 2, 32, 128), BF),
            send_sems,
            recv_sems,
            pltpu.SemaphoreType.DMA((40,)),
        ],
        compiler_params=pltpu.CompilerParams(
            collective_id=1, has_side_effects=True, vmem_limit_bytes=VMEM_LIMIT
        ),
    )(
        x, gy, gain, w2.reshape(4, 1024, 1024), w1.reshape(4, 1024, 1024), wa.reshape(1024, 1408), wot.reshape(1024, 1024),
        n1, q, kv, a, hidden, n2, slope, p, down.reshape(4, 2, 2, 128, 1024),
    )
    gain_grads = lax.dynamic_slice(ga[:, 1280:].reshape(2, 16, 128)[:, 0], (0, lane), (2, 32))
    return (
        layer_output.reshape(tokens.shape),
        grad_x.reshape(tokens.shape),
        gain_grads[0],
        ga[:, :1024],
        ga[:, 1024:1152],
        ga[:, 1152:1280],
        go.T,
        gain_grads[1],
        g1,
        g2,
    )


def root_norm(values, gain):
    factor = lax.rsqrt(jnp.mean(values * values, axis=-1, keepdims=True) + epsilon)
    return values * factor * gain


def smooth_gate(values):
    return jax.nn.gelu(values, approximate=True)


def product(left, right):
    return jnp.dot(left, right, preferred_element_type=jnp.float32)


def inner_rows(left, right):
    return lax.dot_general(
        left, right, (((0,), (0,)), ((), ())), preferred_element_type=jnp.float32
    )


def outer_rows(left, right):
    return lax.dot_general(
        left, right, (((1,), (1,)), ((), ())), preferred_element_type=jnp.float32
    )


def local(
    tokens,
    cotangent,
    prefix,
    attention_gain,
    query_weight,
    key_weight,
    value_weight,
    projection_weight,
    feedforward_gain,
    up_weight,
    down_weight,
):
    seqs_here, span_len, model_width = tokens.shape
    length = span_len * lax.axis_size("seq")
    row_count = seqs_here * span_len
    block_len = min(64, span_len)
    block_count = span_len // block_len
    score_scale = DH ** (-0.5)
    gain_low = attention_gain.astype(jnp.bfloat16)
    query_low = query_weight.astype(jnp.bfloat16)
    key_low = key_weight.astype(jnp.bfloat16)
    value_low = value_weight.astype(jnp.bfloat16)
    projection_low = projection_weight.astype(jnp.bfloat16)
    second_low = feedforward_gain.astype(jnp.bfloat16)
    up_low = up_weight.astype(jnp.bfloat16)
    down_low = down_weight.astype(jnp.bfloat16)
    gathered = (
        lax.all_gather(gain_low, ("dp", "seq"), axis=0, tiled=True),
        lax.all_gather(query_low, ("dp", "seq"), axis=0, tiled=True),
        lax.all_gather(key_low, ("dp", "seq"), axis=0, tiled=True),
        lax.all_gather(value_low, ("dp", "seq"), axis=0, tiled=True),
        lax.all_gather(projection_low, ("dp", "seq"), axis=1, tiled=True),
        lax.all_gather(second_low, ("dp", "seq"), axis=0, tiled=True),
        lax.all_gather(up_low, ("dp", "seq"), axis=0, tiled=True),
        lax.all_gather(down_low, ("dp", "seq"), axis=0, tiled=True),
    )
    gain_one, query_full, key_full, value_full, projection_full, gain_two, up_full, down_full = (
        gathered
    )
    inputs = tokens.reshape(row_count, model_width).astype(jnp.float32)
    gain_first = gain_one.astype(jnp.float32)
    normed = root_norm(inputs, gain_first).astype(jnp.bfloat16)
    queries = product(normed, query_full).astype(jnp.bfloat16)
    pair_weight = jnp.concatenate([key_full, value_full], axis=1)
    pair_rows = product(normed, pair_weight).astype(jnp.bfloat16)
    key_own = pair_rows[:, :DH].reshape(seqs_here, span_len, DH)
    value_own = pair_rows[:, DH:].reshape(seqs_here, span_len, DH)
    key_all, value_all = (
        lax.all_gather(key_own, "seq", axis=1, tiled=True),
        lax.all_gather(value_own, "seq", axis=1, tiled=True),
    )
    query_pos = lax.axis_index("seq") * span_len + jnp.arange(span_len, dtype=jnp.int32)
    pos_blocks = query_pos.reshape(block_count, block_len)
    key_pos = jnp.arange(length, dtype=jnp.int32)

    def masked_scores(query_block, key_rows, positions, prefix_len):
        flat = query_block.reshape(block_len * H, DH)
        scores = (outer_rows(flat, key_rows) * score_scale).reshape(block_len, H, length)
        visible = (key_pos[None, :] <= positions[:, None]) | (key_pos[None, :] < prefix_len)
        return jnp.where(visible[:, None, :], scores, masked_score)

    def forward_sequence(members):
        query_blocks, key_rows, value_rows, prefix_len = members

        def forward_block(pieces):
            query_block, positions = pieces
            scores = masked_scores(query_block, key_rows, positions, prefix_len)
            maxima = jnp.max(scores, axis=-1, keepdims=True)
            exponent = jnp.exp(scores - maxima)
            totals = jnp.sum(exponent, axis=-1, keepdims=True)
            chances = (exponent / totals).astype(jnp.bfloat16)
            mixed = product(chances.reshape(block_len * H, length), value_rows)
            return (
                mixed.reshape(block_len, H * DH).astype(jnp.bfloat16),
                (maxima + jnp.log(totals))[..., 0],
            )

        return lax.map(forward_block, (query_blocks, pos_blocks))

    query_seq = queries.reshape(seqs_here, block_count, block_len, H, DH)
    attended, log_totals = lax.map(forward_sequence, (query_seq, key_all, value_all, prefix))
    attended = attended.reshape(row_count, H * DH)
    hidden = inputs + product(attended, projection_full)
    gain_second = gain_two.astype(jnp.float32)
    normed_two = root_norm(hidden, gain_second).astype(jnp.bfloat16)
    before = product(normed_two, up_full)
    active = smooth_gate(before).astype(jnp.bfloat16)
    layer_output = (hidden + product(active, down_full)).astype(jnp.bfloat16)
    gathered = (
        lax.all_gather(gain_low, ("dp", "seq"), axis=0, tiled=True),
        lax.all_gather(query_low, ("dp", "seq"), axis=0, tiled=True),
        lax.all_gather(key_low, ("dp", "seq"), axis=0, tiled=True),
        lax.all_gather(value_low, ("dp", "seq"), axis=0, tiled=True),
        lax.all_gather(projection_low, ("dp", "seq"), axis=1, tiled=True),
        lax.all_gather(second_low, ("dp", "seq"), axis=0, tiled=True),
        lax.all_gather(up_low, ("dp", "seq"), axis=0, tiled=True),
        lax.all_gather(down_low, ("dp", "seq"), axis=0, tiled=True),
    )
    gain_one, query_full, key_full, value_full, projection_full, gain_two, up_full, down_full = (
        gathered
    )
    gain_first = gain_one.astype(jnp.float32)
    gain_second = gain_two.astype(jnp.float32)
    pair_weight = jnp.concatenate([key_full, value_full], axis=1)
    grad_out = cotangent.reshape(row_count, model_width)
    grad_start = grad_out.astype(jnp.float32)
    down_grad = inner_rows(active, grad_out)
    grad_active = outer_rows(grad_out, down_full)
    _, gate_pull = jax.vjp(smooth_gate, before)
    grad_before = gate_pull(grad_active)[0].astype(jnp.bfloat16)
    up_grad = inner_rows(normed_two, grad_before)
    grad_normed_two = outer_rows(grad_before, up_full)
    _, second_pull = jax.vjp(root_norm, hidden, gain_second)
    grad_hidden_norm, feedforward_gain_grad = second_pull(grad_normed_two)
    grad_hidden = grad_start + grad_hidden_norm
    grad_branch = grad_hidden.astype(jnp.bfloat16)
    projection_grad = inner_rows(attended, grad_branch)
    grad_attended = outer_rows(grad_branch, projection_full).astype(jnp.bfloat16)
    key_all, value_all = (
        lax.all_gather(key_own, "seq", axis=1, tiled=True),
        lax.all_gather(value_own, "seq", axis=1, tiled=True),
    )
    grad_seq = grad_attended.reshape(seqs_here, block_count, block_len, H, DH)

    def backward_sequence(members):
        query_blocks, grad_blocks, total_blocks, key_rows, value_rows, prefix_len = members

        def backward_block(carry, pieces):
            key_sum, value_sum = carry
            query_block, grad_block, total_block, positions = pieces
            scores = masked_scores(query_block, key_rows, positions, prefix_len)
            chances = jnp.exp(scores - total_block[..., None])
            chance_low = chances.astype(jnp.bfloat16).reshape(block_len * H, length)
            grad_rows = grad_block.reshape(block_len * H, DH)
            query_rows = query_block.reshape(block_len * H, DH)
            grad_chances = outer_rows(grad_rows, value_rows).reshape(block_len, H, length)
            center = jnp.sum(chances * grad_chances, axis=-1, keepdims=True)
            grad_scores = (
                (chances * (grad_chances - center))
                .astype(jnp.bfloat16)
                .reshape(block_len * H, length)
            )
            grad_query = (product(grad_scores, key_rows) * score_scale).astype(jnp.bfloat16)
            key_sum = key_sum + inner_rows(grad_scores, query_rows) * score_scale
            value_sum = value_sum + inner_rows(chance_low, grad_rows)
            return ((key_sum, value_sum), grad_query.reshape(block_len, H * DH))

        empty_sum = jnp.zeros((length, DH), jnp.float32)
        (key_sum, value_sum), grad_queries = lax.scan(
            backward_block,
            (empty_sum, empty_sum),
            (query_blocks, grad_blocks, total_blocks, pos_blocks),
        )
        return (key_sum, value_sum, grad_queries)

    key_terms, value_terms, grad_queries = lax.map(
        backward_sequence, (query_seq, grad_seq, log_totals, key_all, value_all, prefix)
    )
    grad_keys, grad_values = (
        lax.psum_scatter(
            key_terms.astype(jnp.bfloat16), "seq", scatter_dimension=1, tiled=True
        ).astype(jnp.float32),
        lax.psum_scatter(
            value_terms.astype(jnp.bfloat16), "seq", scatter_dimension=1, tiled=True
        ).astype(jnp.float32),
    )
    grad_pair = jnp.concatenate(
        [grad_keys.reshape(row_count, DH), grad_values.reshape(row_count, DH)], axis=1
    ).astype(jnp.bfloat16)
    grad_query_rows = grad_queries.reshape(row_count, H * DH)
    query_grad = inner_rows(normed, grad_query_rows)
    pair_grad = inner_rows(normed, grad_pair)
    key_grad = pair_grad[:, :DH]
    value_grad = pair_grad[:, DH:]
    grad_normed = outer_rows(grad_query_rows, query_full) + outer_rows(grad_pair, pair_weight)
    _, first_pull = jax.vjp(root_norm, inputs, gain_first)
    grad_inputs_norm, attention_gain_grad = first_pull(grad_normed)
    input_grad = (grad_hidden + grad_inputs_norm).reshape(seqs_here, span_len, model_width)
    layer_output = layer_output.reshape(seqs_here, span_len, model_width)
    summed = (
        lax.psum_scatter(attention_gain_grad, ("dp", "seq"), scatter_dimension=0, tiled=True),
        lax.psum_scatter(query_grad, ("dp", "seq"), scatter_dimension=0, tiled=True),
        lax.psum_scatter(key_grad, ("dp", "seq"), scatter_dimension=0, tiled=True),
        lax.psum_scatter(value_grad, ("dp", "seq"), scatter_dimension=0, tiled=True),
        lax.psum_scatter(projection_grad, ("dp", "seq"), scatter_dimension=1, tiled=True),
        lax.psum_scatter(feedforward_gain_grad, ("dp", "seq"), scatter_dimension=0, tiled=True),
        lax.psum_scatter(up_grad, ("dp", "seq"), scatter_dimension=0, tiled=True),
        lax.psum_scatter(down_grad, ("dp", "seq"), scatter_dimension=0, tiled=True),
    )
    return (
        layer_output,
        input_grad,
        summed[0],
        summed[1],
        summed[2],
        summed[3],
        summed[4],
        summed[5],
        summed[6],
        summed[7],
    )


def fits(mesh, tokens, up_weight):
    return (
        mesh.shape["dp"] == 16
        and mesh.shape["seq"] == 2
        and tokens.shape == (16, 1024, 1024)
        and up_weight.shape == (1024, 4096)
    )


def solution(mesh):
    def layer(*args):
        return sharded(mesh, on_grid if fits(mesh, args[0], args[9]) else local)(*args)

    return layer


def sharded(mesh, part):
    return jax.shard_map(
        part,
        mesh=mesh,
        in_specs=(
            P("dp", "seq", None),
            P("dp", "seq", None),
            P("dp"),
            P(("dp", "seq")),
            P(("dp", "seq"), None),
            P(("dp", "seq"), None),
            P(("dp", "seq"), None),
            P(None, ("dp", "seq")),
            P(("dp", "seq")),
            P(("dp", "seq"), None),
            P(("dp", "seq"), None),
        ),
        out_specs=(
            P("dp", "seq", None),
            P("dp", "seq", None),
            P(("dp", "seq")),
            P(("dp", "seq"), None),
            P(("dp", "seq"), None),
            P(("dp", "seq"), None),
            P(None, ("dp", "seq")),
            P(("dp", "seq")),
            P(("dp", "seq"), None),
            P(("dp", "seq"), None),
        ),
        check_vma=False,
    )
```

```python
import functools
import jax
import jax.numpy as jnp
from jax import lax
from jax.experimental import pallas as pl
from jax.experimental.pallas import tpu as pltpu
from jax.sharding import PartitionSpec as P

H = 8
DH = 128
BF = jnp.bfloat16
F32 = jnp.float32
MESH = pl.DeviceIdType.MESH
VMEM_LIMIT = 61 * 2**20
GELU_C = 0.7978845608028654
GELU_A = 0.044715

epsilon = 1e-06
masked_score = -10000.0


def dot(left, right, left_dim, right_dim):
    return lax.dot_general(
        left, right, (((left_dim,), (right_dim,)), ((), ())), preferred_element_type=F32
    )


class Place:
    def __init__(self, send_sems, recv_sems, local_sems):
        dp = lax.axis_index("dp")
        self.y = lax.axis_index("seq")
        self.c = lax.rem(dp, 2)
        self.x = lax.rem(lax.div(dp, 2), 2)
        self.z = lax.div(dp, 4)
        self.send_sems, self.recv_sems, self.local_sems = send_sems, recv_sems, local_sems
        self.n_local = 0
        self.xn = self.at(self.z, 1 - self.x, self.c, self.y)
        self.yn = self.at(self.z, self.x, self.c, 1 - self.y)
        self.cn = self.at(self.z, self.x, 1 - self.c, self.y)

    def at(self, z, x, c, y):
        return ((z * 2 + x) * 2 + c, y)

    def z_to(self, step):
        return lax.rem(self.z + step, 4)

    def zn(self, step):
        return self.at(self.z_to(step), self.x, self.c, self.y)

    def greet(self):
        barrier = pltpu.get_barrier_semaphore()
        for device in (self.cn, self.xn, self.yn, self.zn(1), self.zn(2), self.zn(3)):
            pl.semaphore_signal(barrier, inc=1, device_id=device, device_id_type=MESH)
        pl.semaphore_wait(barrier, 6)

    def send(self, src, dst, recv, device, group):
        pltpu.make_async_remote_copy(
            src_ref=src,
            dst_ref=dst,
            send_sem=self.send_sems.at[group],
            recv_sem=self.recv_sems.at[recv],
            device_id=device,
            device_id_type=MESH,
        ).start()

    def wait(self, like, sem):
        pltpu.make_async_copy(like, like, sem).wait()

    def arrived(self, like, recv):
        self.wait(like, self.recv_sems.at[recv])

    def left(self, like, group):
        self.wait(like, self.send_sems.at[group])

    def move(self, src, dst):
        copy = pltpu.make_async_copy(src, dst, self.local_sems.at[self.n_local])
        self.n_local += 1
        copy.start()
        return copy


class Steps:
    def __init__(self, order):
        self.order, self.done = list(order), set()

    def next(self, count=1):
        for _ in range(count):
            if self.order and self.order[0][2]():
                step, i, _ready = self.order.pop(0)
                step(i)
                self.done.add((step, i))

    def until(self, step, i):
        while (step, i) not in self.done:
            self.next()

    def rest(self):
        while self.order:
            self.next()


def gelu_parts(u):
    square = u * u
    t = jnp.tanh(GELU_C * u * (1.0 + GELU_A * square))
    half = 0.5 * (1.0 + t)
    slope = half + (0.5 * GELU_C) * u * (1.0 - t * t) * (1.0 + (3.0 * GELU_A) * square)
    return u * half, slope


PIECES = 10
RECVS = 11
SENDS = 3


def cut(rows, cols):
    if rows < 128:
        first, second = (pl.ds(0, rows), pl.ds(0, cols - 128)), (pl.ds(0, rows), pl.ds(cols - 128, 128))
        halves = (pl.ds(0, rows // 2), first[1]), (pl.ds(rows // 2, rows // 2), first[1])
    else:
        edge = rows - rows // 8
        first, second = (pl.ds(0, edge), pl.ds(0, cols)), (pl.ds(edge, rows // 8), pl.ds(0, cols))
        halves = (pl.ds(0, 64), first[1]), (pl.ds(64, edge - 64), first[1])
    return first, second, halves


def forward_kernel(
    prefix_ref, x_hbm, gy_hbm, wq_hbm, wk_hbm, wv_hbm, g1_ref, g2_ref, wo_hbm, w1_hbm_in, w2_hbm_in,
    out_hbm, w2_hbm, w1_hbm, wa_hbm, wot_hbm, gain_hbm, n1_hbm, q_hbm, kv_hbm, a_hbm, hidden_hbm,
    n2_hbm, slope_hbm, p_hbm, down_hbm,
    wa, wot, w1, w2, x, gy, n1, q, kv, a, hidden, n2, z, slope, p, bias, gain, down_out, down_in, out,
    wq_in, wk_in, wv_in, wo_in, w1_in, w2_in,
    send_sems, recv_sems, local_sems,
):
    me = Place(send_sems, recv_sems, local_sems)
    rows, width = x.shape
    load_qkv = [me.move(src, dst) for src, dst in ((wq_hbm, wq_in), (wk_hbm, wk_in), (wv_hbm, wv_in))]
    load_x = me.move(x_hbm, x)
    load_wo = me.move(wo_hbm, wo_in)
    load_w1 = me.move(w1_hbm_in, w1_in)
    load_w2 = me.move(w2_hbm_in, w2_in)
    load_gy = me.move(gy_hbm, gy)
    views = [wa, wot] + [w1.at[j] for j in range(4)] + [w2.at[k] for k in range(4)]
    saves = []

    every = slice(None)
    own = (me.z, me.x, me.c, me.y)

    def pass_on(i, at, recv, device, group):
        view = views[i].at[at]
        me.send(view, view, i * RECVS + recv, device, i * SENDS + group)

    def came(i, at, recv):
        me.arrived(views[i].at[at], i * RECVS + recv)

    def s0(i):
        first, second, _ = cut(*views[i].shape[4:])
        for step in (1, 3, 2):
            pass_on(i, own + first, step - 1, me.zn(step), 0)
        pass_on(i, own + first, 3, me.xn, 1)
        pass_on(i, own + first, 4, me.yn, 1)
        pass_on(i, own + second, 5, me.xn, 0)
        pass_on(i, own + second, 6, me.yn, 0)

    def s1(i):
        first, second, _ = cut(*views[i].shape[4:])
        for step in (1, 3, 2):
            at = (me.z_to(4 - step), me.x, me.c, me.y) + first
            came(i, at, step - 1)
            pass_on(i, at, 3, me.xn, 1)
            pass_on(i, at, 4, me.yn, 1)
        from_x, from_y = (me.z, 1 - me.x, me.c, me.y) + second, (me.z, me.x, me.c, 1 - me.y) + second
        came(i, from_x, 5)
        came(i, from_y, 6)
        if i % 2:
            pass_on(i, from_y, 7, me.xn, 0)
        else:
            pass_on(i, from_x, 7, me.yn, 0)

    def s2(i):
        first, second, (low, high) = cut(*views[i].shape[4:])
        came(i, (every, 1 - me.x, me.c, me.y) + first, 3)
        pass_on(i, (every, 1 - me.x, me.c, me.y) + low, 9, me.yn, 1)
        came(i, (every, me.x, me.c, 1 - me.y) + first, 4)
        pass_on(i, (every, me.x, me.c, 1 - me.y) + high, 9, me.xn, 1)
        came(i, (me.z, 1 - me.x, me.c, 1 - me.y) + second, 7)
        for step in (1, 3, 2):
            pass_on(i, (me.z, every, me.c, every) + second, 8, me.zn(step), 1)

    def s3(i):
        first, second, _ = cut(*views[i].shape[4:])
        came(i, (every, 1 - me.x, me.c, 1 - me.y) + first, 9)
        came(i, (pl.ds(0, 3), every, me.c, every) + second, 8)
        pass_on(i, (every, every, me.c), 10, me.cn, 2)

    def s4(i):
        came(i, (every, every, 1 - me.c), 10)
        if i == 0:
            saves.append(me.move(wa, wa_hbm))
        elif i == 1:
            saves.append(me.move(wot, wot_hbm))
        elif i < 6:
            saves.append(me.move(w1.at[i - 2], w1_hbm.at[i - 2]))
        else:
            k = i - 6
            saves.append(me.move(w2.at[k], w2_hbm.at[:, :, :, :, :, pl.ds(256 * k, 256)]))

    def order():
        yield s0, 0
        for k in range(-1, PIECES + 3):
            for step, i in ((s1, k + 1), (s0, k + 2), (s2, k), (s3, k - 1), (s4, k - 2)):
                if 0 <= i < PIECES:
                    yield step, i

    steps = Steps((step, i, lambda: True) for step, i in order())

    for kind, ref in ((0, g1_ref), (1, g2_ref)):
        tile = jnp.concatenate([ref[...], jnp.zeros((1, 96), F32)], axis=1)
        for quarter in range(4):
            @pl.when(me.c * 2 + me.y == quarter)
            def _():
                placed = tile if quarter == 0 else pltpu.roll(tile, 32 * quarter, 1)
                wa[(*own, pl.ds(16 * kind, 16), pl.ds(1280, 128))] = jnp.broadcast_to(placed, (16, 128)).astype(BF)
    for load in load_qkv:
        load.wait()
    wa[(*own, every, pl.ds(0, 1024))] = wq_in[...].astype(BF)
    wa[(*own, every, pl.ds(1024, 128))] = wk_in[...].astype(BF)
    wa[(*own, every, pl.ds(1152, 128))] = wv_in[...].astype(BF)
    me.greet()
    steps.next()
    load_wo.wait()
    wot[own] = wo_in[...].astype(BF)
    load_w1.wait()
    for j in range(4):
        w1[(j, *own)] = w1_in[:, pl.ds(1024 * j, 1024)].astype(BF)
    load_w2.wait()
    for k in range(4):
        w2[(k, *own)] = w2_in[:, pl.ds(256 * k, 256)].astype(BF)
    steps.next(2)

    first_pos = me.y * rows

    @pl.loop(0, rows // 64)
    def _(t):
        at = pl.multiple_of(t * 64, 64)
        query_pos = first_pos + at + lax.broadcasted_iota(jnp.int32, (64, 2 * rows), 0)
        key_pos = lax.broadcasted_iota(jnp.int32, (64, 2 * rows), 1)
        visible = (key_pos <= query_pos) | (key_pos < prefix_ref[0])
        bias[pl.ds(at, 64), :] = jnp.where(visible, 0.0, -1e30)

    load_x.wait()
    load_gy.wait()
    steps.until(s4, 0)

    for kind in (0, 1):
        for zi in range(4):
            for xi in range(2):
                tile = jnp.zeros((16, 128), F32)
                for ci in range(2):
                    for yi in range(2):
                        tile += wa[zi, xi, ci, yi, pl.ds(16 * kind, 16), pl.ds(1280, 128)].astype(F32)
                gain[kind, :, pl.ds(128 * (2 * zi + xi), 128)] = tile[:8]
    saves.append(me.move(gain, gain_hbm))

    @pl.loop(0, rows // 64)
    def _(t):
        r = pl.ds(pl.multiple_of(t * 64, 64), 64)
        values = x[r, :].astype(F32)
        factor = lax.rsqrt(jnp.mean(values * values, axis=-1, keepdims=True) + epsilon)
        n1[r, :] = (values * factor * gain[0, 0:1, :]).astype(BF)

    kv[me.y] = dot(
        n1[...], wa[:, :, :, :, :, pl.ds(1024, 256)].reshape(width, 256), 1, 0
    ).astype(BF)
    me.send(kv.at[me.y], kv.at[me.y], PIECES * RECVS, me.yn, PIECES * SENDS)
    for i in range(2):
        steps.next()
        cols = pl.ds(512 * i, 512)
        q[:, cols] = dot(n1[...], wa[:, :, :, :, :, cols].reshape(width, 512), 1, 0).astype(BF)

    saves.append(me.move(n1, n1_hbm))
    saves.append(me.move(q, q_hbm))
    steps.next()
    me.arrived(kv.at[1 - me.y], PIECES * RECVS)
    saves.append(me.move(kv, kv_hbm))
    length = 2 * rows
    to_log2 = (DH ** -0.5) * 1.4426950408889634

    def head(h):
        cols = pl.ds(h * DH, DH)
        keys = kv[:, :, pl.ds(0, DH)].reshape(length, DH)
        vals = kv[:, :, pl.ds(DH, DH)].reshape(length, DH)
        for t in range(rows // 256):
            r = pl.ds(256 * t, 256)
            s = dot(q[r, cols], keys, 1, 1) * to_log2 + bias[r, :]
            e = jnp.exp2(s - jnp.max(s, axis=-1, keepdims=True))
            chances = (e * (1.0 / jnp.sum(e, axis=-1, keepdims=True))).astype(BF)
            p[(h // 2) % 2, pl.ds((h % 2) * rows + 256 * t, 256), :] = chances
            a[r, cols] = dot(chances, vals, 1, 0).astype(BF)

    p_saves = []
    for h in range(H):
        if h >= 4 and h % 2 == 0:
            p_saves[h // 2 - 2].wait()
        head(h)
        if h % 2:
            p_saves.append(me.move(p.at[(h // 2) % 2], p_hbm.at[h // 2]))
        steps.next()
    saves.extend(p_saves[2:])
    saves.append(me.move(a, a_hbm))
    steps.until(s4, 1)
    for i in range(2):
        cols = pl.ds(512 * i, 512)
        weight = wot[pl.ds(2 * i, 2)].reshape(512, width)
        hidden[:, cols] = x[:, cols].astype(F32) + dot(a[...], weight, 1, 1)
        steps.next()

    @pl.loop(0, rows // 64)
    def _(t):
        r = pl.ds(pl.multiple_of(t * 64, 64), 64)
        values = hidden[r, :]
        factor = lax.rsqrt(jnp.mean(values * values, axis=-1, keepdims=True) + epsilon)
        n2[r, :] = (values * factor * gain[1, 0:1, :]).astype(BF)

    saves.append(me.move(hidden, hidden_hbm))
    saves.append(me.move(n2, n2_hbm))
    steps.next()
    for j in range(4):
        steps.until(s4, 2 + j)
        for i in range(2):
            cols, to = pl.ds(512 * i, 512), pl.ds(1024 * j + 512 * i, 512)
            u = dot(n2[...], w1[j, :, :, :, :, :, cols].reshape(width, 512), 1, 0)
            active, steep = gelu_parts(u)
            z[:, to] = active.astype(BF)
            slope[:, to] = steep.astype(BF)
            steps.next()
    saves.append(me.move(slope, slope_hbm))

    for half in range(2):
        @pl.loop(4 * half, 4 * half + 4)
        def _(t):
            cols = pl.ds(pl.multiple_of((2 * t + 1 - me.c) * 256, 256), 256)
            down_out[t] = dot(z[:, cols], gy[...], 0, 0).astype(BF)

        steps.next(2)
    me.send(down_out, down_in, PIECES * RECVS + 1, me.cn, PIECES * SENDS + 1)

    def down(k):
        cols = pl.ds(256 * k, 256)
        for t in range(2):
            r = pl.ds(256 * t, 256)
            y = dot(z[r, :], w2[k].reshape(4096, 256), 1, 0)
            out[r, cols] = (hidden[r, cols] + y).astype(BF)

    steps.until(s4, 6)
    down(0)
    steps.next(2)
    me.arrived(down_in, PIECES * RECVS + 1)
    for half in range(2):
        @pl.loop(4 * half, 4 * half + 4)
        def _(t):
            cols = pl.ds(pl.multiple_of((2 * t + me.c) * 256, 256), 256)
            down_in[t] = (dot(z[:, cols], gy[...], 0, 0) + down_in[t].astype(F32)).astype(BF)

        steps.next(2)
    saves.append(me.move(down_in, down_hbm))
    for k in (1, 2, 3):
        steps.until(s4, 6 + k)
        down(k)
    steps.rest()
    saves.append(me.move(out, out_hbm))
    for copy in saves:
        copy.wait()
    for i in range(PIECES):
        me.left(views[i].at[pl.ds(0, 3), me.x, me.c, me.y], i * SENDS)
        me.left(views[i].at[pl.ds(0, 3), :, me.c], i * SENDS + 1)
        me.left(views[i].at[:, :, me.c], i * SENDS + 2)
    me.left(kv.at[me.y], PIECES * SENDS)
    me.left(down_out, PIECES * SENDS + 1)


def backward_kernel(
    x_hbm, gy_hbm, gain_hbm, w2_hbm, w1_hbm, wa_hbm, wot_hbm, n1_hbm, q_hbm, kv_hbm, a_hbm, hidden_hbm,
    n2_hbm, slope_hbm, p_hbm, down_hbm,
    grad_x_hbm, g2_ref, g1_ref, go_ref, ga_ref,
    gy, n2, hidden, gn, a, q, kv, gain, wbuf, gu, wkv, att, sums, kvsum, kvout, kvin,
    down, pup, pproj, patt, pair_up, pair_att, diag2, diag1, diaga, side2, side1, sidea, line2, line1, linea,
    plane2, plane1, planea,
    send_sems, recv_sems, local_sems,
):
    me = Place(send_sems, recv_sems, local_sems)
    rows, width = gy.shape
    length = 2 * rows
    load_down = [
        me.move(down_hbm.at[:, :, :, :, pl.ds(256 * k, 256)], down.at[:, :, :, :, pl.ds(256 * k, 256)])
        for k in range(4)
    ]
    load_gy = me.move(gy_hbm, gy)
    load_w2 = [me.move(w2_hbm.at[j], wbuf.at[j]) for j in range(2)]
    load_slope = [me.move(slope_hbm.at[:, pl.ds(1024 * j, 1024)], gu.at[j]) for j in range(2)]
    load_n2 = me.move(n2_hbm, n2)
    load_w1 = [me.move(w1_hbm.at[j], wbuf.at[2 + j]) for j in range(2)]
    load_rest = [
        me.move(src, dst)
        for src, dst in (
            (hidden_hbm, hidden), (gain_hbm, gain), (a_hbm, a), (q_hbm, q), (kv_hbm, kv),
            (wa_hbm.at[:, pl.ds(1024, 256)], wkv),
        )
    ]

    def source(i):
        return pup.at[i - 4] if i < 8 else pproj if i == 8 else patt

    def pair(i):
        return pair_up.at[i - 4] if i < 9 else pair_att

    def part(i, zi, xi, yi, at):
        if i < 4:
            return down.at[zi, xi, yi, at[0], pl.ds(256 * i + at[1].start, at[1].size)]
        return source(i).at[(zi, xi, me.c, yi) + at]

    def group(i, two, one, last):
        return two.at[i] if i < 4 else one.at[i - 4] if i < 9 else last

    def cut_of(i):
        return cut(*((128, 256) if i < 4 else (32, 1024) if i < 9 else (32, 1408)))

    every = slice(None)
    given = set(range(4))

    def send(src, dst, i, recv, device, to):
        me.send(src, dst, i * RECVS + recv, device, i * SENDS + to)

    def came(like, i, recv):
        me.arrived(like, i * RECVS + recv)

    def t0(i):
        send(source(i).at[:, :, 1 - me.c], pair(i), i, 0, me.cn, 2)
        given.add(i)

    def t1(i):
        first, second, (low, high) = cut_of(i)
        diag, plane = group(i, diag2, diag1, diaga), group(i, plane2, plane1, planea)
        if i < 4:
            load_down[i].wait()
        else:
            total, term = source(i), pair(i)
            came(term, i, 0)

            @pl.loop(0, 4)
            def _(zi):
                for xi in range(2):
                    total[zi, xi, me.c] = total[zi, xi, me.c] + term[zi, xi]

        send(part(i, every, 1 - me.x, 1 - me.y, low), diag.at[(every,) + low], i, 1, me.yn, 1)
        send(part(i, every, 1 - me.x, 1 - me.y, high), diag.at[(every,) + high], i, 1, me.xn, 1)
        for step in (1, 3, 2):
            send(part(i, me.z_to(step), every, every, second), plane.at[step - 1], i, 2, me.zn(step), 1)

    def t2(i):
        first, second, (low, high) = cut_of(i)
        diag, plane = group(i, diag2, diag1, diaga), group(i, plane2, plane1, planea)
        side = group(i, side2, side1, sidea)
        came(diag.at[(every,) + first], i, 1)
        for step in (1, 3, 2, 0):
            zi = me.z_to(step)
            for xi, yi, half in ((1 - me.x, me.y, low), (me.x, 1 - me.y, high)):
                mine = part(i, zi, xi, yi, half)
                mine[...] = mine[...] + diag[(zi,) + half]
            recv = 2 + step if step else 6
            send(part(i, zi, 1 - me.x, me.y, first), side.at[(0, zi) + first], i, recv, me.xn, 1)
            send(part(i, zi, me.x, 1 - me.y, first), side.at[(1, zi) + first], i, recv, me.yn, 1)
        came(plane, i, 2)
        for xi in range(2):
            for yi in range(2):
                mine = part(i, me.z, xi, yi, second)
                total = mine[...].astype(F32)
                for step in range(3):
                    total += plane[step, xi, yi].astype(F32)
                mine[...] = total.astype(BF)
        send(
            part(i, me.z, 1 - me.x, 1 - me.y, second), diag.at[(me.z,) + second], i, 7,
            me.xn if i % 2 else me.yn, 0,
        )

    def t3(i):
        first, second, _ = cut_of(i)
        diag, side = group(i, diag2, diag1, diaga), group(i, side2, side1, sidea)
        line = group(i, line2, line1, linea)
        for step in (1, 3, 2):
            zi = me.z_to(step)
            came(side.at[(every, zi) + first], i, 2 + step)
            mine = part(i, zi, me.x, me.y, first)
            total = mine[...].astype(F32) + side[(0, zi) + first].astype(F32) + side[(1, zi) + first].astype(F32)
            mine[...] = total.astype(BF)
            send(mine, line.at[(step - 1,) + first], i, 8, me.zn(step), 0)
        came(diag.at[(me.z,) + second], i, 7)
        mine = part(i, me.z, *((me.x, 1 - me.y) if i % 2 else (1 - me.x, me.y)), second)
        mine[...] = mine[...] + diag[(me.z,) + second]
        send(part(i, me.z, 1 - me.x, me.y, second), side.at[(0, me.z) + second], i, 9, me.xn, 0)
        send(part(i, me.z, me.x, 1 - me.y, second), side.at[(1, me.z) + second], i, 9, me.yn, 0)

    def t4(i):
        first, second, _ = cut_of(i)
        side, line = group(i, side2, side1, sidea), group(i, line2, line1, linea)
        came(side.at[(every, me.z) + first], i, 6)
        came(line.at[(every,) + first], i, 8)
        came(side.at[(every, me.z) + second], i, 9)
        out, shift = (
            (g2_ref, 256 * i) if i < 4 else (g1_ref, 1024 * (i - 4)) if i < 8 else (go_ref, 0) if i == 8 else (ga_ref, 0)
        )
        for at in (first, second):
            total = part(i, me.z, me.x, me.y, at)[...].astype(F32)
            total += side[(0, me.z) + at].astype(F32) + side[(1, me.z) + at].astype(F32)
            if at is first:
                for step in range(3):
                    total += line[(step,) + first].astype(F32)
            out[at[0], pl.ds(shift + at[1].start, at[1].size)] = total

    def order():
        yield t1, 0
        for k in range(PIECES + 2):
            for step, i in ((t1, k + 1), (t2, k), (t3, k - 1), (t4, k - 2)):
                if 0 <= i < PIECES:
                    yield step, i

    steps = Steps((step, i, lambda step=step, i=i: step is not t1 or i in given) for step, i in order())
    me.greet()
    steps.next()

    def feed_forward(j):
        slot = j % 2
        load_w2[j].wait()
        load_slope[j].wait()
        for i in range(2):
            cols = pl.ds(512 * i, 512)
            grad_active = dot(gy[...], wbuf[slot, cols, :], 1, 1)
            gu[slot, :, cols] = (grad_active * gu[slot, :, cols].astype(F32)).astype(BF)
        steps.next()
        if j < 2:
            load_w2.append(me.move(w2_hbm.at[j + 2], wbuf.at[slot]))
        elif j == 2:
            load_w2.append(me.move(wot_hbm, wbuf.at[0]))
        else:
            load_w2.append(me.move(p_hbm.at[1], wbuf.at[1]))
        for i in range(2):
            term = dot(n2[:, pl.ds(512 * i, 512)], gu[slot], 0, 0)
            pup[j, pl.ds(2 * i, 2)] = term.reshape(2, 2, 2, 2, 32, 1024).astype(BF)
        t0(4 + j)
        steps.next()
        load_w1[j].wait()
        for i in range(2):
            cols = pl.ds(512 * i, 512)
            term = dot(gu[slot], wbuf[2 + slot, cols, :], 1, 1)
            if j == 0:
                gn[:, cols] = term
            else:
                gn[:, cols] = gn[:, cols] + term
        if j < 2:
            load_slope.append(me.move(slope_hbm.at[:, pl.ds(1024 * (j + 2), 1024)], gu.at[slot]))
            load_w1.append(me.move(w1_hbm.at[j + 2], wbuf.at[2 + slot]))
        else:
            load_w1.append(me.move(p_hbm.at[(0, 2)[j - 2]], wbuf.at[2 + slot]))
        steps.next()

    load_gy.wait()
    load_n2.wait()
    for j in range(4):
        feed_forward(j)
    load_x = me.move(x_hbm, n2)
    for copy in load_rest:
        copy.wait()

    sums[...] = jnp.zeros_like(sums)

    @pl.loop(0, rows // 64)
    def _(t):
        r = pl.ds(pl.multiple_of(t * 64, 64), 64)
        grad, values = gn[r, :], hidden[r, :]
        factor = lax.rsqrt(jnp.mean(values * values, axis=-1, keepdims=True) + epsilon)
        scaled = grad * gain[1, 0:1, :]
        middle = jnp.mean(scaled * values, axis=-1, keepdims=True)
        total = gy[r, :].astype(F32) + factor * scaled - values * (factor * factor * factor * middle)
        sums[1] += jnp.sum((grad * values * factor).reshape(8, 8, width), axis=0)
        gn[r, :] = total
        gy[r, :] = total.astype(BF)

    for i in range(2):
        term = dot(gy[:, pl.ds(512 * i, 512)], a[...], 0, 0)
        pproj[pl.ds(2 * i, 2)] = term.reshape(2, 2, 2, 2, 32, width).astype(BF)
    t0(8)
    steps.next()
    load_w2[4].wait()
    for i in range(2):
        cols = pl.ds(512 * i, 512)
        att[:, cols] = dot(gy[...], wbuf[0, :, cols], 1, 0).astype(BF)
    load_p3 = me.move(p_hbm.at[3], wbuf.at[0])
    load_n1 = me.move(n1_hbm, gy)
    steps.next()
    kvsum[...] = jnp.zeros_like(kvsum)
    scale = DH ** -0.5

    def head(h):
        slot = (2, 1, 3, 0)[h // 2]
        cols = pl.ds(h * DH, DH)
        keys = kv[:, :, pl.ds(0, DH)].reshape(length, DH)
        vals = kv[:, :, pl.ds(DH, DH)].reshape(length, DH)
        for t in range(rows // 256):
            r = pl.ds(256 * t, 256)
            grad = att[r, cols]
            chances = wbuf[slot, pl.ds((h % 2) * rows + 256 * t, 256), :]
            grad_chances = dot(grad, vals, 1, 1)
            wide = chances.astype(F32)
            center = jnp.sum(wide * grad_chances, axis=-1, keepdims=True)
            grad_scores = (wide * (grad_chances - center)).astype(BF)
            kvsum[0] += dot(q[r, cols], grad_scores, 0, 0)
            kvsum[1] += dot(grad, chances, 0, 0)
            att[r, cols] = (dot(grad_scores, keys, 1, 0) * scale).astype(BF)

    load_p = (load_w1[4], load_w2[5], load_w1[5], load_p3)
    for h in range(H):
        if h % 2 == 0:
            load_p[h // 2].wait()
        head(h)
        if h == 1:
            load_wq = me.move(wa_hbm.at[:, pl.ds(0, 1024)], wbuf.at[2])
        steps.next()
    for half in (0, 1):
        cols = pl.ds(half * rows, rows)
        kvout[half, :, pl.ds(0, DH)] = (kvsum[0, :, cols] * scale).T.astype(BF)
        kvout[half, :, pl.ds(DH, DH)] = kvsum[1, :, cols].T.astype(BF)
    me.send(kvout.at[1 - me.y], kvin, PIECES * RECVS, me.yn, PIECES * SENDS)
    load_n1.wait()
    for i in range(2):
        term = dot(gy[:, pl.ds(512 * i, 512)], att[...], 0, 0)
        patt[pl.ds(2 * i, 2), :, :, :, :, pl.ds(0, 1024)] = term.reshape(2, 2, 2, 2, 32, width).astype(BF)
    steps.next()
    me.arrived(kvin, PIECES * RECVS)
    kvin[...] = kvin[...] + kvout[me.y]
    for i in range(2):
        term = dot(gy[:, pl.ds(512 * i, 512)], kvin[...], 0, 0)
        patt[pl.ds(2 * i, 2), :, :, :, :, pl.ds(1024, 256)] = term.reshape(2, 2, 2, 2, 32, 256).astype(BF)
    load_wq.wait()
    for i in range(2):
        cols = pl.ds(512 * i, 512)
        hidden[:, cols] = dot(att[...], wbuf[2, cols, :], 1, 1) + dot(kvin[...], wkv[cols, :], 1, 1)
        steps.next()
    load_x.wait()

    @pl.loop(0, rows // 64)
    def _(t):
        r = pl.ds(pl.multiple_of(t * 64, 64), 64)
        grad, values = hidden[r, :], n2[r, :].astype(F32)
        factor = lax.rsqrt(jnp.mean(values * values, axis=-1, keepdims=True) + epsilon)
        scaled = grad * gain[0, 0:1, :]
        middle = jnp.mean(scaled * values, axis=-1, keepdims=True)
        sums[0] += jnp.sum((grad * values * factor).reshape(8, 8, width), axis=0)
        gn[r, :] = gn[r, :] + factor * scaled - values * (factor * factor * factor * middle)

    save_x = me.move(gn, grad_x_hbm)
    for kind in (0, 1):
        row = jnp.sum(sums[kind], axis=0, keepdims=True)
        for zi in range(4):
            for xi in range(2):
                lanes = slice(128 * (2 * zi + xi), 128 * (2 * zi + xi) + 128)
                tile = jnp.broadcast_to(row[:, lanes], (16, 128)).astype(BF)
                for ci in range(2):
                    for yi in range(2):
                        patt[zi, xi, ci, yi, pl.ds(16 * kind, 16), pl.ds(1280, 128)] = tile
    t0(9)
    steps.rest()
    save_x.wait()
    for i in range(PIECES):
        if i < 4:
            at = (every, pl.ds(256 * i, 256))
            me.left(down.at[(pl.ds(0, 3), 0, 0) + at], i * SENDS)
            me.left(down.at[(pl.ds(0, 3), every, every) + at], i * SENDS + 1)
        else:
            me.left(source(i).at[pl.ds(0, 3), 0, 0, 0], i * SENDS)
            me.left(source(i).at[pl.ds(0, 3), :, 0], i * SENDS + 1)
            me.left(source(i).at[:, :, 0], i * SENDS + 2)
    me.left(kvin, PIECES * SENDS)


def on_grid(
    tokens, cotangent, prefix, attention_gain, query_weight, key_weight, value_weight, projection_weight,
    feedforward_gain, up_weight, down_weight,
):
    rows, width = tokens.shape[1:]
    vmem, hbm = pl.BlockSpec(memory_space=pltpu.VMEM), pl.BlockSpec(memory_space=pl.ANY)
    smem = pl.BlockSpec(memory_space=pltpu.SMEM)
    x, gy = tokens.reshape(rows, width), cotangent.reshape(rows, width)
    sds = jax.ShapeDtypeStruct
    grid = (4, 2, 2, 2)
    send_sems, recv_sems = (pltpu.SemaphoreType.DMA((PIECES * n + 2,)) for n in (SENDS, RECVS))
    length = 2 * rows
    out = pl.pallas_call(
        forward_kernel,
        out_shape=(
            sds((rows, width), BF),
            sds((*grid, 128, 1024), BF),
            sds((4, *grid, 32, 1024), BF),
            sds((*grid, 32, 1408), BF),
            sds((*grid, 32, 1024), BF),
            sds((2, 8, width), F32),
            sds((rows, width), BF),
            sds((rows, width), BF),
            sds((2, rows, 256), BF),
            sds((rows, width), BF),
            sds((rows, width), F32),
            sds((rows, width), BF),
            sds((rows, 4096), BF),
            sds((4, 2 * rows, length), BF),
            sds((8, 256, width), BF),
        ),
        in_specs=[smem] + [hbm] * 5 + [vmem] * 2 + [hbm] * 3,
        out_specs=[hbm] * 15,
        scratch_shapes=[
            pltpu.VMEM((*grid, 32, 1408), BF),
            pltpu.VMEM((*grid, 32, 1024), BF),
            pltpu.VMEM((4, *grid, 32, 1024), BF),
            pltpu.VMEM((4, *grid, 128, 256), BF),
            pltpu.VMEM((rows, width), BF),
            pltpu.VMEM((rows, width), BF),
            pltpu.VMEM((rows, width), BF),
            pltpu.VMEM((rows, width), BF),
            pltpu.VMEM((2, rows, 256), BF),
            pltpu.VMEM((rows, width), BF),
            pltpu.VMEM((rows, width), F32),
            pltpu.VMEM((rows, width), BF),
            pltpu.VMEM((rows, 4096), BF),
            pltpu.VMEM((rows, 4096), BF),
            pltpu.VMEM((2, 2 * rows, length), BF),
            pltpu.VMEM((rows, length), F32),
            pltpu.VMEM((2, 8, width), F32),
            pltpu.VMEM((8, 256, width), BF),
            pltpu.VMEM((8, 256, width), BF),
            pltpu.VMEM((rows, width), BF),
            pltpu.VMEM(query_weight.shape, F32),
            pltpu.VMEM(key_weight.shape, F32),
            pltpu.VMEM(value_weight.shape, F32),
            pltpu.VMEM((32, width), F32),
            pltpu.VMEM(up_weight.shape, F32),
            pltpu.VMEM(down_weight.shape, F32),
            send_sems,
            recv_sems,
            pltpu.SemaphoreType.DMA((40,)),
        ],
        compiler_params=pltpu.CompilerParams(
            collective_id=0, has_side_effects=True, vmem_limit_bytes=VMEM_LIMIT
        ),
    )(
        prefix, x, gy, query_weight, key_weight, value_weight, attention_gain.reshape(1, 32),
        feedforward_gain.reshape(1, 32), projection_weight.T, up_weight, down_weight,
    )
    layer_output, w2, w1, wa, wot, gain, n1, q, kv, a, hidden, n2, slope, p, down = out
    grad_x, g2, g1, go, ga = pl.pallas_call(
        backward_kernel,
        out_shape=(
            sds((rows, width), F32),
            sds((128, 1024), F32),
            sds((32, 4096), F32),
            sds((32, 1024), F32),
            sds((32, 1408), F32),
        ),
        in_specs=[hbm] * 16,
        out_specs=[hbm] + [vmem] * 4,
        scratch_shapes=[
            pltpu.VMEM((rows, width), BF),
            pltpu.VMEM((rows, width), BF),
            pltpu.VMEM((rows, width), F32),
            pltpu.VMEM((rows, width), F32),
            pltpu.VMEM((rows, width), BF),
            pltpu.VMEM((rows, width), BF),
            pltpu.VMEM((2, rows, 256), BF),
            pltpu.VMEM((2, 8, width), F32),
            pltpu.VMEM((4, 1024, 1024), BF),
            pltpu.VMEM((2, rows, 1024), BF),
            pltpu.VMEM((width, 256), BF),
            pltpu.VMEM((rows, width), BF),
            pltpu.VMEM((2, 8, width), F32),
            pltpu.VMEM((2, DH, length), F32),
            pltpu.VMEM((2, rows, 256), BF),
            pltpu.VMEM((rows, 256), BF),
            pltpu.VMEM((4, 2, 2, 128, 1024), BF),
            pltpu.VMEM((4, *grid, 32, 1024), BF),
            pltpu.VMEM((*grid, 32, 1024), BF),
            pltpu.VMEM((*grid, 32, 1408), BF),
            pltpu.VMEM((5, 4, 2, 2, 32, 1024), BF),
            pltpu.VMEM((4, 2, 2, 32, 1408), BF),
            pltpu.VMEM((4, 4, 128, 256), BF), pltpu.VMEM((5, 4, 32, 1024), BF), pltpu.VMEM((4, 32, 1408), BF),
            pltpu.VMEM((4, 2, 4, 128, 256), BF), pltpu.VMEM((5, 2, 4, 32, 1024), BF), pltpu.VMEM((2, 4, 32, 1408), BF),
            pltpu.VMEM((4, 3, 128, 256), BF), pltpu.VMEM((5, 3, 32, 1024), BF), pltpu.VMEM((3, 32, 1408), BF),
            pltpu.VMEM((4, 3, 2, 2, 16, 256), BF), pltpu.VMEM((5, 3, 2, 2, 32, 128), BF), pltpu.VMEM((3, 2, 2, 32, 128), BF),
            send_sems,
            recv_sems,
            pltpu.SemaphoreType.DMA((40,)),
        ],
        compiler_params=pltpu.CompilerParams(
            collective_id=1, has_side_effects=True, vmem_limit_bytes=VMEM_LIMIT
        ),
    )(
        x, gy, gain, w2.reshape(4, 1024, 1024), w1.reshape(4, 1024, 1024), wa.reshape(1024, 1408), wot.reshape(1024, 1024),
        n1, q, kv, a, hidden, n2, slope, p, down.reshape(4, 2, 2, 128, 1024),
    )
    layer_output, grad_x, g1_gain, gq, gk, gv, gp, g2_gain, g1, g2 = pl.pallas_call(
        hand_out,
        out_shape=(
            sds((rows, width), BF),
            sds((rows, width), F32),
            sds((1, 32), F32),
            sds((32, 1024), F32),
            sds((32, 128), F32),
            sds((32, 128), F32),
            sds((32, 1024), F32),
            sds((1, 32), F32),
            sds((32, 4096), F32),
            sds((128, 1024), F32),
        ),
        in_specs=[hbm] * 6,
        out_specs=[hbm, hbm, vmem, hbm, hbm, hbm, hbm, vmem, hbm, hbm],
        scratch_shapes=[
            pltpu.VMEM((rows, width), BF),
            pltpu.VMEM((rows, width), F32),
            pltpu.VMEM((32, 1408), F32),
            pltpu.VMEM((32, 1024), F32),
            pltpu.VMEM((32, 4096), F32),
            pltpu.VMEM((128, 1024), F32),
            pltpu.SemaphoreType.DMA((16,)),
        ],
        compiler_params=pltpu.CompilerParams(vmem_limit_bytes=VMEM_LIMIT),
    )(layer_output, grad_x, ga, go, g1, g2)
    return (
        layer_output.reshape(tokens.shape),
        grad_x.reshape(tokens.shape),
        g1_gain.reshape(32),
        gq,
        gk,
        gv,
        gp.T,
        g2_gain.reshape(32),
        g1,
        g2,
    )


def hand_out(
    y_in, x_in, a_in, p_in, up_in, down_in,
    y_out, x_out, g1_out, q_out, k_out, v_out, p_out, g2_out, up_out, down_out,
    y, x, a, p, up, down, sems,
):
    started = 0

    def move(src, dst):
        nonlocal started
        copy = pltpu.make_async_copy(src, dst, sems.at[started])
        started += 1
        copy.start()
        return copy

    loads = [move(src, dst) for src, dst in ((a_in, a), (p_in, p), (x_in, x), (y_in, y), (up_in, up), (down_in, down))]
    stores = []
    loads[0].wait()
    for cols, out in ((pl.ds(0, 1024), q_out), (pl.ds(1024, 128), k_out), (pl.ds(1152, 128), v_out)):
        stores.append(move(a.at[:, cols], out))
    for load, src, dst in zip(loads[1:], (p, x, y, up, down), (p_out, x_out, y_out, up_out, down_out)):
        load.wait()
        stores.append(move(src, dst))
    quarter = lax.rem(lax.axis_index("dp"), 2) * 2 + lax.axis_index("seq")
    for row, out in ((0, g1_out), (16, g2_out)):
        for k in range(4):
            @pl.when(quarter == k)
            def _():
                out[...] = a[row : row + 1, 1280 + 32 * k : 1312 + 32 * k]
    for copy in stores:
        copy.wait()


def root_norm(values, gain):
    factor = lax.rsqrt(jnp.mean(values * values, axis=-1, keepdims=True) + epsilon)
    return values * factor * gain


def smooth_gate(values):
    return jax.nn.gelu(values, approximate=True)


def product(left, right):
    return jnp.dot(left, right, preferred_element_type=jnp.float32)


def inner_rows(left, right):
    return lax.dot_general(
        left, right, (((0,), (0,)), ((), ())), preferred_element_type=jnp.float32
    )


def outer_rows(left, right):
    return lax.dot_general(
        left, right, (((1,), (1,)), ((), ())), preferred_element_type=jnp.float32
    )


def local(
    tokens,
    cotangent,
    prefix,
    attention_gain,
    query_weight,
    key_weight,
    value_weight,
    projection_weight,
    feedforward_gain,
    up_weight,
    down_weight,
):
    seqs_here, span_len, model_width = tokens.shape
    length = span_len * lax.axis_size("seq")
    row_count = seqs_here * span_len
    block_len = min(64, span_len)
    block_count = span_len // block_len
    score_scale = DH ** (-0.5)
    gain_low = attention_gain.astype(jnp.bfloat16)
    query_low = query_weight.astype(jnp.bfloat16)
    key_low = key_weight.astype(jnp.bfloat16)
    value_low = value_weight.astype(jnp.bfloat16)
    projection_low = projection_weight.astype(jnp.bfloat16)
    second_low = feedforward_gain.astype(jnp.bfloat16)
    up_low = up_weight.astype(jnp.bfloat16)
    down_low = down_weight.astype(jnp.bfloat16)
    gathered = (
        lax.all_gather(gain_low, ("dp", "seq"), axis=0, tiled=True),
        lax.all_gather(query_low, ("dp", "seq"), axis=0, tiled=True),
        lax.all_gather(key_low, ("dp", "seq"), axis=0, tiled=True),
        lax.all_gather(value_low, ("dp", "seq"), axis=0, tiled=True),
        lax.all_gather(projection_low, ("dp", "seq"), axis=1, tiled=True),
        lax.all_gather(second_low, ("dp", "seq"), axis=0, tiled=True),
        lax.all_gather(up_low, ("dp", "seq"), axis=0, tiled=True),
        lax.all_gather(down_low, ("dp", "seq"), axis=0, tiled=True),
    )
    gain_one, query_full, key_full, value_full, projection_full, gain_two, up_full, down_full = (
        gathered
    )
    inputs = tokens.reshape(row_count, model_width).astype(jnp.float32)
    gain_first = gain_one.astype(jnp.float32)
    normed = root_norm(inputs, gain_first).astype(jnp.bfloat16)
    queries = product(normed, query_full).astype(jnp.bfloat16)
    pair_weight = jnp.concatenate([key_full, value_full], axis=1)
    pair_rows = product(normed, pair_weight).astype(jnp.bfloat16)
    key_own = pair_rows[:, :DH].reshape(seqs_here, span_len, DH)
    value_own = pair_rows[:, DH:].reshape(seqs_here, span_len, DH)
    key_all, value_all = (
        lax.all_gather(key_own, "seq", axis=1, tiled=True),
        lax.all_gather(value_own, "seq", axis=1, tiled=True),
    )
    query_pos = lax.axis_index("seq") * span_len + jnp.arange(span_len, dtype=jnp.int32)
    pos_blocks = query_pos.reshape(block_count, block_len)
    key_pos = jnp.arange(length, dtype=jnp.int32)

    def masked_scores(query_block, key_rows, positions, prefix_len):
        flat = query_block.reshape(block_len * H, DH)
        scores = (outer_rows(flat, key_rows) * score_scale).reshape(block_len, H, length)
        visible = (key_pos[None, :] <= positions[:, None]) | (key_pos[None, :] < prefix_len)
        return jnp.where(visible[:, None, :], scores, masked_score)

    def forward_sequence(members):
        query_blocks, key_rows, value_rows, prefix_len = members

        def forward_block(pieces):
            query_block, positions = pieces
            scores = masked_scores(query_block, key_rows, positions, prefix_len)
            maxima = jnp.max(scores, axis=-1, keepdims=True)
            exponent = jnp.exp(scores - maxima)
            totals = jnp.sum(exponent, axis=-1, keepdims=True)
            chances = (exponent / totals).astype(jnp.bfloat16)
            mixed = product(chances.reshape(block_len * H, length), value_rows)
            return (
                mixed.reshape(block_len, H * DH).astype(jnp.bfloat16),
                (maxima + jnp.log(totals))[..., 0],
            )

        return lax.map(forward_block, (query_blocks, pos_blocks))

    query_seq = queries.reshape(seqs_here, block_count, block_len, H, DH)
    attended, log_totals = lax.map(forward_sequence, (query_seq, key_all, value_all, prefix))
    attended = attended.reshape(row_count, H * DH)
    hidden = inputs + product(attended, projection_full)
    gain_second = gain_two.astype(jnp.float32)
    normed_two = root_norm(hidden, gain_second).astype(jnp.bfloat16)
    before = product(normed_two, up_full)
    active = smooth_gate(before).astype(jnp.bfloat16)
    layer_output = (hidden + product(active, down_full)).astype(jnp.bfloat16)
    gathered = (
        lax.all_gather(gain_low, ("dp", "seq"), axis=0, tiled=True),
        lax.all_gather(query_low, ("dp", "seq"), axis=0, tiled=True),
        lax.all_gather(key_low, ("dp", "seq"), axis=0, tiled=True),
        lax.all_gather(value_low, ("dp", "seq"), axis=0, tiled=True),
        lax.all_gather(projection_low, ("dp", "seq"), axis=1, tiled=True),
        lax.all_gather(second_low, ("dp", "seq"), axis=0, tiled=True),
        lax.all_gather(up_low, ("dp", "seq"), axis=0, tiled=True),
        lax.all_gather(down_low, ("dp", "seq"), axis=0, tiled=True),
    )
    gain_one, query_full, key_full, value_full, projection_full, gain_two, up_full, down_full = (
        gathered
    )
    gain_first = gain_one.astype(jnp.float32)
    gain_second = gain_two.astype(jnp.float32)
    pair_weight = jnp.concatenate([key_full, value_full], axis=1)
    grad_out = cotangent.reshape(row_count, model_width)
    grad_start = grad_out.astype(jnp.float32)
    down_grad = inner_rows(active, grad_out)
    grad_active = outer_rows(grad_out, down_full)
    _, gate_pull = jax.vjp(smooth_gate, before)
    grad_before = gate_pull(grad_active)[0].astype(jnp.bfloat16)
    up_grad = inner_rows(normed_two, grad_before)
    grad_normed_two = outer_rows(grad_before, up_full)
    _, second_pull = jax.vjp(root_norm, hidden, gain_second)
    grad_hidden_norm, feedforward_gain_grad = second_pull(grad_normed_two)
    grad_hidden = grad_start + grad_hidden_norm
    grad_branch = grad_hidden.astype(jnp.bfloat16)
    projection_grad = inner_rows(attended, grad_branch)
    grad_attended = outer_rows(grad_branch, projection_full).astype(jnp.bfloat16)
    key_all, value_all = (
        lax.all_gather(key_own, "seq", axis=1, tiled=True),
        lax.all_gather(value_own, "seq", axis=1, tiled=True),
    )
    grad_seq = grad_attended.reshape(seqs_here, block_count, block_len, H, DH)

    def backward_sequence(members):
        query_blocks, grad_blocks, total_blocks, key_rows, value_rows, prefix_len = members

        def backward_block(carry, pieces):
            key_sum, value_sum = carry
            query_block, grad_block, total_block, positions = pieces
            scores = masked_scores(query_block, key_rows, positions, prefix_len)
            chances = jnp.exp(scores - total_block[..., None])
            chance_low = chances.astype(jnp.bfloat16).reshape(block_len * H, length)
            grad_rows = grad_block.reshape(block_len * H, DH)
            query_rows = query_block.reshape(block_len * H, DH)
            grad_chances = outer_rows(grad_rows, value_rows).reshape(block_len, H, length)
            center = jnp.sum(chances * grad_chances, axis=-1, keepdims=True)
            grad_scores = (
                (chances * (grad_chances - center))
                .astype(jnp.bfloat16)
                .reshape(block_len * H, length)
            )
            grad_query = (product(grad_scores, key_rows) * score_scale).astype(jnp.bfloat16)
            key_sum = key_sum + inner_rows(grad_scores, query_rows) * score_scale
            value_sum = value_sum + inner_rows(chance_low, grad_rows)
            return ((key_sum, value_sum), grad_query.reshape(block_len, H * DH))

        empty_sum = jnp.zeros((length, DH), jnp.float32)
        (key_sum, value_sum), grad_queries = lax.scan(
            backward_block,
            (empty_sum, empty_sum),
            (query_blocks, grad_blocks, total_blocks, pos_blocks),
        )
        return (key_sum, value_sum, grad_queries)

    key_terms, value_terms, grad_queries = lax.map(
        backward_sequence, (query_seq, grad_seq, log_totals, key_all, value_all, prefix)
    )
    grad_keys, grad_values = (
        lax.psum_scatter(
            key_terms.astype(jnp.bfloat16), "seq", scatter_dimension=1, tiled=True
        ).astype(jnp.float32),
        lax.psum_scatter(
            value_terms.astype(jnp.bfloat16), "seq", scatter_dimension=1, tiled=True
        ).astype(jnp.float32),
    )
    grad_pair = jnp.concatenate(
        [grad_keys.reshape(row_count, DH), grad_values.reshape(row_count, DH)], axis=1
    ).astype(jnp.bfloat16)
    grad_query_rows = grad_queries.reshape(row_count, H * DH)
    query_grad = inner_rows(normed, grad_query_rows)
    pair_grad = inner_rows(normed, grad_pair)
    key_grad = pair_grad[:, :DH]
    value_grad = pair_grad[:, DH:]
    grad_normed = outer_rows(grad_query_rows, query_full) + outer_rows(grad_pair, pair_weight)
    _, first_pull = jax.vjp(root_norm, inputs, gain_first)
    grad_inputs_norm, attention_gain_grad = first_pull(grad_normed)
    input_grad = (grad_hidden + grad_inputs_norm).reshape(seqs_here, span_len, model_width)
    layer_output = layer_output.reshape(seqs_here, span_len, model_width)
    summed = (
        lax.psum_scatter(attention_gain_grad, ("dp", "seq"), scatter_dimension=0, tiled=True),
        lax.psum_scatter(query_grad, ("dp", "seq"), scatter_dimension=0, tiled=True),
        lax.psum_scatter(key_grad, ("dp", "seq"), scatter_dimension=0, tiled=True),
        lax.psum_scatter(value_grad, ("dp", "seq"), scatter_dimension=0, tiled=True),
        lax.psum_scatter(projection_grad, ("dp", "seq"), scatter_dimension=1, tiled=True),
        lax.psum_scatter(feedforward_gain_grad, ("dp", "seq"), scatter_dimension=0, tiled=True),
        lax.psum_scatter(up_grad, ("dp", "seq"), scatter_dimension=0, tiled=True),
        lax.psum_scatter(down_grad, ("dp", "seq"), scatter_dimension=0, tiled=True),
    )
    return (
        layer_output,
        input_grad,
        summed[0],
        summed[1],
        summed[2],
        summed[3],
        summed[4],
        summed[5],
        summed[6],
        summed[7],
    )


def fits(mesh, tokens, up_weight):
    return (
        mesh.shape["dp"] == 16
        and mesh.shape["seq"] == 2
        and tokens.shape == (16, 1024, 1024)
        and up_weight.shape == (1024, 4096)
    )


def solution(mesh):
    def layer(*args):
        return sharded(mesh, on_grid if fits(mesh, args[0], args[9]) else local)(*args)

    return layer


def sharded(mesh, part):
    return jax.shard_map(
        part,
        mesh=mesh,
        in_specs=(
            P("dp", "seq", None),
            P("dp", "seq", None),
            P("dp"),
            P(("dp", "seq")),
            P(("dp", "seq"), None),
            P(("dp", "seq"), None),
            P(("dp", "seq"), None),
            P(None, ("dp", "seq")),
            P(("dp", "seq")),
            P(("dp", "seq"), None),
            P(("dp", "seq"), None),
        ),
        out_specs=(
            P("dp", "seq", None),
            P("dp", "seq", None),
            P(("dp", "seq")),
            P(("dp", "seq"), None),
            P(("dp", "seq"), None),
            P(("dp", "seq"), None),
            P(None, ("dp", "seq")),
            P(("dp", "seq")),
            P(("dp", "seq"), None),
            P(("dp", "seq"), None),
        ),
        check_vma=False,
    )
```

```python
import functools
import jax
import jax.numpy as jnp
from jax import lax
from jax.experimental import pallas as pl
from jax.experimental.pallas import tpu as pltpu
from jax.sharding import PartitionSpec as P

H = 8
DH = 128
BF = jnp.bfloat16
F32 = jnp.float32
MESH = pl.DeviceIdType.MESH
VMEM_LIMIT = 61 * 2**20
GELU_C = 0.7978845608028654
GELU_A = 0.044715

epsilon = 1e-06
masked_score = -10000.0


def dot(left, right, left_dim, right_dim):
    return lax.dot_general(
        left, right, (((left_dim,), (right_dim,)), ((), ())), preferred_element_type=F32
    )


class Place:
    def __init__(self, send_sems, recv_sems, local_sems):
        dp = lax.axis_index("dp")
        self.y = lax.axis_index("seq")
        self.c = lax.rem(dp, 2)
        self.x = lax.rem(lax.div(dp, 2), 2)
        self.z = lax.div(dp, 4)
        self.send_sems, self.recv_sems, self.local_sems = send_sems, recv_sems, local_sems
        self.n_local = 0
        self.xn = self.at(self.z, 1 - self.x, self.c, self.y)
        self.yn = self.at(self.z, self.x, self.c, 1 - self.y)
        self.cn = self.at(self.z, self.x, 1 - self.c, self.y)

    def at(self, z, x, c, y):
        return ((z * 2 + x) * 2 + c, y)

    def z_to(self, step):
        return lax.rem(self.z + step, 4)

    def zn(self, step):
        return self.at(self.z_to(step), self.x, self.c, self.y)

    def greet(self):
        for device in (self.cn, self.xn, self.yn, self.zn(1), self.zn(2), self.zn(3)):
            pl.semaphore_signal(
                pltpu.get_barrier_semaphore(), inc=1, device_id=device, device_id_type=MESH
            )

    def met(self):
        pl.semaphore_wait(pltpu.get_barrier_semaphore(), 6)

    def send(self, src, dst, recv, device, group):
        pltpu.make_async_remote_copy(
            src_ref=src,
            dst_ref=dst,
            send_sem=self.send_sems.at[group],
            recv_sem=self.recv_sems.at[recv],
            device_id=device,
            device_id_type=MESH,
        ).start()

    def wait(self, like, sem):
        pltpu.make_async_copy(like, like, sem).wait()

    def arrived(self, like, recv):
        self.wait(like, self.recv_sems.at[recv])

    def left(self, like, group):
        self.wait(like, self.send_sems.at[group])

    def move(self, src, dst):
        copy = pltpu.make_async_copy(src, dst, self.local_sems.at[self.n_local])
        self.n_local += 1
        copy.start()
        return copy


class Steps:
    def __init__(self, order):
        self.order, self.done = list(order), set()

    def next(self, count=1):
        for _ in range(count):
            if self.order and self.order[0][2]():
                step, i, _ready = self.order.pop(0)
                step(i)
                self.done.add((step, i))

    def until(self, step, i):
        while (step, i) not in self.done:
            self.next()

    def rest(self):
        while self.order:
            self.next()


def gelu_parts(u):
    square = u * u
    t = jnp.tanh(GELU_C * u * (1.0 + GELU_A * square))
    half = 0.5 * (1.0 + t)
    slope = half + (0.5 * GELU_C) * u * (1.0 - t * t) * (1.0 + (3.0 * GELU_A) * square)
    return u * half, slope


PIECES = 10
RECVS = 11
SENDS = 3
EXTRA = 5
SHIFT_F = (2,)
SHIFT_B = (7,)


def cut(rows, cols):
    if rows < 128:
        first, second = (pl.ds(0, rows), pl.ds(0, cols - 128)), (pl.ds(0, rows), pl.ds(cols - 128, 128))
        halves = (pl.ds(0, rows // 2), first[1]), (pl.ds(rows // 2, rows // 2), first[1])
    else:
        edge = rows - rows // 8
        first, second = (pl.ds(0, edge), pl.ds(0, cols)), (pl.ds(edge, rows // 8), pl.ds(0, cols))
        halves = (pl.ds(0, 64), first[1]), (pl.ds(64, edge - 64), first[1])
    return first, second, halves


def forward_kernel(
    prefix_ref, x_hbm, gy_hbm, wq_hbm, wk_hbm, wv_hbm, g1_ref, g2_ref, wo_hbm, w1_hbm_in, w2_hbm_in,
    out_hbm, w2_hbm, w1_hbm, wa_hbm, wot_hbm, gain_hbm, n1_hbm, q_hbm, kv_hbm, a_hbm, hidden_hbm,
    n2_hbm, slope_hbm, p_hbm, down_hbm,
    wa, wot, w1, w2, x, gy, n1, q, kv, a, hidden, n2, z, slope, p, bias, gain, down_out, down_in, out,
    wq_in, wk_in, wv_in, wo_in, w1_in, w2_in,
    send_sems, recv_sems, local_sems,
):
    me = Place(send_sems, recv_sems, local_sems)
    rows, width = x.shape
    me.greet()
    load_qkv = [me.move(src, dst) for src, dst in ((wq_hbm, wq_in), (wk_hbm, wk_in), (wv_hbm, wv_in))]
    load_x = me.move(x_hbm, x)
    load_wo = me.move(wo_hbm, wo_in)
    load_w1 = me.move(w1_hbm_in, w1_in)
    load_w2 = me.move(w2_hbm_in, w2_in)
    load_gy = me.move(gy_hbm, gy)
    views = [wa, wot] + [w1.at[j] for j in range(4)] + [w2.at[k] for k in range(4)]
    saves = []

    every = slice(None)
    own = (me.z, me.x, me.c, me.y)

    def pass_on(i, at, recv, device, group):
        view = views[i].at[at]
        me.send(view, view, i * RECVS + recv, device, i * SENDS + group)

    def came(i, at, recv):
        me.arrived(views[i].at[at], i * RECVS + recv)

    def s0(i):
        first, second, _ = cut(*views[i].shape[4:])
        for step in (1, 3, 2):
            pass_on(i, own + first, step - 1, me.zn(step), 0)
        pass_on(i, own + first, 3, me.xn, 1)
        pass_on(i, own + first, 4, me.yn, 1)
        pass_on(i, own + second, 5, me.xn, 0)
        pass_on(i, own + second, 6, me.yn, 0)

    def s1(i):
        first, second, _ = cut(*views[i].shape[4:])
        for step in (1, 3, 2):
            at = (me.z_to(4 - step), me.x, me.c, me.y) + first
            came(i, at, step - 1)
            pass_on(i, at, 3, me.xn, 1)
            pass_on(i, at, 4, me.yn, 1)
        from_x, from_y = (me.z, 1 - me.x, me.c, me.y) + second, (me.z, me.x, me.c, 1 - me.y) + second
        came(i, from_x, 5)
        came(i, from_y, 6)
        if i % 2:
            pass_on(i, from_y, 7, me.xn, 0)
        else:
            pass_on(i, from_x, 7, me.yn, 0)

    def s2(i):
        first, second, (low, high) = cut(*views[i].shape[4:])
        came(i, (every, 1 - me.x, me.c, me.y) + first, 3)
        if i not in SHIFT_F:
            pass_on(i, (every, 1 - me.x, me.c, me.y) + low, 9, me.yn, 1)
        came(i, (every, me.x, me.c, 1 - me.y) + first, 4)
        pass_on(i, (every, me.x, me.c, 1 - me.y) + (first if i in SHIFT_F else high), 9, me.xn, 1)
        came(i, (me.z, 1 - me.x, me.c, 1 - me.y) + second, 7)
        for step in (1, 3, 2):
            pass_on(i, (me.z, every, me.c, every) + second, 8, me.zn(step), 1)

    def s3(i):
        first, second, _ = cut(*views[i].shape[4:])
        came(i, (every, 1 - me.x, me.c, 1 - me.y) + first, 9)
        came(i, (pl.ds(0, 3), every, me.c, every) + second, 8)
        pass_on(i, (every, every, me.c), 10, me.cn, 2)

    def s4(i):
        came(i, (every, every, 1 - me.c), 10)
        if i == 0:
            saves.append(me.move(wa, wa_hbm))
        elif i == 1:
            saves.append(me.move(wot, wot_hbm))
        elif i < 6:
            saves.append(me.move(w1.at[i - 2], w1_hbm.at[i - 2]))
        else:
            k = i - 6
            saves.append(me.move(w2.at[k], w2_hbm.at[:, :, :, :, :, pl.ds(256 * k, 256)]))

    def order():
        yield s0, 0
        for k in range(-1, PIECES + 3):
            for step, i in ((s1, k + 1), (s0, k + 2), (s2, k), (s3, k - 1), (s4, k - 2)):
                if 0 <= i < PIECES:
                    yield step, i

    steps = Steps((step, i, lambda: True) for step, i in order())

    for kind, ref in ((0, g1_ref), (1, g2_ref)):
        tile = jnp.concatenate([ref[...], jnp.zeros((1, 96), F32)], axis=1)
        for quarter in range(4):
            @pl.when(me.c * 2 + me.y == quarter)
            def _():
                placed = tile if quarter == 0 else pltpu.roll(tile, 32 * quarter, 1)
                wa[(*own, pl.ds(16 * kind, 16), pl.ds(1280, 128))] = jnp.broadcast_to(placed, (16, 128)).astype(BF)
    for load in load_qkv:
        load.wait()
    wa[(*own, every, pl.ds(0, 1024))] = wq_in[...].astype(BF)
    wa[(*own, every, pl.ds(1024, 128))] = wk_in[...].astype(BF)
    wa[(*own, every, pl.ds(1152, 128))] = wv_in[...].astype(BF)
    me.met()
    steps.next()
    load_wo.wait()
    wot[own] = wo_in[...].astype(BF)
    load_w1.wait()
    for j in range(4):
        w1[(j, *own)] = w1_in[:, pl.ds(1024 * j, 1024)].astype(BF)
    load_w2.wait()
    for k in range(4):
        w2[(k, *own)] = w2_in[:, pl.ds(256 * k, 256)].astype(BF)
    steps.next(2)

    first_pos = me.y * rows

    @pl.loop(0, rows // 64)
    def _(t):
        at = pl.multiple_of(t * 64, 64)
        query_pos = first_pos + at + lax.broadcasted_iota(jnp.int32, (64, 2 * rows), 0)
        key_pos = lax.broadcasted_iota(jnp.int32, (64, 2 * rows), 1)
        visible = (key_pos <= query_pos) | (key_pos < prefix_ref[0])
        bias[pl.ds(at, 64), :] = jnp.where(visible, 0.0, -1e30)

    load_x.wait()
    load_gy.wait()
    steps.until(s4, 0)

    for kind in (0, 1):
        for zi in range(4):
            for xi in range(2):
                tile = jnp.zeros((16, 128), F32)
                for ci in range(2):
                    for yi in range(2):
                        tile += wa[zi, xi, ci, yi, pl.ds(16 * kind, 16), pl.ds(1280, 128)].astype(F32)
                gain[kind, :, pl.ds(128 * (2 * zi + xi), 128)] = tile[:8]
    saves.append(me.move(gain, gain_hbm))

    @pl.loop(0, rows // 64)
    def _(t):
        r = pl.ds(pl.multiple_of(t * 64, 64), 64)
        values = x[r, :].astype(F32)
        factor = lax.rsqrt(jnp.mean(values * values, axis=-1, keepdims=True) + epsilon)
        n1[r, :] = (values * factor * gain[0, 0:1, :]).astype(BF)

    kv[me.y] = dot(
        n1[...], wa[:, :, :, :, :, pl.ds(1024, 256)].reshape(width, 256), 1, 0
    ).astype(BF)
    me.send(kv.at[me.y], kv.at[me.y], PIECES * RECVS, me.yn, PIECES * SENDS)
    for i in range(2):
        steps.next()
        cols = pl.ds(512 * i, 512)
        q[:, cols] = dot(n1[...], wa[:, :, :, :, :, cols].reshape(width, 512), 1, 0).astype(BF)

    saves.append(me.move(n1, n1_hbm))
    saves.append(me.move(q, q_hbm))
    steps.next()
    me.arrived(kv.at[1 - me.y], PIECES * RECVS)
    saves.append(me.move(kv, kv_hbm))
    length = 2 * rows
    to_log2 = (DH ** -0.5) * 1.4426950408889634

    def head(h):
        cols = pl.ds(h * DH, DH)
        keys = kv[:, :, pl.ds(0, DH)].reshape(length, DH)
        vals = kv[:, :, pl.ds(DH, DH)].reshape(length, DH)
        for t in range(rows // 256):
            r = pl.ds(256 * t, 256)
            s = dot(q[r, cols], keys, 1, 1) * to_log2 + bias[r, :]
            e = jnp.exp2(s - jnp.max(s, axis=-1, keepdims=True))
            chances = (e * (1.0 / jnp.sum(e, axis=-1, keepdims=True))).astype(BF)
            p[(h // 2) % 2, pl.ds((h % 2) * rows + 256 * t, 256), :] = chances
            a[r, cols] = dot(chances, vals, 1, 0).astype(BF)

    p_saves = []
    for h in range(H):
        if h >= 4 and h % 2 == 0:
            p_saves[h // 2 - 2].wait()
        head(h)
        if h % 2:
            p_saves.append(me.move(p.at[(h // 2) % 2], p_hbm.at[h // 2]))
        steps.next()
    saves.extend(p_saves[2:])
    saves.append(me.move(a, a_hbm))
    steps.until(s4, 1)
    for i in range(2):
        cols = pl.ds(512 * i, 512)
        weight = wot[pl.ds(2 * i, 2)].reshape(512, width)
        hidden[:, cols] = x[:, cols].astype(F32) + dot(a[...], weight, 1, 1)
        steps.next()

    @pl.loop(0, rows // 64)
    def _(t):
        r = pl.ds(pl.multiple_of(t * 64, 64), 64)
        values = hidden[r, :]
        factor = lax.rsqrt(jnp.mean(values * values, axis=-1, keepdims=True) + epsilon)
        n2[r, :] = (values * factor * gain[1, 0:1, :]).astype(BF)

    saves.append(me.move(hidden, hidden_hbm))
    saves.append(me.move(n2, n2_hbm))
    steps.next()

    def down_grad_out(j):
        for t in (2 * j, 2 * j + 1):
            cols = pl.ds(pl.multiple_of((2 * t + 1 - me.c) * 256, 256), 256)
            down_out[t] = dot(z[:, cols], gy[...], 0, 0).astype(BF)
        at = pl.ds(2 * j, 2)
        me.send(down_out.at[at], down_in.at[at], PIECES * RECVS + 1 + j, me.cn, PIECES * SENDS + 1 + j)

    def down_grad_own(j):
        me.arrived(down_in.at[pl.ds(2 * j, 2)], PIECES * RECVS + 1 + j)
        for t in (2 * j, 2 * j + 1):
            cols = pl.ds(pl.multiple_of((2 * t + me.c) * 256, 256), 256)
            down_in[t] = (dot(z[:, cols], gy[...], 0, 0) + down_in[t].astype(F32)).astype(BF)

    def down(k):
        cols = pl.ds(256 * k, 256)
        for t in range(2):
            r = pl.ds(256 * t, 256)
            y = dot(z[r, :], w2[k].reshape(4096, 256), 1, 0)
            out[r, cols] = (hidden[r, cols] + y).astype(BF)

    for j in range(4):
        steps.until(s4, 2 + j)
        for i in range(2):
            cols, to = pl.ds(512 * i, 512), pl.ds(1024 * j + 512 * i, 512)
            u = dot(n2[...], w1[j, :, :, :, :, :, cols].reshape(width, 512), 1, 0)
            active, steep = gelu_parts(u)
            z[:, to] = active.astype(BF)
            slope[:, to] = steep.astype(BF)
            steps.next()
        down_grad_out(j)
        steps.next()
        if j:
            down_grad_own(j - 1)
            steps.next()
    saves.append(me.move(slope, slope_hbm))
    steps.until(s4, 6)
    down_grad_own(3)
    saves.append(me.move(down_in, down_hbm))
    steps.next()
    down(0)
    for k in (1, 2, 3):
        steps.until(s4, 6 + k)
        down(k)
    steps.rest()
    saves.append(me.move(out, out_hbm))
    for copy in saves:
        copy.wait()
    for i in range(PIECES):
        me.left(views[i].at[pl.ds(0, 3), me.x, me.c, me.y], i * SENDS)
        me.left(views[i].at[pl.ds(0, 3), :, me.c], i * SENDS + 1)
        me.left(views[i].at[:, :, me.c], i * SENDS + 2)
    me.left(kv.at[me.y], PIECES * SENDS)
    for j in range(4):
        me.left(down_out.at[pl.ds(2 * j, 2)], PIECES * SENDS + 1 + j)


def backward_kernel(
    x_hbm, gy_hbm, gain_hbm, w2_hbm, w1_hbm, wa_hbm, wot_hbm, n1_hbm, q_hbm, kv_hbm, a_hbm, hidden_hbm,
    n2_hbm, slope_hbm, p_hbm, down_hbm,
    grad_x_hbm, g2_ref, g1_ref, go_ref, ga_ref,
    gy, n2, hidden, gn, a, q, kv, gain, wbuf, gu, wkv, att, sums, kvsum, kvout, kvin,
    down, pup, pproj, patt, pair_up, pair_att, diag2, diag1, diaga, side2, side1, sidea, line2, line1, linea,
    plane2, plane1, planea,
    send_sems, recv_sems, local_sems,
):
    me = Place(send_sems, recv_sems, local_sems)
    rows, width = gy.shape
    length = 2 * rows
    me.greet()
    load_down = [
        me.move(down_hbm.at[:, :, :, :, pl.ds(256 * k, 256)], down.at[:, :, :, :, pl.ds(256 * k, 256)])
        for k in range(4)
    ]
    load_gy = me.move(gy_hbm, gy)
    load_w2 = [me.move(w2_hbm.at[j], wbuf.at[j]) for j in range(2)]
    load_slope = [me.move(slope_hbm.at[:, pl.ds(1024 * j, 1024)], gu.at[j]) for j in range(2)]
    load_n2 = me.move(n2_hbm, n2)
    load_w1 = [me.move(w1_hbm.at[j], wbuf.at[2 + j]) for j in range(2)]
    load_rest = [
        me.move(src, dst)
        for src, dst in (
            (hidden_hbm, hidden), (gain_hbm, gain), (a_hbm, a), (q_hbm, q), (kv_hbm, kv),
            (wa_hbm.at[:, pl.ds(1024, 256)], wkv),
        )
    ]

    def source(i):
        return pup.at[i - 4] if i < 8 else pproj if i == 8 else patt

    def pair(i):
        return pair_up.at[i - 4] if i < 9 else pair_att

    def part(i, zi, xi, yi, at):
        if i < 4:
            return down.at[zi, xi, yi, at[0], pl.ds(256 * i + at[1].start, at[1].size)]
        return source(i).at[(zi, xi, me.c, yi) + at]

    def group(i, two, one, last):
        return two.at[i] if i < 4 else one.at[i - 4] if i < 9 else last

    def cut_of(i):
        return cut(*((128, 256) if i < 4 else (32, 1024) if i < 9 else (32, 1408)))

    every = slice(None)
    given = set(range(4))

    def send(src, dst, i, recv, device, to):
        me.send(src, dst, i * RECVS + recv, device, i * SENDS + to)

    def came(like, i, recv):
        me.arrived(like, i * RECVS + recv)

    def t0(i):
        send(source(i).at[:, :, 1 - me.c], pair(i), i, 0, me.cn, 2)
        given.add(i)

    def t1(i):
        first, second, (low, high) = cut_of(i)
        diag, plane = group(i, diag2, diag1, diaga), group(i, plane2, plane1, planea)
        if i < 4:
            load_down[i].wait()
        else:
            total, term = source(i), pair(i)
            came(term, i, 0)

            @pl.loop(0, 4)
            def _(zi):
                for xi in range(2):
                    total[zi, xi, me.c] = total[zi, xi, me.c] + term[zi, xi]

        if i not in SHIFT_B:
            send(part(i, every, 1 - me.x, 1 - me.y, low), diag.at[(every,) + low], i, 1, me.yn, 1)
        else:
            high = first
        send(part(i, every, 1 - me.x, 1 - me.y, high), diag.at[(every,) + high], i, 1, me.xn, 1)
        for step in (1, 3, 2):
            send(part(i, me.z_to(step), every, every, second), plane.at[step - 1], i, 2, me.zn(step), 1)

    def t2(i):
        first, second, (low, high) = cut_of(i)
        diag, plane = group(i, diag2, diag1, diaga), group(i, plane2, plane1, planea)
        side = group(i, side2, side1, sidea)
        came(diag.at[(every,) + first], i, 1)
        for step in (1, 3, 2, 0):
            zi = me.z_to(step)
            by_y, by_x = (1 - me.x, me.y, low), (me.x, 1 - me.y, first if i in SHIFT_B else high)
            for xi, yi, half in ((by_x,) if i in SHIFT_B else (by_y, by_x)):
                mine = part(i, zi, xi, yi, half)
                mine[...] = mine[...] + diag[(zi,) + half]
            recv = 2 + step if step else 6
            send(part(i, zi, 1 - me.x, me.y, first), side.at[(0, zi) + first], i, recv, me.xn, 1)
            send(part(i, zi, me.x, 1 - me.y, first), side.at[(1, zi) + first], i, recv, me.yn, 1)
        came(plane, i, 2)
        for xi in range(2):
            for yi in range(2):
                mine = part(i, me.z, xi, yi, second)
                total = mine[...].astype(F32)
                for step in range(3):
                    total += plane[step, xi, yi].astype(F32)
                mine[...] = total.astype(BF)
        send(
            part(i, me.z, 1 - me.x, 1 - me.y, second), diag.at[(me.z,) + second], i, 7,
            me.xn if i % 2 else me.yn, 0,
        )

    def t3(i):
        first, second, _ = cut_of(i)
        diag, side = group(i, diag2, diag1, diaga), group(i, side2, side1, sidea)
        line = group(i, line2, line1, linea)
        for step in (1, 3, 2):
            zi = me.z_to(step)
            came(side.at[(every, zi) + first], i, 2 + step)
            mine = part(i, zi, me.x, me.y, first)
            total = mine[...].astype(F32) + side[(0, zi) + first].astype(F32) + side[(1, zi) + first].astype(F32)
            mine[...] = total.astype(BF)
            send(mine, line.at[(step - 1,) + first], i, 8, me.zn(step), 0)
        came(diag.at[(me.z,) + second], i, 7)
        mine = part(i, me.z, *((me.x, 1 - me.y) if i % 2 else (1 - me.x, me.y)), second)
        mine[...] = mine[...] + diag[(me.z,) + second]
        send(part(i, me.z, 1 - me.x, me.y, second), side.at[(0, me.z) + second], i, 9, me.xn, 0)
        send(part(i, me.z, me.x, 1 - me.y, second), side.at[(1, me.z) + second], i, 9, me.yn, 0)

    def t4(i):
        first, second, _ = cut_of(i)
        side, line = group(i, side2, side1, sidea), group(i, line2, line1, linea)
        came(side.at[(every, me.z) + first], i, 6)
        came(line.at[(every,) + first], i, 8)
        came(side.at[(every, me.z) + second], i, 9)
        out, shift = (
            (g2_ref, 256 * i) if i < 4 else (g1_ref, 1024 * (i - 4)) if i < 8 else (go_ref, 0) if i == 8 else (ga_ref, 0)
        )
        for at in (first, second):
            total = part(i, me.z, me.x, me.y, at)[...].astype(F32)
            total += side[(0, me.z) + at].astype(F32) + side[(1, me.z) + at].astype(F32)
            if at is first:
                for step in range(3):
                    total += line[(step,) + first].astype(F32)
            out[at[0], pl.ds(shift + at[1].start, at[1].size)] = total

    def order():
        yield t1, 0
        for k in range(PIECES + 2):
            for step, i in ((t1, k + 1), (t2, k), (t3, k - 1), (t4, k - 2)):
                if 0 <= i < PIECES:
                    yield step, i

    steps = Steps((step, i, lambda step=step, i=i: step is not t1 or i in given) for step, i in order())
    me.met()
    steps.next()

    def feed_forward(j):
        slot = j % 2
        load_w2[j].wait()
        load_slope[j].wait()
        for i in range(2):
            cols = pl.ds(512 * i, 512)
            grad_active = dot(gy[...], wbuf[slot, cols, :], 1, 1)
            gu[slot, :, cols] = (grad_active * gu[slot, :, cols].astype(F32)).astype(BF)
        steps.next()
        if j < 2:
            load_w2.append(me.move(w2_hbm.at[j + 2], wbuf.at[slot]))
        elif j == 2:
            load_w2.append(me.move(wot_hbm, wbuf.at[0]))
        else:
            load_w2.append(me.move(p_hbm.at[1], wbuf.at[1]))
        for i in range(2):
            term = dot(n2[:, pl.ds(512 * i, 512)], gu[slot], 0, 0)
            pup[j, pl.ds(2 * i, 2)] = term.reshape(2, 2, 2, 2, 32, 1024).astype(BF)
        t0(4 + j)
        steps.next()
        load_w1[j].wait()
        for i in range(2):
            cols = pl.ds(512 * i, 512)
            term = dot(gu[slot], wbuf[2 + slot, cols, :], 1, 1)
            if j == 0:
                gn[:, cols] = term
            else:
                gn[:, cols] = gn[:, cols] + term
        if j < 2:
            load_slope.append(me.move(slope_hbm.at[:, pl.ds(1024 * (j + 2), 1024)], gu.at[slot]))
            load_w1.append(me.move(w1_hbm.at[j + 2], wbuf.at[2 + slot]))
        else:
            load_w1.append(me.move(p_hbm.at[(0, 2)[j - 2]], wbuf.at[2 + slot]))
        steps.next()

    load_gy.wait()
    load_n2.wait()
    for j in range(4):
        feed_forward(j)
    load_x = me.move(x_hbm, n2)
    for copy in load_rest:
        copy.wait()

    sums[...] = jnp.zeros_like(sums)

    @pl.loop(0, rows // 64)
    def _(t):
        r = pl.ds(pl.multiple_of(t * 64, 64), 64)
        grad, values = gn[r, :], hidden[r, :]
        factor = lax.rsqrt(jnp.mean(values * values, axis=-1, keepdims=True) + epsilon)
        scaled = grad * gain[1, 0:1, :]
        middle = jnp.mean(scaled * values, axis=-1, keepdims=True)
        total = gy[r, :].astype(F32) + factor * scaled - values * (factor * factor * factor * middle)
        sums[1] += jnp.sum((grad * values * factor).reshape(8, 8, width), axis=0)
        gn[r, :] = total
        gy[r, :] = total.astype(BF)

    for i in range(2):
        term = dot(gy[:, pl.ds(512 * i, 512)], a[...], 0, 0)
        pproj[pl.ds(2 * i, 2)] = term.reshape(2, 2, 2, 2, 32, width).astype(BF)
    t0(8)
    steps.next()
    load_w2[4].wait()
    for i in range(2):
        cols = pl.ds(512 * i, 512)
        att[:, cols] = dot(gy[...], wbuf[0, :, cols], 1, 0).astype(BF)
    load_p3 = me.move(p_hbm.at[3], wbuf.at[0])
    load_n1 = me.move(n1_hbm, gy)
    steps.next()
    kvsum[...] = jnp.zeros_like(kvsum)
    scale = DH ** -0.5

    def head(h):
        slot = (2, 1, 3, 0)[h // 2]
        cols = pl.ds(h * DH, DH)
        keys = kv[:, :, pl.ds(0, DH)].reshape(length, DH)
        vals = kv[:, :, pl.ds(DH, DH)].reshape(length, DH)
        for t in range(rows // 256):
            r = pl.ds(256 * t, 256)
            grad = att[r, cols]
            chances = wbuf[slot, pl.ds((h % 2) * rows + 256 * t, 256), :]
            grad_chances = dot(grad, vals, 1, 1)
            wide = chances.astype(F32)
            center = jnp.sum(wide * grad_chances, axis=-1, keepdims=True)
            grad_scores = (wide * (grad_chances - center)).astype(BF)
            kvsum[0] += dot(q[r, cols], grad_scores, 0, 0)
            kvsum[1] += dot(grad, chances, 0, 0)
            att[r, cols] = (dot(grad_scores, keys, 1, 0) * scale).astype(BF)

    load_p = (load_w1[4], load_w2[5], load_w1[5], load_p3)
    for h in range(H):
        if h % 2 == 0:
            load_p[h // 2].wait()
        head(h)
        if h == 1:
            load_wq = me.move(wa_hbm.at[:, pl.ds(0, 1024)], wbuf.at[2])
        steps.next()
    for half in (0, 1):
        cols = pl.ds(half * rows, rows)
        kvout[half, :, pl.ds(0, DH)] = (kvsum[0, :, cols] * scale).T.astype(BF)
        kvout[half, :, pl.ds(DH, DH)] = kvsum[1, :, cols].T.astype(BF)
    me.send(kvout.at[1 - me.y], kvin, PIECES * RECVS, me.yn, PIECES * SENDS)
    load_n1.wait()
    for i in range(2):
        term = dot(gy[:, pl.ds(512 * i, 512)], att[...], 0, 0)
        patt[pl.ds(2 * i, 2), :, :, :, :, pl.ds(0, 1024)] = term.reshape(2, 2, 2, 2, 32, width).astype(BF)
    steps.next()
    me.arrived(kvin, PIECES * RECVS)
    kvin[...] = kvin[...] + kvout[me.y]
    for i in range(2):
        term = dot(gy[:, pl.ds(512 * i, 512)], kvin[...], 0, 0)
        patt[pl.ds(2 * i, 2), :, :, :, :, pl.ds(1024, 256)] = term.reshape(2, 2, 2, 2, 32, 256).astype(BF)
    load_wq.wait()
    for i in range(2):
        cols = pl.ds(512 * i, 512)
        hidden[:, cols] = dot(att[...], wbuf[2, cols, :], 1, 1) + dot(kvin[...], wkv[cols, :], 1, 1)
        steps.next()
    load_x.wait()

    @pl.loop(0, rows // 64)
    def _(t):
        r = pl.ds(pl.multiple_of(t * 64, 64), 64)
        grad, values = hidden[r, :], n2[r, :].astype(F32)
        factor = lax.rsqrt(jnp.mean(values * values, axis=-1, keepdims=True) + epsilon)
        scaled = grad * gain[0, 0:1, :]
        middle = jnp.mean(scaled * values, axis=-1, keepdims=True)
        sums[0] += jnp.sum((grad * values * factor).reshape(8, 8, width), axis=0)
        gn[r, :] = gn[r, :] + factor * scaled - values * (factor * factor * factor * middle)

    save_x = me.move(gn, grad_x_hbm)
    for kind in (0, 1):
        row = jnp.sum(sums[kind], axis=0, keepdims=True)
        for zi in range(4):
            for xi in range(2):
                lanes = slice(128 * (2 * zi + xi), 128 * (2 * zi + xi) + 128)
                tile = jnp.broadcast_to(row[:, lanes], (16, 128)).astype(BF)
                for ci in range(2):
                    for yi in range(2):
                        patt[zi, xi, ci, yi, pl.ds(16 * kind, 16), pl.ds(1280, 128)] = tile
    t0(9)
    steps.rest()
    save_x.wait()
    for i in range(PIECES):
        if i < 4:
            at = (every, pl.ds(256 * i, 256))
            me.left(down.at[(pl.ds(0, 3), 0, 0) + at], i * SENDS)
            me.left(down.at[(pl.ds(0, 3), every, every) + at], i * SENDS + 1)
        else:
            me.left(source(i).at[pl.ds(0, 3), 0, 0, 0], i * SENDS)
            me.left(source(i).at[pl.ds(0, 3), :, 0], i * SENDS + 1)
            me.left(source(i).at[:, :, 0], i * SENDS + 2)
    me.left(kvin, PIECES * SENDS)


def on_grid(
    tokens, cotangent, prefix, attention_gain, query_weight, key_weight, value_weight, projection_weight,
    feedforward_gain, up_weight, down_weight,
):
    rows, width = tokens.shape[1:]
    vmem, hbm = pl.BlockSpec(memory_space=pltpu.VMEM), pl.BlockSpec(memory_space=pl.ANY)
    smem = pl.BlockSpec(memory_space=pltpu.SMEM)
    x, gy = tokens.reshape(rows, width), cotangent.reshape(rows, width)
    sds = jax.ShapeDtypeStruct
    grid = (4, 2, 2, 2)
    send_sems, recv_sems = (pltpu.SemaphoreType.DMA((PIECES * n + EXTRA,)) for n in (SENDS, RECVS))
    length = 2 * rows
    out = pl.pallas_call(
        forward_kernel,
        out_shape=(
            sds((rows, width), BF),
            sds((*grid, 128, 1024), BF),
            sds((4, *grid, 32, 1024), BF),
            sds((*grid, 32, 1408), BF),
            sds((*grid, 32, 1024), BF),
            sds((2, 8, width), F32),
            sds((rows, width), BF),
            sds((rows, width), BF),
            sds((2, rows, 256), BF),
            sds((rows, width), BF),
            sds((rows, width), F32),
            sds((rows, width), BF),
            sds((rows, 4096), BF),
            sds((4, 2 * rows, length), BF),
            sds((8, 256, width), BF),
        ),
        in_specs=[smem] + [hbm] * 5 + [vmem] * 2 + [hbm] * 3,
        out_specs=[hbm] * 15,
        scratch_shapes=[
            pltpu.VMEM((*grid, 32, 1408), BF),
            pltpu.VMEM((*grid, 32, 1024), BF),
            pltpu.VMEM((4, *grid, 32, 1024), BF),
            pltpu.VMEM((4, *grid, 128, 256), BF),
            pltpu.VMEM((rows, width), BF),
            pltpu.VMEM((rows, width), BF),
            pltpu.VMEM((rows, width), BF),
            pltpu.VMEM((rows, width), BF),
            pltpu.VMEM((2, rows, 256), BF),
            pltpu.VMEM((rows, width), BF),
            pltpu.VMEM((rows, width), F32),
            pltpu.VMEM((rows, width), BF),
            pltpu.VMEM((rows, 4096), BF),
            pltpu.VMEM((rows, 4096), BF),
            pltpu.VMEM((2, 2 * rows, length), BF),
            pltpu.VMEM((rows, length), F32),
            pltpu.VMEM((2, 8, width), F32),
            pltpu.VMEM((8, 256, width), BF),
            pltpu.VMEM((8, 256, width), BF),
            pltpu.VMEM((rows, width), BF),
            pltpu.VMEM(query_weight.shape, F32),
            pltpu.VMEM(key_weight.shape, F32),
            pltpu.VMEM(value_weight.shape, F32),
            pltpu.VMEM((32, width), F32),
            pltpu.VMEM(up_weight.shape, F32),
            pltpu.VMEM(down_weight.shape, F32),
            send_sems,
            recv_sems,
            pltpu.SemaphoreType.DMA((40,)),
        ],
        compiler_params=pltpu.CompilerParams(
            collective_id=0, has_side_effects=True, vmem_limit_bytes=VMEM_LIMIT
        ),
    )(
        prefix, x, gy, query_weight, key_weight, value_weight, attention_gain.reshape(1, 32),
        feedforward_gain.reshape(1, 32), projection_weight.T, up_weight, down_weight,
    )
    layer_output, w2, w1, wa, wot, gain, n1, q, kv, a, hidden, n2, slope, p, down = out
    grad_x, g2, g1, go, ga = pl.pallas_call(
        backward_kernel,
        out_shape=(
            sds((rows, width), F32),
            sds((128, 1024), F32),
            sds((32, 4096), F32),
            sds((32, 1024), F32),
            sds((32, 1408), F32),
        ),
        in_specs=[hbm] * 16,
        out_specs=[hbm] + [vmem] * 4,
        scratch_shapes=[
            pltpu.VMEM((rows, width), BF),
            pltpu.VMEM((rows, width), BF),
            pltpu.VMEM((rows, width), F32),
            pltpu.VMEM((rows, width), F32),
            pltpu.VMEM((rows, width), BF),
            pltpu.VMEM((rows, width), BF),
            pltpu.VMEM((2, rows, 256), BF),
            pltpu.VMEM((2, 8, width), F32),
            pltpu.VMEM((4, 1024, 1024), BF),
            pltpu.VMEM((2, rows, 1024), BF),
            pltpu.VMEM((width, 256), BF),
            pltpu.VMEM((rows, width), BF),
            pltpu.VMEM((2, 8, width), F32),
            pltpu.VMEM((2, DH, length), F32),
            pltpu.VMEM((2, rows, 256), BF),
            pltpu.VMEM((rows, 256), BF),
            pltpu.VMEM((4, 2, 2, 128, 1024), BF),
            pltpu.VMEM((4, *grid, 32, 1024), BF),
            pltpu.VMEM((*grid, 32, 1024), BF),
            pltpu.VMEM((*grid, 32, 1408), BF),
            pltpu.VMEM((5, 4, 2, 2, 32, 1024), BF),
            pltpu.VMEM((4, 2, 2, 32, 1408), BF),
            pltpu.VMEM((4, 4, 128, 256), BF), pltpu.VMEM((5, 4, 32, 1024), BF), pltpu.VMEM((4, 32, 1408), BF),
            pltpu.VMEM((4, 2, 4, 128, 256), BF), pltpu.VMEM((5, 2, 4, 32, 1024), BF), pltpu.VMEM((2, 4, 32, 1408), BF),
            pltpu.VMEM((4, 3, 128, 256), BF), pltpu.VMEM((5, 3, 32, 1024), BF), pltpu.VMEM((3, 32, 1408), BF),
            pltpu.VMEM((4, 3, 2, 2, 16, 256), BF), pltpu.VMEM((5, 3, 2, 2, 32, 128), BF), pltpu.VMEM((3, 2, 2, 32, 128), BF),
            send_sems,
            recv_sems,
            pltpu.SemaphoreType.DMA((40,)),
        ],
        compiler_params=pltpu.CompilerParams(
            collective_id=1, has_side_effects=True, vmem_limit_bytes=VMEM_LIMIT
        ),
    )(
        x, gy, gain, w2.reshape(4, 1024, 1024), w1.reshape(4, 1024, 1024), wa.reshape(1024, 1408), wot.reshape(1024, 1024),
        n1, q, kv, a, hidden, n2, slope, p, down.reshape(4, 2, 2, 128, 1024),
    )
    layer_output, grad_x, g1_gain, gq, gk, gv, gp, g2_gain, g1, g2 = pl.pallas_call(
        hand_out,
        out_shape=(
            sds((rows, width), BF),
            sds((rows, width), F32),
            sds((1, 32), F32),
            sds((32, 1024), F32),
            sds((32, 128), F32),
            sds((32, 128), F32),
            sds((32, 1024), F32),
            sds((1, 32), F32),
            sds((32, 4096), F32),
            sds((128, 1024), F32),
        ),
        in_specs=[hbm] * 6,
        out_specs=[hbm, hbm, vmem, hbm, hbm, hbm, hbm, vmem, hbm, hbm],
        scratch_shapes=[
            pltpu.VMEM((rows, width), BF),
            pltpu.VMEM((rows, width), F32),
            pltpu.VMEM((32, 1408), F32),
            pltpu.VMEM((32, 1024), F32),
            pltpu.VMEM((32, 4096), F32),
            pltpu.VMEM((128, 1024), F32),
            pltpu.SemaphoreType.DMA((16,)),
        ],
        compiler_params=pltpu.CompilerParams(vmem_limit_bytes=VMEM_LIMIT),
    )(layer_output, grad_x, ga, go, g1, g2)
    return (
        layer_output.reshape(tokens.shape),
        grad_x.reshape(tokens.shape),
        g1_gain.reshape(32),
        gq,
        gk,
        gv,
        gp.T,
        g2_gain.reshape(32),
        g1,
        g2,
    )


def hand_out(
    y_in, x_in, a_in, p_in, up_in, down_in,
    y_out, x_out, g1_out, q_out, k_out, v_out, p_out, g2_out, up_out, down_out,
    y, x, a, p, up, down, sems,
):
    started = 0

    def move(src, dst):
        nonlocal started
        copy = pltpu.make_async_copy(src, dst, sems.at[started])
        started += 1
        copy.start()
        return copy

    loads = [move(src, dst) for src, dst in ((a_in, a), (p_in, p), (x_in, x), (y_in, y), (up_in, up), (down_in, down))]
    stores = []
    loads[0].wait()
    for cols, out in ((pl.ds(0, 1024), q_out), (pl.ds(1024, 128), k_out), (pl.ds(1152, 128), v_out)):
        stores.append(move(a.at[:, cols], out))
    for load, src, dst in zip(loads[1:], (p, x, y, up, down), (p_out, x_out, y_out, up_out, down_out)):
        load.wait()
        stores.append(move(src, dst))
    quarter = lax.rem(lax.axis_index("dp"), 2) * 2 + lax.axis_index("seq")
    for row, out in ((0, g1_out), (16, g2_out)):
        for k in range(4):
            @pl.when(quarter == k)
            def _():
                out[...] = a[row : row + 1, 1280 + 32 * k : 1312 + 32 * k]
    for copy in stores:
        copy.wait()


def root_norm(values, gain):
    factor = lax.rsqrt(jnp.mean(values * values, axis=-1, keepdims=True) + epsilon)
    return values * factor * gain


def smooth_gate(values):
    return jax.nn.gelu(values, approximate=True)


def product(left, right):
    return jnp.dot(left, right, preferred_element_type=jnp.float32)


def inner_rows(left, right):
    return lax.dot_general(
        left, right, (((0,), (0,)), ((), ())), preferred_element_type=jnp.float32
    )


def outer_rows(left, right):
    return lax.dot_general(
        left, right, (((1,), (1,)), ((), ())), preferred_element_type=jnp.float32
    )


def local(
    tokens,
    cotangent,
    prefix,
    attention_gain,
    query_weight,
    key_weight,
    value_weight,
    projection_weight,
    feedforward_gain,
    up_weight,
    down_weight,
):
    seqs_here, span_len, model_width = tokens.shape
    length = span_len * lax.axis_size("seq")
    row_count = seqs_here * span_len
    block_len = min(64, span_len)
    block_count = span_len // block_len
    score_scale = DH ** (-0.5)
    gain_low = attention_gain.astype(jnp.bfloat16)
    query_low = query_weight.astype(jnp.bfloat16)
    key_low = key_weight.astype(jnp.bfloat16)
    value_low = value_weight.astype(jnp.bfloat16)
    projection_low = projection_weight.astype(jnp.bfloat16)
    second_low = feedforward_gain.astype(jnp.bfloat16)
    up_low = up_weight.astype(jnp.bfloat16)
    down_low = down_weight.astype(jnp.bfloat16)
    gathered = (
        lax.all_gather(gain_low, ("dp", "seq"), axis=0, tiled=True),
        lax.all_gather(query_low, ("dp", "seq"), axis=0, tiled=True),
        lax.all_gather(key_low, ("dp", "seq"), axis=0, tiled=True),
        lax.all_gather(value_low, ("dp", "seq"), axis=0, tiled=True),
        lax.all_gather(projection_low, ("dp", "seq"), axis=1, tiled=True),
        lax.all_gather(second_low, ("dp", "seq"), axis=0, tiled=True),
        lax.all_gather(up_low, ("dp", "seq"), axis=0, tiled=True),
        lax.all_gather(down_low, ("dp", "seq"), axis=0, tiled=True),
    )
    gain_one, query_full, key_full, value_full, projection_full, gain_two, up_full, down_full = (
        gathered
    )
    inputs = tokens.reshape(row_count, model_width).astype(jnp.float32)
    gain_first = gain_one.astype(jnp.float32)
    normed = root_norm(inputs, gain_first).astype(jnp.bfloat16)
    queries = product(normed, query_full).astype(jnp.bfloat16)
    pair_weight = jnp.concatenate([key_full, value_full], axis=1)
    pair_rows = product(normed, pair_weight).astype(jnp.bfloat16)
    key_own = pair_rows[:, :DH].reshape(seqs_here, span_len, DH)
    value_own = pair_rows[:, DH:].reshape(seqs_here, span_len, DH)
    key_all, value_all = (
        lax.all_gather(key_own, "seq", axis=1, tiled=True),
        lax.all_gather(value_own, "seq", axis=1, tiled=True),
    )
    query_pos = lax.axis_index("seq") * span_len + jnp.arange(span_len, dtype=jnp.int32)
    pos_blocks = query_pos.reshape(block_count, block_len)
    key_pos = jnp.arange(length, dtype=jnp.int32)

    def masked_scores(query_block, key_rows, positions, prefix_len):
        flat = query_block.reshape(block_len * H, DH)
        scores = (outer_rows(flat, key_rows) * score_scale).reshape(block_len, H, length)
        visible = (key_pos[None, :] <= positions[:, None]) | (key_pos[None, :] < prefix_len)
        return jnp.where(visible[:, None, :], scores, masked_score)

    def forward_sequence(members):
        query_blocks, key_rows, value_rows, prefix_len = members

        def forward_block(pieces):
            query_block, positions = pieces
            scores = masked_scores(query_block, key_rows, positions, prefix_len)
            maxima = jnp.max(scores, axis=-1, keepdims=True)
            exponent = jnp.exp(scores - maxima)
            totals = jnp.sum(exponent, axis=-1, keepdims=True)
            chances = (exponent / totals).astype(jnp.bfloat16)
            mixed = product(chances.reshape(block_len * H, length), value_rows)
            return (
                mixed.reshape(block_len, H * DH).astype(jnp.bfloat16),
                (maxima + jnp.log(totals))[..., 0],
            )

        return lax.map(forward_block, (query_blocks, pos_blocks))

    query_seq = queries.reshape(seqs_here, block_count, block_len, H, DH)
    attended, log_totals = lax.map(forward_sequence, (query_seq, key_all, value_all, prefix))
    attended = attended.reshape(row_count, H * DH)
    hidden = inputs + product(attended, projection_full)
    gain_second = gain_two.astype(jnp.float32)
    normed_two = root_norm(hidden, gain_second).astype(jnp.bfloat16)
    before = product(normed_two, up_full)
    active = smooth_gate(before).astype(jnp.bfloat16)
    layer_output = (hidden + product(active, down_full)).astype(jnp.bfloat16)
    gathered = (
        lax.all_gather(gain_low, ("dp", "seq"), axis=0, tiled=True),
        lax.all_gather(query_low, ("dp", "seq"), axis=0, tiled=True),
        lax.all_gather(key_low, ("dp", "seq"), axis=0, tiled=True),
        lax.all_gather(value_low, ("dp", "seq"), axis=0, tiled=True),
        lax.all_gather(projection_low, ("dp", "seq"), axis=1, tiled=True),
        lax.all_gather(second_low, ("dp", "seq"), axis=0, tiled=True),
        lax.all_gather(up_low, ("dp", "seq"), axis=0, tiled=True),
        lax.all_gather(down_low, ("dp", "seq"), axis=0, tiled=True),
    )
    gain_one, query_full, key_full, value_full, projection_full, gain_two, up_full, down_full = (
        gathered
    )
    gain_first = gain_one.astype(jnp.float32)
    gain_second = gain_two.astype(jnp.float32)
    pair_weight = jnp.concatenate([key_full, value_full], axis=1)
    grad_out = cotangent.reshape(row_count, model_width)
    grad_start = grad_out.astype(jnp.float32)
    down_grad = inner_rows(active, grad_out)
    grad_active = outer_rows(grad_out, down_full)
    _, gate_pull = jax.vjp(smooth_gate, before)
    grad_before = gate_pull(grad_active)[0].astype(jnp.bfloat16)
    up_grad = inner_rows(normed_two, grad_before)
    grad_normed_two = outer_rows(grad_before, up_full)
    _, second_pull = jax.vjp(root_norm, hidden, gain_second)
    grad_hidden_norm, feedforward_gain_grad = second_pull(grad_normed_two)
    grad_hidden = grad_start + grad_hidden_norm
    grad_branch = grad_hidden.astype(jnp.bfloat16)
    projection_grad = inner_rows(attended, grad_branch)
    grad_attended = outer_rows(grad_branch, projection_full).astype(jnp.bfloat16)
    key_all, value_all = (
        lax.all_gather(key_own, "seq", axis=1, tiled=True),
        lax.all_gather(value_own, "seq", axis=1, tiled=True),
    )
    grad_seq = grad_attended.reshape(seqs_here, block_count, block_len, H, DH)

    def backward_sequence(members):
        query_blocks, grad_blocks, total_blocks, key_rows, value_rows, prefix_len = members

        def backward_block(carry, pieces):
            key_sum, value_sum = carry
            query_block, grad_block, total_block, positions = pieces
            scores = masked_scores(query_block, key_rows, positions, prefix_len)
            chances = jnp.exp(scores - total_block[..., None])
            chance_low = chances.astype(jnp.bfloat16).reshape(block_len * H, length)
            grad_rows = grad_block.reshape(block_len * H, DH)
            query_rows = query_block.reshape(block_len * H, DH)
            grad_chances = outer_rows(grad_rows, value_rows).reshape(block_len, H, length)
            center = jnp.sum(chances * grad_chances, axis=-1, keepdims=True)
            grad_scores = (
                (chances * (grad_chances - center))
                .astype(jnp.bfloat16)
                .reshape(block_len * H, length)
            )
            grad_query = (product(grad_scores, key_rows) * score_scale).astype(jnp.bfloat16)
            key_sum = key_sum + inner_rows(grad_scores, query_rows) * score_scale
            value_sum = value_sum + inner_rows(chance_low, grad_rows)
            return ((key_sum, value_sum), grad_query.reshape(block_len, H * DH))

        empty_sum = jnp.zeros((length, DH), jnp.float32)
        (key_sum, value_sum), grad_queries = lax.scan(
            backward_block,
            (empty_sum, empty_sum),
            (query_blocks, grad_blocks, total_blocks, pos_blocks),
        )
        return (key_sum, value_sum, grad_queries)

    key_terms, value_terms, grad_queries = lax.map(
        backward_sequence, (query_seq, grad_seq, log_totals, key_all, value_all, prefix)
    )
    grad_keys, grad_values = (
        lax.psum_scatter(
            key_terms.astype(jnp.bfloat16), "seq", scatter_dimension=1, tiled=True
        ).astype(jnp.float32),
        lax.psum_scatter(
            value_terms.astype(jnp.bfloat16), "seq", scatter_dimension=1, tiled=True
        ).astype(jnp.float32),
    )
    grad_pair = jnp.concatenate(
        [grad_keys.reshape(row_count, DH), grad_values.reshape(row_count, DH)], axis=1
    ).astype(jnp.bfloat16)
    grad_query_rows = grad_queries.reshape(row_count, H * DH)
    query_grad = inner_rows(normed, grad_query_rows)
    pair_grad = inner_rows(normed, grad_pair)
    key_grad = pair_grad[:, :DH]
    value_grad = pair_grad[:, DH:]
    grad_normed = outer_rows(grad_query_rows, query_full) + outer_rows(grad_pair, pair_weight)
    _, first_pull = jax.vjp(root_norm, inputs, gain_first)
    grad_inputs_norm, attention_gain_grad = first_pull(grad_normed)
    input_grad = (grad_hidden + grad_inputs_norm).reshape(seqs_here, span_len, model_width)
    layer_output = layer_output.reshape(seqs_here, span_len, model_width)
    summed = (
        lax.psum_scatter(attention_gain_grad, ("dp", "seq"), scatter_dimension=0, tiled=True),
        lax.psum_scatter(query_grad, ("dp", "seq"), scatter_dimension=0, tiled=True),
        lax.psum_scatter(key_grad, ("dp", "seq"), scatter_dimension=0, tiled=True),
        lax.psum_scatter(value_grad, ("dp", "seq"), scatter_dimension=0, tiled=True),
        lax.psum_scatter(projection_grad, ("dp", "seq"), scatter_dimension=1, tiled=True),
        lax.psum_scatter(feedforward_gain_grad, ("dp", "seq"), scatter_dimension=0, tiled=True),
        lax.psum_scatter(up_grad, ("dp", "seq"), scatter_dimension=0, tiled=True),
        lax.psum_scatter(down_grad, ("dp", "seq"), scatter_dimension=0, tiled=True),
    )
    return (
        layer_output,
        input_grad,
        summed[0],
        summed[1],
        summed[2],
        summed[3],
        summed[4],
        summed[5],
        summed[6],
        summed[7],
    )


def fits(mesh, tokens, up_weight):
    return (
        mesh.shape["dp"] == 16
        and mesh.shape["seq"] == 2
        and tokens.shape == (16, 1024, 1024)
        and up_weight.shape == (1024, 4096)
    )


def solution(mesh):
    def layer(*args):
        return sharded(mesh, on_grid if fits(mesh, args[0], args[9]) else local)(*args)

    return layer


def sharded(mesh, part):
    return jax.shard_map(
        part,
        mesh=mesh,
        in_specs=(
            P("dp", "seq", None),
            P("dp", "seq", None),
            P("dp"),
            P(("dp", "seq")),
            P(("dp", "seq"), None),
            P(("dp", "seq"), None),
            P(("dp", "seq"), None),
            P(None, ("dp", "seq")),
            P(("dp", "seq")),
            P(("dp", "seq"), None),
            P(("dp", "seq"), None),
        ),
        out_specs=(
            P("dp", "seq", None),
            P("dp", "seq", None),
            P(("dp", "seq")),
            P(("dp", "seq"), None),
            P(("dp", "seq"), None),
            P(("dp", "seq"), None),
            P(None, ("dp", "seq")),
            P(("dp", "seq")),
            P(("dp", "seq"), None),
            P(("dp", "seq"), None),
        ),
        check_vma=False,
    )
```

```python
import functools
import jax
import jax.numpy as jnp
from jax import lax
from jax.experimental import pallas as pl
from jax.experimental.pallas import tpu as pltpu
from jax.sharding import PartitionSpec as P

H = 8
DH = 128
BF = jnp.bfloat16
F32 = jnp.float32
MESH = pl.DeviceIdType.MESH
VMEM_LIMIT = 61 * 2**20
GELU_C = 0.7978845608028654
GELU_A = 0.044715

epsilon = 1e-06
masked_score = -10000.0


def dot(left, right, left_dim, right_dim):
    return lax.dot_general(
        left, right, (((left_dim,), (right_dim,)), ((), ())), preferred_element_type=F32
    )


class Place:
    def __init__(self, send_sems, recv_sems, local_sems):
        dp = lax.axis_index("dp")
        self.y = lax.axis_index("seq")
        self.c = lax.rem(dp, 2)
        self.x = lax.rem(lax.div(dp, 2), 2)
        self.z = lax.div(dp, 4)
        self.send_sems, self.recv_sems, self.local_sems = send_sems, recv_sems, local_sems
        self.n_local = 0
        self.xn = self.at(self.z, 1 - self.x, self.c, self.y)
        self.yn = self.at(self.z, self.x, self.c, 1 - self.y)
        self.cn = self.at(self.z, self.x, 1 - self.c, self.y)

    def at(self, z, x, c, y):
        return ((z * 2 + x) * 2 + c, y)

    def z_to(self, step):
        return lax.rem(self.z + step, 4)

    def zn(self, step):
        return self.at(self.z_to(step), self.x, self.c, self.y)

    def greet(self):
        for device in (self.cn, self.xn, self.yn, self.zn(1), self.zn(2), self.zn(3)):
            pl.semaphore_signal(
                pltpu.get_barrier_semaphore(), inc=1, device_id=device, device_id_type=MESH
            )

    def met(self):
        pl.semaphore_wait(pltpu.get_barrier_semaphore(), 6)

    def send(self, src, dst, recv, device, group):
        pltpu.make_async_remote_copy(
            src_ref=src,
            dst_ref=dst,
            send_sem=self.send_sems.at[group],
            recv_sem=self.recv_sems.at[recv],
            device_id=device,
            device_id_type=MESH,
        ).start()

    def wait(self, like, sem):
        pltpu.make_async_copy(like, like, sem).wait()

    def arrived(self, like, recv):
        self.wait(like, self.recv_sems.at[recv])

    def left(self, like, group):
        self.wait(like, self.send_sems.at[group])

    def move(self, src, dst):
        copy = pltpu.make_async_copy(src, dst, self.local_sems.at[self.n_local])
        self.n_local += 1
        copy.start()
        return copy


class Steps:
    def __init__(self, order):
        self.order, self.done = list(order), set()

    def next(self, count=1):
        for _ in range(count):
            if self.order and self.order[0][2]():
                step, i, _ready = self.order.pop(0)
                step(i)
                self.done.add((step, i))

    def until(self, step, i):
        while (step, i) not in self.done:
            self.next()

    def rest(self):
        while self.order:
            self.next()


def gelu_parts(u):
    square = u * u
    t = jnp.tanh(GELU_C * u * (1.0 + GELU_A * square))
    half = 0.5 * (1.0 + t)
    slope = half + (0.5 * GELU_C) * u * (1.0 - t * t) * (1.0 + (3.0 * GELU_A) * square)
    return u * half, slope


PIECES = 10
RECVS = 11
SENDS = 3
EXTRA = 5
SHIFT_F = (2,)
SHIFT_B = (7,)


SENDS_F = 7
AHEAD = 2


def cut(rows, cols, eighths=1):
    if rows < 128:
        edge = cols - 128 * eighths
        first, second = (pl.ds(0, rows), pl.ds(0, edge)), (pl.ds(0, rows), pl.ds(edge, 128 * eighths))
        halves = (pl.ds(0, rows // 2), first[1]), (pl.ds(rows // 2, rows // 2), first[1])
    else:
        edge = rows - rows * eighths // 8
        half = -(-edge // 32) * 16
        first, second = (pl.ds(0, edge), pl.ds(0, cols)), (pl.ds(edge, rows - edge), pl.ds(0, cols))
        halves = (pl.ds(0, half), first[1]), (pl.ds(half, edge - half), first[1])
    return first, second, halves


def forward_kernel(
    prefix_ref, x_hbm, gy_hbm, wq_hbm, wk_hbm, wv_hbm, g1_ref, g2_ref, wo_hbm, w1_hbm_in, w2_hbm_in,
    out_hbm, w2_hbm, w1_hbm, wa_hbm, wot_hbm, gain_hbm, n1_hbm, q_hbm, kv_hbm, a_hbm, hidden_hbm,
    n2_hbm, slope_hbm, p_hbm, down_hbm,
    wa, wot, w1, w2, x, gy, n1, q, kv, a, hidden, n2, z, slope, p, bias, gain, down_out, down_in, out,
    wq_in, wk_in, wv_in, wo_in, w1_in, w2_in,
    send_sems, recv_sems, local_sems,
):
    me = Place(send_sems, recv_sems, local_sems)
    rows, width = x.shape
    me.greet()
    load_qkv = [me.move(src, dst) for src, dst in ((wq_hbm, wq_in), (wk_hbm, wk_in), (wv_hbm, wv_in))]
    load_x = me.move(x_hbm, x)
    load_wo = me.move(wo_hbm, wo_in)
    load_w1 = me.move(w1_hbm_in, w1_in)
    load_w2 = me.move(w2_hbm_in, w2_in)
    load_gy = me.move(gy_hbm, gy)
    views = [wa, wot] + [w1.at[j] for j in range(4)] + [w2.at[k] for k in range(4)]
    saves = []

    every = slice(None)
    own = (me.z, me.x, me.c, me.y)
    near = me.z + 1 - 2 * lax.rem(me.z, 2)
    upper = lax.div(me.z, 2)
    others = pl.ds(2 - 2 * upper, 2)
    inner = (me.z == 1) | (me.z == 2)
    to_near, to_inner = me.at(near, me.x, me.c, me.y), me.at(2 - upper, me.x, me.c, me.y)

    def shares(i):
        return cut(*views[i].shape[4:], 2)

    def pass_on(i, at, recv, device, group):
        view = views[i].at[at]
        me.send(view, view, i * RECVS + recv, device, i * SENDS_F + group)

    def came(i, at, recv):
        me.arrived(views[i].at[at], i * RECVS + recv)

    def s0(i):
        first, second, _ = shares(i)
        pass_on(i, own + first, 0, to_near, 0)
        pass_on(i, own + first, 1, to_inner, 0)
        pass_on(i, own + first, 3, me.xn, 1)
        pass_on(i, own + first, 4, me.yn, 1)
        pass_on(i, own + second, 5, me.xn, 6)
        pass_on(i, own + second, 6, me.yn, 6)

    def s1(i):
        first, second, _ = shares(i)
        at = (near, me.x, me.c, me.y) + first
        came(i, at, 0)
        pass_on(i, at, 3, me.xn, 1)
        pass_on(i, at, 4, me.yn, 1)
        from_x, from_y = (me.z, 1 - me.x, me.c, me.y) + second, (me.z, me.x, me.c, 1 - me.y) + second
        came(i, from_x, 5)
        came(i, from_y, 6)
        if i % 2:
            pass_on(i, from_y, 7, me.xn, 6)
        else:
            pass_on(i, from_x, 7, me.yn, 6)
        at = (others, me.x, me.c, me.y) + first
        came(i, at, 1)

        @pl.when(inner)
        def _():
            pass_on(i, at, 1, to_near, 3)

        pass_on(i, at, 3, me.xn, 1)
        pass_on(i, at, 4, me.yn, 1)

    def s2(i):
        first, second, (low, high) = shares(i)
        came(i, (every, 1 - me.x, me.c, me.y) + first, 3)
        if i not in SHIFT_F:
            pass_on(i, (every, 1 - me.x, me.c, me.y) + low, 9, me.yn, 1)
        came(i, (every, me.x, me.c, 1 - me.y) + first, 4)
        pass_on(i, (every, me.x, me.c, 1 - me.y) + (first if i in SHIFT_F else high), 9, me.xn, 1)
        came(i, (me.z, 1 - me.x, me.c, 1 - me.y) + second, 7)
        pass_on(i, (me.z, every, me.c, every) + second, 8, to_near, 5)
        pass_on(i, (me.z, every, me.c, every) + second, 2, to_inner, 5)

    def s3(i):
        first, second, _ = shares(i)
        at = (others, every, me.c, every) + second
        came(i, at, 2)

        @pl.when(inner)
        def _():
            pass_on(i, at, 2, to_near, 4)

        came(i, (near, every, me.c, every) + second, 8)
        came(i, (every, 1 - me.x, me.c, 1 - me.y) + first, 9)
        pass_on(i, (every, every, me.c), 10, me.cn, 2)

    def s4(i):
        came(i, (every, every, 1 - me.c), 10)
        if i == 0:
            saves.append(me.move(wa, wa_hbm))
        elif i == 1:
            saves.append(me.move(wot, wot_hbm))
        elif i < 6:
            saves.append(me.move(w1.at[i - 2], w1_hbm.at[i - 2]))
        else:
            k = i - 6
            saves.append(me.move(w2.at[k], w2_hbm.at[:, :, :, :, :, pl.ds(256 * k, 256)]))

    def order():
        for i in range(AHEAD):
            yield s0, i
        for k in range(-1, PIECES + 3):
            for step, i in ((s1, k + 1), (s2, k), (s3, k - 1), (s0, k + 1 + AHEAD), (s4, k - 2)):
                if 0 <= i < PIECES:
                    yield step, i

    steps = Steps((step, i, lambda: True) for step, i in order())

    for kind, ref in ((0, g1_ref), (1, g2_ref)):
        tile = jnp.concatenate([ref[...], jnp.zeros((1, 96), F32)], axis=1)
        for quarter in range(4):
            @pl.when(me.c * 2 + me.y == quarter)
            def _():
                placed = tile if quarter == 0 else pltpu.roll(tile, 32 * quarter, 1)
                wa[(*own, pl.ds(16 * kind, 16), pl.ds(1280, 128))] = jnp.broadcast_to(placed, (16, 128)).astype(BF)
    for load in load_qkv:
        load.wait()
    wa[(*own, every, pl.ds(0, 1024))] = wq_in[...].astype(BF)
    wa[(*own, every, pl.ds(1024, 128))] = wk_in[...].astype(BF)
    wa[(*own, every, pl.ds(1152, 128))] = wv_in[...].astype(BF)
    me.met()
    steps.next()
    load_wo.wait()
    wot[own] = wo_in[...].astype(BF)
    load_w1.wait()
    for j in range(4):
        w1[(j, *own)] = w1_in[:, pl.ds(1024 * j, 1024)].astype(BF)
    load_w2.wait()
    for k in range(4):
        w2[(k, *own)] = w2_in[:, pl.ds(256 * k, 256)].astype(BF)
    steps.next(2)

    first_pos = me.y * rows

    @pl.loop(0, rows // 64)
    def _(t):
        at = pl.multiple_of(t * 64, 64)
        query_pos = first_pos + at + lax.broadcasted_iota(jnp.int32, (64, 2 * rows), 0)
        key_pos = lax.broadcasted_iota(jnp.int32, (64, 2 * rows), 1)
        visible = (key_pos <= query_pos) | (key_pos < prefix_ref[0])
        bias[pl.ds(at, 64), :] = jnp.where(visible, 0.0, -1e30)

    load_x.wait()
    load_gy.wait()
    steps.until(s4, 0)

    for kind in (0, 1):
        for zi in range(4):
            for xi in range(2):
                tile = jnp.zeros((16, 128), F32)
                for ci in range(2):
                    for yi in range(2):
                        tile += wa[zi, xi, ci, yi, pl.ds(16 * kind, 16), pl.ds(1280, 128)].astype(F32)
                gain[kind, :, pl.ds(128 * (2 * zi + xi), 128)] = tile[:8]
    saves.append(me.move(gain, gain_hbm))

    @pl.loop(0, rows // 64)
    def _(t):
        r = pl.ds(pl.multiple_of(t * 64, 64), 64)
        values = x[r, :].astype(F32)
        factor = lax.rsqrt(jnp.mean(values * values, axis=-1, keepdims=True) + epsilon)
        n1[r, :] = (values * factor * gain[0, 0:1, :]).astype(BF)

    kv[me.y] = dot(
        n1[...], wa[:, :, :, :, :, pl.ds(1024, 256)].reshape(width, 256), 1, 0
    ).astype(BF)
    me.send(kv.at[me.y], kv.at[me.y], PIECES * RECVS, me.yn, PIECES * SENDS_F)
    for i in range(2):
        steps.next()
        cols = pl.ds(512 * i, 512)
        q[:, cols] = dot(n1[...], wa[:, :, :, :, :, cols].reshape(width, 512), 1, 0).astype(BF)

    saves.append(me.move(n1, n1_hbm))
    saves.append(me.move(q, q_hbm))
    steps.next()
    me.arrived(kv.at[1 - me.y], PIECES * RECVS)
    saves.append(me.move(kv, kv_hbm))
    length = 2 * rows
    to_log2 = (DH ** -0.5) * 1.4426950408889634

    def head(h):
        cols = pl.ds(h * DH, DH)
        keys = kv[:, :, pl.ds(0, DH)].reshape(length, DH)
        vals = kv[:, :, pl.ds(DH, DH)].reshape(length, DH)
        for t in range(rows // 256):
            r = pl.ds(256 * t, 256)
            s = dot(q[r, cols], keys, 1, 1) * to_log2 + bias[r, :]
            e = jnp.exp2(s - jnp.max(s, axis=-1, keepdims=True))
            chances = (e * (1.0 / jnp.sum(e, axis=-1, keepdims=True))).astype(BF)
            p[(h // 2) % 2, pl.ds((h % 2) * rows + 256 * t, 256), :] = chances
            a[r, cols] = dot(chances, vals, 1, 0).astype(BF)

    p_saves = []
    for h in range(H):
        if h >= 4 and h % 2 == 0:
            p_saves[h // 2 - 2].wait()
        head(h)
        if h % 2:
            p_saves.append(me.move(p.at[(h // 2) % 2], p_hbm.at[h // 2]))
        steps.next()
    saves.extend(p_saves[2:])
    saves.append(me.move(a, a_hbm))
    steps.until(s4, 1)
    for i in range(2):
        cols = pl.ds(512 * i, 512)
        weight = wot[pl.ds(2 * i, 2)].reshape(512, width)
        hidden[:, cols] = x[:, cols].astype(F32) + dot(a[...], weight, 1, 1)
        steps.next()

    @pl.loop(0, rows // 64)
    def _(t):
        r = pl.ds(pl.multiple_of(t * 64, 64), 64)
        values = hidden[r, :]
        factor = lax.rsqrt(jnp.mean(values * values, axis=-1, keepdims=True) + epsilon)
        n2[r, :] = (values * factor * gain[1, 0:1, :]).astype(BF)

    saves.append(me.move(hidden, hidden_hbm))
    saves.append(me.move(n2, n2_hbm))
    steps.next()

    def down_grad_out(j):
        for t in (2 * j, 2 * j + 1):
            cols = pl.ds(pl.multiple_of((2 * t + 1 - me.c) * 256, 256), 256)
            down_out[t] = dot(z[:, cols], gy[...], 0, 0).astype(BF)
        at = pl.ds(2 * j, 2)
        me.send(down_out.at[at], down_in.at[at], PIECES * RECVS + 1 + j, me.cn, PIECES * SENDS_F + 1 + j)

    def down_grad_own(j):
        me.arrived(down_in.at[pl.ds(2 * j, 2)], PIECES * RECVS + 1 + j)
        for t in (2 * j, 2 * j + 1):
            cols = pl.ds(pl.multiple_of((2 * t + me.c) * 256, 256), 256)
            down_in[t] = (dot(z[:, cols], gy[...], 0, 0) + down_in[t].astype(F32)).astype(BF)

    def down(k):
        cols = pl.ds(256 * k, 256)
        for t in range(2):
            r = pl.ds(256 * t, 256)
            y = dot(z[r, :], w2[k].reshape(4096, 256), 1, 0)
            out[r, cols] = (hidden[r, cols] + y).astype(BF)

    for j in range(4):
        steps.until(s4, 2 + j)
        for i in range(2):
            cols, to = pl.ds(512 * i, 512), pl.ds(1024 * j + 512 * i, 512)
            u = dot(n2[...], w1[j, :, :, :, :, :, cols].reshape(width, 512), 1, 0)
            active, steep = gelu_parts(u)
            z[:, to] = active.astype(BF)
            slope[:, to] = steep.astype(BF)
            steps.next()
        down_grad_out(j)
        steps.next()
        if j:
            down_grad_own(j - 1)
            steps.next()
    saves.append(me.move(slope, slope_hbm))
    steps.until(s4, 6)
    down_grad_own(3)
    saves.append(me.move(down_in, down_hbm))
    steps.next()
    down(0)
    for k in (1, 2, 3):
        steps.until(s4, 6 + k)
        down(k)
    steps.rest()
    saves.append(me.move(out, out_hbm))
    for copy in saves:
        copy.wait()
    for i in range(PIECES):
        first, second, _ = shares(i)
        one, four = (0, 0, 0), (every, 0, every)
        for group, at in (
            (0, (pl.ds(0, 2), *one, *first)),
            (1, (pl.ds(0, 3), *four, *first)),
            (2, (every, every, 0)),
            (5, (pl.ds(0, 2), *four, *second)),
            (6, (pl.ds(0, 3), *one, *second)),
        ):
            me.left(views[i].at[at], i * SENDS_F + group)

    @pl.when(inner)
    def _():
        for i in range(PIECES):
            first, second, _ = shares(i)
            me.left(views[i].at[(pl.ds(0, 2), 0, 0, 0) + first], i * SENDS_F + 3)
            me.left(views[i].at[(pl.ds(0, 2), every, 0, every) + second], i * SENDS_F + 4)

    me.left(kv.at[me.y], PIECES * SENDS_F)
    for j in range(4):
        me.left(down_out.at[pl.ds(2 * j, 2)], PIECES * SENDS_F + 1 + j)


def backward_kernel(
    x_hbm, gy_hbm, gain_hbm, w2_hbm, w1_hbm, wa_hbm, wot_hbm, n1_hbm, q_hbm, kv_hbm, a_hbm, hidden_hbm,
    n2_hbm, slope_hbm, p_hbm, down_hbm,
    grad_x_hbm, g2_ref, g1_ref, go_ref, ga_ref,
    gy, n2, hidden, gn, a, q, kv, gain, wbuf, gu, wkv, att, sums, kvsum, kvout, kvin,
    down, pup, pproj, patt, pair_up, pair_att, diag2, diag1, diaga, side2, side1, sidea, line2, line1, linea,
    plane2, plane1, planea,
    send_sems, recv_sems, local_sems,
):
    me = Place(send_sems, recv_sems, local_sems)
    rows, width = gy.shape
    length = 2 * rows
    me.greet()
    load_down = [
        me.move(down_hbm.at[:, :, :, :, pl.ds(256 * k, 256)], down.at[:, :, :, :, pl.ds(256 * k, 256)])
        for k in range(4)
    ]
    load_gy = me.move(gy_hbm, gy)
    load_w2 = [me.move(w2_hbm.at[j], wbuf.at[j]) for j in range(2)]
    load_slope = [me.move(slope_hbm.at[:, pl.ds(1024 * j, 1024)], gu.at[j]) for j in range(2)]
    load_n2 = me.move(n2_hbm, n2)
    load_w1 = [me.move(w1_hbm.at[j], wbuf.at[2 + j]) for j in range(2)]
    load_rest = [
        me.move(src, dst)
        for src, dst in (
            (hidden_hbm, hidden), (gain_hbm, gain), (a_hbm, a), (q_hbm, q), (kv_hbm, kv),
            (wa_hbm.at[:, pl.ds(1024, 256)], wkv),
        )
    ]

    def source(i):
        return pup.at[i - 4] if i < 8 else pproj if i == 8 else patt

    def pair(i):
        return pair_up.at[i - 4] if i < 9 else pair_att

    def part(i, zi, xi, yi, at):
        if i < 4:
            return down.at[zi, xi, yi, at[0], pl.ds(256 * i + at[1].start, at[1].size)]
        return source(i).at[(zi, xi, me.c, yi) + at]

    def group(i, two, one, last):
        return two.at[i] if i < 4 else one.at[i - 4] if i < 9 else last

    def cut_of(i):
        return cut(*((128, 256) if i < 4 else (32, 1024) if i < 9 else (32, 1408)))

    every = slice(None)
    given = set(range(4))

    def send(src, dst, i, recv, device, to):
        me.send(src, dst, i * RECVS + recv, device, i * SENDS + to)

    def came(like, i, recv):
        me.arrived(like, i * RECVS + recv)

    def t0(i):
        send(source(i).at[:, :, 1 - me.c], pair(i), i, 0, me.cn, 2)
        given.add(i)

    def t1(i):
        first, second, (low, high) = cut_of(i)
        diag, plane = group(i, diag2, diag1, diaga), group(i, plane2, plane1, planea)
        if i < 4:
            load_down[i].wait()
        else:
            total, term = source(i), pair(i)
            came(term, i, 0)

            @pl.loop(0, 4)
            def _(zi):
                for xi in range(2):
                    total[zi, xi, me.c] = total[zi, xi, me.c] + term[zi, xi]

        if i not in SHIFT_B:
            send(part(i, every, 1 - me.x, 1 - me.y, low), diag.at[(every,) + low], i, 1, me.yn, 1)
        else:
            high = first
        send(part(i, every, 1 - me.x, 1 - me.y, high), diag.at[(every,) + high], i, 1, me.xn, 1)
        for step in (1, 3, 2):
            send(part(i, me.z_to(step), every, every, second), plane.at[step - 1], i, 2, me.zn(step), 1)

    def t2(i):
        first, second, (low, high) = cut_of(i)
        diag, plane = group(i, diag2, diag1, diaga), group(i, plane2, plane1, planea)
        side = group(i, side2, side1, sidea)
        came(diag.at[(every,) + first], i, 1)
        for step in (1, 3, 2, 0):
            zi = me.z_to(step)
            by_y, by_x = (1 - me.x, me.y, low), (me.x, 1 - me.y, first if i in SHIFT_B else high)
            for xi, yi, half in ((by_x,) if i in SHIFT_B else (by_y, by_x)):
                mine = part(i, zi, xi, yi, half)
                mine[...] = mine[...] + diag[(zi,) + half]
            recv = 2 + step if step else 6
            send(part(i, zi, 1 - me.x, me.y, first), side.at[(0, zi) + first], i, recv, me.xn, 1)
            send(part(i, zi, me.x, 1 - me.y, first), side.at[(1, zi) + first], i, recv, me.yn, 1)
        came(plane, i, 2)
        for xi in range(2):
            for yi in range(2):
                mine = part(i, me.z, xi, yi, second)
                total = mine[...].astype(F32)
                for step in range(3):
                    total += plane[step, xi, yi].astype(F32)
                mine[...] = total.astype(BF)
        send(
            part(i, me.z, 1 - me.x, 1 - me.y, second), diag.at[(me.z,) + second], i, 7,
            me.xn if i % 2 else me.yn, 0,
        )

    def t3(i):
        first, second, _ = cut_of(i)
        diag, side = group(i, diag2, diag1, diaga), group(i, side2, side1, sidea)
        line = group(i, line2, line1, linea)
        for step in (1, 3, 2):
            zi = me.z_to(step)
            came(side.at[(every, zi) + first], i, 2 + step)
            mine = part(i, zi, me.x, me.y, first)
            total = mine[...].astype(F32) + side[(0, zi) + first].astype(F32) + side[(1, zi) + first].astype(F32)
            mine[...] = total.astype(BF)
            send(mine, line.at[(step - 1,) + first], i, 8, me.zn(step), 0)
        came(diag.at[(me.z,) + second], i, 7)
        mine = part(i, me.z, *((me.x, 1 - me.y) if i % 2 else (1 - me.x, me.y)), second)
        mine[...] = mine[...] + diag[(me.z,) + second]
        send(part(i, me.z, 1 - me.x, me.y, second), side.at[(0, me.z) + second], i, 9, me.xn, 0)
        send(part(i, me.z, me.x, 1 - me.y, second), side.at[(1, me.z) + second], i, 9, me.yn, 0)

    def t4(i):
        first, second, _ = cut_of(i)
        side, line = group(i, side2, side1, sidea), group(i, line2, line1, linea)
        came(side.at[(every, me.z) + first], i, 6)
        came(line.at[(every,) + first], i, 8)
        came(side.at[(every, me.z) + second], i, 9)
        out, shift = (
            (g2_ref, 256 * i) if i < 4 else (g1_ref, 1024 * (i - 4)) if i < 8 else (go_ref, 0) if i == 8 else (ga_ref, 0)
        )
        for at in (first, second):
            total = part(i, me.z, me.x, me.y, at)[...].astype(F32)
            total += side[(0, me.z) + at].astype(F32) + side[(1, me.z) + at].astype(F32)
            if at is first:
                for step in range(3):
                    total += line[(step,) + first].astype(F32)
            out[at[0], pl.ds(shift + at[1].start, at[1].size)] = total

    def order():
        yield t1, 0
        for k in range(PIECES + 2):
            for step, i in ((t1, k + 1), (t2, k), (t3, k - 1), (t4, k - 2)):
                if 0 <= i < PIECES:
                    yield step, i

    steps = Steps((step, i, lambda step=step, i=i: step is not t1 or i in given) for step, i in order())
    me.met()
    steps.next()

    def feed_forward(j):
        slot = j % 2
        load_w2[j].wait()
        load_slope[j].wait()
        for i in range(2):
            cols = pl.ds(512 * i, 512)
            grad_active = dot(gy[...], wbuf[slot, cols, :], 1, 1)
            gu[slot, :, cols] = (grad_active * gu[slot, :, cols].astype(F32)).astype(BF)
        steps.next()
        if j < 2:
            load_w2.append(me.move(w2_hbm.at[j + 2], wbuf.at[slot]))
        elif j == 2:
            load_w2.append(me.move(wot_hbm, wbuf.at[0]))
        else:
            load_w2.append(me.move(p_hbm.at[1], wbuf.at[1]))
        for i in range(2):
            term = dot(n2[:, pl.ds(512 * i, 512)], gu[slot], 0, 0)
            pup[j, pl.ds(2 * i, 2)] = term.reshape(2, 2, 2, 2, 32, 1024).astype(BF)
        t0(4 + j)
        steps.next()
        load_w1[j].wait()
        for i in range(2):
            cols = pl.ds(512 * i, 512)
            term = dot(gu[slot], wbuf[2 + slot, cols, :], 1, 1)
            if j == 0:
                gn[:, cols] = term
            else:
                gn[:, cols] = gn[:, cols] + term
        if j < 2:
            load_slope.append(me.move(slope_hbm.at[:, pl.ds(1024 * (j + 2), 1024)], gu.at[slot]))
            load_w1.append(me.move(w1_hbm.at[j + 2], wbuf.at[2 + slot]))
        else:
            load_w1.append(me.move(p_hbm.at[(0, 2)[j - 2]], wbuf.at[2 + slot]))
        steps.next()

    load_gy.wait()
    load_n2.wait()
    for j in range(4):
        feed_forward(j)
    load_x = me.move(x_hbm, n2)
    for copy in load_rest:
        copy.wait()

    sums[...] = jnp.zeros_like(sums)

    @pl.loop(0, rows // 64)
    def _(t):
        r = pl.ds(pl.multiple_of(t * 64, 64), 64)
        grad, values = gn[r, :], hidden[r, :]
        factor = lax.rsqrt(jnp.mean(values * values, axis=-1, keepdims=True) + epsilon)
        scaled = grad * gain[1, 0:1, :]
        middle = jnp.mean(scaled * values, axis=-1, keepdims=True)
        total = gy[r, :].astype(F32) + factor * scaled - values * (factor * factor * factor * middle)
        sums[1] += jnp.sum((grad * values * factor).reshape(8, 8, width), axis=0)
        gn[r, :] = total
        gy[r, :] = total.astype(BF)

    for i in range(2):
        term = dot(gy[:, pl.ds(512 * i, 512)], a[...], 0, 0)
        pproj[pl.ds(2 * i, 2)] = term.reshape(2, 2, 2, 2, 32, width).astype(BF)
    t0(8)
    steps.next()
    load_w2[4].wait()
    for i in range(2):
        cols = pl.ds(512 * i, 512)
        att[:, cols] = dot(gy[...], wbuf[0, :, cols], 1, 0).astype(BF)
    load_p3 = me.move(p_hbm.at[3], wbuf.at[0])
    load_n1 = me.move(n1_hbm, gy)
    steps.next()
    kvsum[...] = jnp.zeros_like(kvsum)
    scale = DH ** -0.5

    def head(h):
        slot = (2, 1, 3, 0)[h // 2]
        cols = pl.ds(h * DH, DH)
        keys = kv[:, :, pl.ds(0, DH)].reshape(length, DH)
        vals = kv[:, :, pl.ds(DH, DH)].reshape(length, DH)
        for t in range(rows // 256):
            r = pl.ds(256 * t, 256)
            grad = att[r, cols]
            chances = wbuf[slot, pl.ds((h % 2) * rows + 256 * t, 256), :]
            grad_chances = dot(grad, vals, 1, 1)
            wide = chances.astype(F32)
            center = jnp.sum(wide * grad_chances, axis=-1, keepdims=True)
            grad_scores = (wide * (grad_chances - center)).astype(BF)
            kvsum[0] += dot(q[r, cols], grad_scores, 0, 0)
            kvsum[1] += dot(grad, chances, 0, 0)
            att[r, cols] = (dot(grad_scores, keys, 1, 0) * scale).astype(BF)

    load_p = (load_w1[4], load_w2[5], load_w1[5], load_p3)
    for h in range(H):
        if h % 2 == 0:
            load_p[h // 2].wait()
        head(h)
        if h == 1:
            load_wq = me.move(wa_hbm.at[:, pl.ds(0, 1024)], wbuf.at[2])
        steps.next()
    for half in (0, 1):
        cols = pl.ds(half * rows, rows)
        kvout[half, :, pl.ds(0, DH)] = (kvsum[0, :, cols] * scale).T.astype(BF)
        kvout[half, :, pl.ds(DH, DH)] = kvsum[1, :, cols].T.astype(BF)
    me.send(kvout.at[1 - me.y], kvin, PIECES * RECVS, me.yn, PIECES * SENDS)
    load_n1.wait()
    for i in range(2):
        term = dot(gy[:, pl.ds(512 * i, 512)], att[...], 0, 0)
        patt[pl.ds(2 * i, 2), :, :, :, :, pl.ds(0, 1024)] = term.reshape(2, 2, 2, 2, 32, width).astype(BF)
    steps.next()
    me.arrived(kvin, PIECES * RECVS)
    kvin[...] = kvin[...] + kvout[me.y]
    for i in range(2):
        term = dot(gy[:, pl.ds(512 * i, 512)], kvin[...], 0, 0)
        patt[pl.ds(2 * i, 2), :, :, :, :, pl.ds(1024, 256)] = term.reshape(2, 2, 2, 2, 32, 256).astype(BF)
    load_wq.wait()
    for i in range(2):
        cols = pl.ds(512 * i, 512)
        hidden[:, cols] = dot(att[...], wbuf[2, cols, :], 1, 1) + dot(kvin[...], wkv[cols, :], 1, 1)
        steps.next()
    load_x.wait()

    @pl.loop(0, rows // 64)
    def _(t):
        r = pl.ds(pl.multiple_of(t * 64, 64), 64)
        grad, values = hidden[r, :], n2[r, :].astype(F32)
        factor = lax.rsqrt(jnp.mean(values * values, axis=-1, keepdims=True) + epsilon)
        scaled = grad * gain[0, 0:1, :]
        middle = jnp.mean(scaled * values, axis=-1, keepdims=True)
        sums[0] += jnp.sum((grad * values * factor).reshape(8, 8, width), axis=0)
        gn[r, :] = gn[r, :] + factor * scaled - values * (factor * factor * factor * middle)

    save_x = me.move(gn, grad_x_hbm)
    for kind in (0, 1):
        row = jnp.sum(sums[kind], axis=0, keepdims=True)
        for zi in range(4):
            for xi in range(2):
                lanes = slice(128 * (2 * zi + xi), 128 * (2 * zi + xi) + 128)
                tile = jnp.broadcast_to(row[:, lanes], (16, 128)).astype(BF)
                for ci in range(2):
                    for yi in range(2):
                        patt[zi, xi, ci, yi, pl.ds(16 * kind, 16), pl.ds(1280, 128)] = tile
    t0(9)
    steps.rest()
    save_x.wait()
    for i in range(PIECES):
        if i < 4:
            at = (every, pl.ds(256 * i, 256))
            me.left(down.at[(pl.ds(0, 3), 0, 0) + at], i * SENDS)
            me.left(down.at[(pl.ds(0, 3), every, every) + at], i * SENDS + 1)
        else:
            me.left(source(i).at[pl.ds(0, 3), 0, 0, 0], i * SENDS)
            me.left(source(i).at[pl.ds(0, 3), :, 0], i * SENDS + 1)
            me.left(source(i).at[:, :, 0], i * SENDS + 2)
    me.left(kvin, PIECES * SENDS)


def on_grid(
    tokens, cotangent, prefix, attention_gain, query_weight, key_weight, value_weight, projection_weight,
    feedforward_gain, up_weight, down_weight,
):
    rows, width = tokens.shape[1:]
    vmem, hbm = pl.BlockSpec(memory_space=pltpu.VMEM), pl.BlockSpec(memory_space=pl.ANY)
    smem = pl.BlockSpec(memory_space=pltpu.SMEM)
    x, gy = tokens.reshape(rows, width), cotangent.reshape(rows, width)
    sds = jax.ShapeDtypeStruct
    grid = (4, 2, 2, 2)
    send_sems_f, send_sems, recv_sems = (
        pltpu.SemaphoreType.DMA((PIECES * n + EXTRA,)) for n in (SENDS_F, SENDS, RECVS)
    )
    length = 2 * rows
    out = pl.pallas_call(
        forward_kernel,
        out_shape=(
            sds((rows, width), BF),
            sds((*grid, 128, 1024), BF),
            sds((4, *grid, 32, 1024), BF),
            sds((*grid, 32, 1408), BF),
            sds((*grid, 32, 1024), BF),
            sds((2, 8, width), F32),
            sds((rows, width), BF),
            sds((rows, width), BF),
            sds((2, rows, 256), BF),
            sds((rows, width), BF),
            sds((rows, width), F32),
            sds((rows, width), BF),
            sds((rows, 4096), BF),
            sds((4, 2 * rows, length), BF),
            sds((8, 256, width), BF),
        ),
        in_specs=[smem] + [hbm] * 5 + [vmem] * 2 + [hbm] * 3,
        out_specs=[hbm] * 15,
        scratch_shapes=[
            pltpu.VMEM((*grid, 32, 1408), BF),
            pltpu.VMEM((*grid, 32, 1024), BF),
            pltpu.VMEM((4, *grid, 32, 1024), BF),
            pltpu.VMEM((4, *grid, 128, 256), BF),
            pltpu.VMEM((rows, width), BF),
            pltpu.VMEM((rows, width), BF),
            pltpu.VMEM((rows, width), BF),
            pltpu.VMEM((rows, width), BF),
            pltpu.VMEM((2, rows, 256), BF),
            pltpu.VMEM((rows, width), BF),
            pltpu.VMEM((rows, width), F32),
            pltpu.VMEM((rows, width), BF),
            pltpu.VMEM((rows, 4096), BF),
            pltpu.VMEM((rows, 4096), BF),
            pltpu.VMEM((2, 2 * rows, length), BF),
            pltpu.VMEM((rows, length), F32),
            pltpu.VMEM((2, 8, width), F32),
            pltpu.VMEM((8, 256, width), BF),
            pltpu.VMEM((8, 256, width), BF),
            pltpu.VMEM((rows, width), BF),
            pltpu.VMEM(query_weight.shape, F32),
            pltpu.VMEM(key_weight.shape, F32),
            pltpu.VMEM(value_weight.shape, F32),
            pltpu.VMEM((32, width), F32),
            pltpu.VMEM(up_weight.shape, F32),
            pltpu.VMEM(down_weight.shape, F32),
            send_sems_f,
            recv_sems,
            pltpu.SemaphoreType.DMA((40,)),
        ],
        compiler_params=pltpu.CompilerParams(
            collective_id=0, has_side_effects=True, vmem_limit_bytes=VMEM_LIMIT
        ),
    )(
        prefix, x, gy, query_weight, key_weight, value_weight, attention_gain.reshape(1, 32),
        feedforward_gain.reshape(1, 32), projection_weight.T, up_weight, down_weight,
    )
    layer_output, w2, w1, wa, wot, gain, n1, q, kv, a, hidden, n2, slope, p, down = out
    grad_x, g2, g1, go, ga = pl.pallas_call(
        backward_kernel,
        out_shape=(
            sds((rows, width), F32),
            sds((128, 1024), F32),
            sds((32, 4096), F32),
            sds((32, 1024), F32),
            sds((32, 1408), F32),
        ),
        in_specs=[hbm] * 16,
        out_specs=[hbm] + [vmem] * 4,
        scratch_shapes=[
            pltpu.VMEM((rows, width), BF),
            pltpu.VMEM((rows, width), BF),
            pltpu.VMEM((rows, width), F32),
            pltpu.VMEM((rows, width), F32),
            pltpu.VMEM((rows, width), BF),
            pltpu.VMEM((rows, width), BF),
            pltpu.VMEM((2, rows, 256), BF),
            pltpu.VMEM((2, 8, width), F32),
            pltpu.VMEM((4, 1024, 1024), BF),
            pltpu.VMEM((2, rows, 1024), BF),
            pltpu.VMEM((width, 256), BF),
            pltpu.VMEM((rows, width), BF),
            pltpu.VMEM((2, 8, width), F32),
            pltpu.VMEM((2, DH, length), F32),
            pltpu.VMEM((2, rows, 256), BF),
            pltpu.VMEM((rows, 256), BF),
            pltpu.VMEM((4, 2, 2, 128, 1024), BF),
            pltpu.VMEM((4, *grid, 32, 1024), BF),
            pltpu.VMEM((*grid, 32, 1024), BF),
            pltpu.VMEM((*grid, 32, 1408), BF),
            pltpu.VMEM((5, 4, 2, 2, 32, 1024), BF),
            pltpu.VMEM((4, 2, 2, 32, 1408), BF),
            pltpu.VMEM((4, 4, 128, 256), BF), pltpu.VMEM((5, 4, 32, 1024), BF), pltpu.VMEM((4, 32, 1408), BF),
            pltpu.VMEM((4, 2, 4, 128, 256), BF), pltpu.VMEM((5, 2, 4, 32, 1024), BF), pltpu.VMEM((2, 4, 32, 1408), BF),
            pltpu.VMEM((4, 3, 128, 256), BF), pltpu.VMEM((5, 3, 32, 1024), BF), pltpu.VMEM((3, 32, 1408), BF),
            pltpu.VMEM((4, 3, 2, 2, 16, 256), BF), pltpu.VMEM((5, 3, 2, 2, 32, 128), BF), pltpu.VMEM((3, 2, 2, 32, 128), BF),
            send_sems,
            recv_sems,
            pltpu.SemaphoreType.DMA((40,)),
        ],
        compiler_params=pltpu.CompilerParams(
            collective_id=1, has_side_effects=True, vmem_limit_bytes=VMEM_LIMIT
        ),
    )(
        x, gy, gain, w2.reshape(4, 1024, 1024), w1.reshape(4, 1024, 1024), wa.reshape(1024, 1408), wot.reshape(1024, 1024),
        n1, q, kv, a, hidden, n2, slope, p, down.reshape(4, 2, 2, 128, 1024),
    )
    layer_output, grad_x, g1_gain, gq, gk, gv, gp, g2_gain, g1, g2 = pl.pallas_call(
        hand_out,
        out_shape=(
            sds((rows, width), BF),
            sds((rows, width), F32),
            sds((1, 32), F32),
            sds((32, 1024), F32),
            sds((32, 128), F32),
            sds((32, 128), F32),
            sds((32, 1024), F32),
            sds((1, 32), F32),
            sds((32, 4096), F32),
            sds((128, 1024), F32),
        ),
        in_specs=[hbm] * 6,
        out_specs=[hbm, hbm, vmem, hbm, hbm, hbm, hbm, vmem, hbm, hbm],
        scratch_shapes=[
            pltpu.VMEM((rows, width), BF),
            pltpu.VMEM((rows, width), F32),
            pltpu.VMEM((32, 1408), F32),
            pltpu.VMEM((32, 1024), F32),
            pltpu.VMEM((32, 4096), F32),
            pltpu.VMEM((128, 1024), F32),
            pltpu.SemaphoreType.DMA((24,)),
        ],
        compiler_params=pltpu.CompilerParams(vmem_limit_bytes=VMEM_LIMIT),
    )(layer_output, grad_x, ga, go, g1, g2)
    return (
        layer_output.reshape(tokens.shape),
        grad_x.reshape(tokens.shape),
        g1_gain.reshape(32),
        gq,
        gk,
        gv,
        gp.T,
        g2_gain.reshape(32),
        g1,
        g2,
    )


def hand_out(
    y_in, x_in, a_in, p_in, up_in, down_in,
    y_out, x_out, g1_out, q_out, k_out, v_out, p_out, g2_out, up_out, down_out,
    y, x, a, p, up, down, sems,
):
    started = 0

    def move(src, dst):
        nonlocal started
        copy = pltpu.make_async_copy(src, dst, sems.at[started])
        started += 1
        copy.start()
        return copy

    quarters = [pl.ds(i * (x.shape[0] // 4), x.shape[0] // 4) for i in range(4)]
    moves = [(x_in.at[r], x.at[r], x_out.at[r]) for r in quarters]
    moves += [(y_in, y, y_out), (up_in, up, up_out), (down_in, down, down_out), (p_in, p, p_out)]
    loads = [move(a_in, a)] + [move(src, by) for src, by, _ in moves]
    stores = []
    loads[0].wait()
    for cols, out in ((pl.ds(0, 1024), q_out), (pl.ds(1024, 128), k_out), (pl.ds(1152, 128), v_out)):
        stores.append(move(a.at[:, cols], out))
    for load, (_, by, dst) in zip(loads[1:], moves):
        load.wait()
        stores.append(move(by, dst))
    quarter = lax.rem(lax.axis_index("dp"), 2) * 2 + lax.axis_index("seq")
    for row, out in ((0, g1_out), (16, g2_out)):
        for k in range(4):
            @pl.when(quarter == k)
            def _():
                out[...] = a[row : row + 1, 1280 + 32 * k : 1312 + 32 * k]
    for copy in stores:
        copy.wait()


def root_norm(values, gain):
    factor = lax.rsqrt(jnp.mean(values * values, axis=-1, keepdims=True) + epsilon)
    return values * factor * gain


def smooth_gate(values):
    return jax.nn.gelu(values, approximate=True)


def product(left, right):
    return jnp.dot(left, right, preferred_element_type=jnp.float32)


def inner_rows(left, right):
    return lax.dot_general(
        left, right, (((0,), (0,)), ((), ())), preferred_element_type=jnp.float32
    )


def outer_rows(left, right):
    return lax.dot_general(
        left, right, (((1,), (1,)), ((), ())), preferred_element_type=jnp.float32
    )


def local(
    tokens,
    cotangent,
    prefix,
    attention_gain,
    query_weight,
    key_weight,
    value_weight,
    projection_weight,
    feedforward_gain,
    up_weight,
    down_weight,
):
    seqs_here, span_len, model_width = tokens.shape
    length = span_len * lax.axis_size("seq")
    row_count = seqs_here * span_len
    block_len = min(64, span_len)
    block_count = span_len // block_len
    score_scale = DH ** (-0.5)
    gain_low = attention_gain.astype(jnp.bfloat16)
    query_low = query_weight.astype(jnp.bfloat16)
    key_low = key_weight.astype(jnp.bfloat16)
    value_low = value_weight.astype(jnp.bfloat16)
    projection_low = projection_weight.astype(jnp.bfloat16)
    second_low = feedforward_gain.astype(jnp.bfloat16)
    up_low = up_weight.astype(jnp.bfloat16)
    down_low = down_weight.astype(jnp.bfloat16)
    gathered = (
        lax.all_gather(gain_low, ("dp", "seq"), axis=0, tiled=True),
        lax.all_gather(query_low, ("dp", "seq"), axis=0, tiled=True),
        lax.all_gather(key_low, ("dp", "seq"), axis=0, tiled=True),
        lax.all_gather(value_low, ("dp", "seq"), axis=0, tiled=True),
        lax.all_gather(projection_low, ("dp", "seq"), axis=1, tiled=True),
        lax.all_gather(second_low, ("dp", "seq"), axis=0, tiled=True),
        lax.all_gather(up_low, ("dp", "seq"), axis=0, tiled=True),
        lax.all_gather(down_low, ("dp", "seq"), axis=0, tiled=True),
    )
    gain_one, query_full, key_full, value_full, projection_full, gain_two, up_full, down_full = (
        gathered
    )
    inputs = tokens.reshape(row_count, model_width).astype(jnp.float32)
    gain_first = gain_one.astype(jnp.float32)
    normed = root_norm(inputs, gain_first).astype(jnp.bfloat16)
    queries = product(normed, query_full).astype(jnp.bfloat16)
    pair_weight = jnp.concatenate([key_full, value_full], axis=1)
    pair_rows = product(normed, pair_weight).astype(jnp.bfloat16)
    key_own = pair_rows[:, :DH].reshape(seqs_here, span_len, DH)
    value_own = pair_rows[:, DH:].reshape(seqs_here, span_len, DH)
    key_all, value_all = (
        lax.all_gather(key_own, "seq", axis=1, tiled=True),
        lax.all_gather(value_own, "seq", axis=1, tiled=True),
    )
    query_pos = lax.axis_index("seq") * span_len + jnp.arange(span_len, dtype=jnp.int32)
    pos_blocks = query_pos.reshape(block_count, block_len)
    key_pos = jnp.arange(length, dtype=jnp.int32)

    def masked_scores(query_block, key_rows, positions, prefix_len):
        flat = query_block.reshape(block_len * H, DH)
        scores = (outer_rows(flat, key_rows) * score_scale).reshape(block_len, H, length)
        visible = (key_pos[None, :] <= positions[:, None]) | (key_pos[None, :] < prefix_len)
        return jnp.where(visible[:, None, :], scores, masked_score)

    def forward_sequence(members):
        query_blocks, key_rows, value_rows, prefix_len = members

        def forward_block(pieces):
            query_block, positions = pieces
            scores = masked_scores(query_block, key_rows, positions, prefix_len)
            maxima = jnp.max(scores, axis=-1, keepdims=True)
            exponent = jnp.exp(scores - maxima)
            totals = jnp.sum(exponent, axis=-1, keepdims=True)
            chances = (exponent / totals).astype(jnp.bfloat16)
            mixed = product(chances.reshape(block_len * H, length), value_rows)
            return (
                mixed.reshape(block_len, H * DH).astype(jnp.bfloat16),
                (maxima + jnp.log(totals))[..., 0],
            )

        return lax.map(forward_block, (query_blocks, pos_blocks))

    query_seq = queries.reshape(seqs_here, block_count, block_len, H, DH)
    attended, log_totals = lax.map(forward_sequence, (query_seq, key_all, value_all, prefix))
    attended = attended.reshape(row_count, H * DH)
    hidden = inputs + product(attended, projection_full)
    gain_second = gain_two.astype(jnp.float32)
    normed_two = root_norm(hidden, gain_second).astype(jnp.bfloat16)
    before = product(normed_two, up_full)
    active = smooth_gate(before).astype(jnp.bfloat16)
    layer_output = (hidden + product(active, down_full)).astype(jnp.bfloat16)
    gathered = (
        lax.all_gather(gain_low, ("dp", "seq"), axis=0, tiled=True),
        lax.all_gather(query_low, ("dp", "seq"), axis=0, tiled=True),
        lax.all_gather(key_low, ("dp", "seq"), axis=0, tiled=True),
        lax.all_gather(value_low, ("dp", "seq"), axis=0, tiled=True),
        lax.all_gather(projection_low, ("dp", "seq"), axis=1, tiled=True),
        lax.all_gather(second_low, ("dp", "seq"), axis=0, tiled=True),
        lax.all_gather(up_low, ("dp", "seq"), axis=0, tiled=True),
        lax.all_gather(down_low, ("dp", "seq"), axis=0, tiled=True),
    )
    gain_one, query_full, key_full, value_full, projection_full, gain_two, up_full, down_full = (
        gathered
    )
    gain_first = gain_one.astype(jnp.float32)
    gain_second = gain_two.astype(jnp.float32)
    pair_weight = jnp.concatenate([key_full, value_full], axis=1)
    grad_out = cotangent.reshape(row_count, model_width)
    grad_start = grad_out.astype(jnp.float32)
    down_grad = inner_rows(active, grad_out)
    grad_active = outer_rows(grad_out, down_full)
    _, gate_pull = jax.vjp(smooth_gate, before)
    grad_before = gate_pull(grad_active)[0].astype(jnp.bfloat16)
    up_grad = inner_rows(normed_two, grad_before)
    grad_normed_two = outer_rows(grad_before, up_full)
    _, second_pull = jax.vjp(root_norm, hidden, gain_second)
    grad_hidden_norm, feedforward_gain_grad = second_pull(grad_normed_two)
    grad_hidden = grad_start + grad_hidden_norm
    grad_branch = grad_hidden.astype(jnp.bfloat16)
    projection_grad = inner_rows(attended, grad_branch)
    grad_attended = outer_rows(grad_branch, projection_full).astype(jnp.bfloat16)
    key_all, value_all = (
        lax.all_gather(key_own, "seq", axis=1, tiled=True),
        lax.all_gather(value_own, "seq", axis=1, tiled=True),
    )
    grad_seq = grad_attended.reshape(seqs_here, block_count, block_len, H, DH)

    def backward_sequence(members):
        query_blocks, grad_blocks, total_blocks, key_rows, value_rows, prefix_len = members

        def backward_block(carry, pieces):
            key_sum, value_sum = carry
            query_block, grad_block, total_block, positions = pieces
            scores = masked_scores(query_block, key_rows, positions, prefix_len)
            chances = jnp.exp(scores - total_block[..., None])
            chance_low = chances.astype(jnp.bfloat16).reshape(block_len * H, length)
            grad_rows = grad_block.reshape(block_len * H, DH)
            query_rows = query_block.reshape(block_len * H, DH)
            grad_chances = outer_rows(grad_rows, value_rows).reshape(block_len, H, length)
            center = jnp.sum(chances * grad_chances, axis=-1, keepdims=True)
            grad_scores = (
                (chances * (grad_chances - center))
                .astype(jnp.bfloat16)
                .reshape(block_len * H, length)
            )
            grad_query = (product(grad_scores, key_rows) * score_scale).astype(jnp.bfloat16)
            key_sum = key_sum + inner_rows(grad_scores, query_rows) * score_scale
            value_sum = value_sum + inner_rows(chance_low, grad_rows)
            return ((key_sum, value_sum), grad_query.reshape(block_len, H * DH))

        empty_sum = jnp.zeros((length, DH), jnp.float32)
        (key_sum, value_sum), grad_queries = lax.scan(
            backward_block,
            (empty_sum, empty_sum),
            (query_blocks, grad_blocks, total_blocks, pos_blocks),
        )
        return (key_sum, value_sum, grad_queries)

    key_terms, value_terms, grad_queries = lax.map(
        backward_sequence, (query_seq, grad_seq, log_totals, key_all, value_all, prefix)
    )
    grad_keys, grad_values = (
        lax.psum_scatter(
            key_terms.astype(jnp.bfloat16), "seq", scatter_dimension=1, tiled=True
        ).astype(jnp.float32),
        lax.psum_scatter(
            value_terms.astype(jnp.bfloat16), "seq", scatter_dimension=1, tiled=True
        ).astype(jnp.float32),
    )
    grad_pair = jnp.concatenate(
        [grad_keys.reshape(row_count, DH), grad_values.reshape(row_count, DH)], axis=1
    ).astype(jnp.bfloat16)
    grad_query_rows = grad_queries.reshape(row_count, H * DH)
    query_grad = inner_rows(normed, grad_query_rows)
    pair_grad = inner_rows(normed, grad_pair)
    key_grad = pair_grad[:, :DH]
    value_grad = pair_grad[:, DH:]
    grad_normed = outer_rows(grad_query_rows, query_full) + outer_rows(grad_pair, pair_weight)
    _, first_pull = jax.vjp(root_norm, inputs, gain_first)
    grad_inputs_norm, attention_gain_grad = first_pull(grad_normed)
    input_grad = (grad_hidden + grad_inputs_norm).reshape(seqs_here, span_len, model_width)
    layer_output = layer_output.reshape(seqs_here, span_len, model_width)
    summed = (
        lax.psum_scatter(attention_gain_grad, ("dp", "seq"), scatter_dimension=0, tiled=True),
        lax.psum_scatter(query_grad, ("dp", "seq"), scatter_dimension=0, tiled=True),
        lax.psum_scatter(key_grad, ("dp", "seq"), scatter_dimension=0, tiled=True),
        lax.psum_scatter(value_grad, ("dp", "seq"), scatter_dimension=0, tiled=True),
        lax.psum_scatter(projection_grad, ("dp", "seq"), scatter_dimension=1, tiled=True),
        lax.psum_scatter(feedforward_gain_grad, ("dp", "seq"), scatter_dimension=0, tiled=True),
        lax.psum_scatter(up_grad, ("dp", "seq"), scatter_dimension=0, tiled=True),
        lax.psum_scatter(down_grad, ("dp", "seq"), scatter_dimension=0, tiled=True),
    )
    return (
        layer_output,
        input_grad,
        summed[0],
        summed[1],
        summed[2],
        summed[3],
        summed[4],
        summed[5],
        summed[6],
        summed[7],
    )


def fits(mesh, tokens, up_weight):
    return (
        mesh.shape["dp"] == 16
        and mesh.shape["seq"] == 2
        and tokens.shape == (16, 1024, 1024)
        and up_weight.shape == (1024, 4096)
    )


def solution(mesh):
    def layer(*args):
        return sharded(mesh, on_grid if fits(mesh, args[0], args[9]) else local)(*args)

    return layer


def sharded(mesh, part):
    return jax.shard_map(
        part,
        mesh=mesh,
        in_specs=(
            P("dp", "seq", None),
            P("dp", "seq", None),
            P("dp"),
            P(("dp", "seq")),
            P(("dp", "seq"), None),
            P(("dp", "seq"), None),
            P(("dp", "seq"), None),
            P(None, ("dp", "seq")),
            P(("dp", "seq")),
            P(("dp", "seq"), None),
            P(("dp", "seq"), None),
        ),
        out_specs=(
            P("dp", "seq", None),
            P("dp", "seq", None),
            P(("dp", "seq")),
            P(("dp", "seq"), None),
            P(("dp", "seq"), None),
            P(("dp", "seq"), None),
            P(None, ("dp", "seq")),
            P(("dp", "seq")),
            P(("dp", "seq"), None),
            P(("dp", "seq"), None),
        ),
        check_vma=False,
    )
```

```python
import functools
import jax
import jax.numpy as jnp
from jax import lax
from jax.experimental import pallas as pl
from jax.experimental.pallas import tpu as pltpu
from jax.sharding import PartitionSpec as P

H = 8
DH = 128
BF = jnp.bfloat16
F32 = jnp.float32
MESH = pl.DeviceIdType.MESH
VMEM_LIMIT = 61 * 2**20
GELU_C = 0.7978845608028654
GELU_A = 0.044715

epsilon = 1e-06
masked_score = -10000.0


def dot(left, right, left_dim, right_dim):
    return lax.dot_general(
        left, right, (((left_dim,), (right_dim,)), ((), ())), preferred_element_type=F32
    )


class Place:
    def __init__(self, send_sems, recv_sems, local_sems):
        dp = lax.axis_index("dp")
        self.y = lax.axis_index("seq")
        self.c = lax.rem(dp, 2)
        self.x = lax.rem(lax.div(dp, 2), 2)
        self.z = lax.div(dp, 4)
        self.send_sems, self.recv_sems, self.local_sems = send_sems, recv_sems, local_sems
        self.n_local = 0
        self.xn = self.at(self.z, 1 - self.x, self.c, self.y)
        self.yn = self.at(self.z, self.x, self.c, 1 - self.y)
        self.cn = self.at(self.z, self.x, 1 - self.c, self.y)

    def at(self, z, x, c, y):
        return ((z * 2 + x) * 2 + c, y)

    def z_to(self, step):
        return lax.rem(self.z + step, 4)

    def zn(self, step):
        return self.at(self.z_to(step), self.x, self.c, self.y)

    def greet(self):
        for device in (self.cn, self.xn, self.yn, self.zn(1), self.zn(2), self.zn(3)):
            pl.semaphore_signal(
                pltpu.get_barrier_semaphore(), inc=1, device_id=device, device_id_type=MESH
            )

    def met(self):
        pl.semaphore_wait(pltpu.get_barrier_semaphore(), 6)

    def send(self, src, dst, recv, device, group):
        pltpu.make_async_remote_copy(
            src_ref=src,
            dst_ref=dst,
            send_sem=self.send_sems.at[group],
            recv_sem=self.recv_sems.at[recv],
            device_id=device,
            device_id_type=MESH,
        ).start()

    def wait(self, like, sem):
        pltpu.make_async_copy(like, like, sem).wait()

    def arrived(self, like, recv):
        self.wait(like, self.recv_sems.at[recv])

    def left(self, like, group):
        self.wait(like, self.send_sems.at[group])

    def move(self, src, dst):
        copy = pltpu.make_async_copy(src, dst, self.local_sems.at[self.n_local])
        self.n_local += 1
        copy.start()
        return copy


class Steps:
    def __init__(self, order):
        self.order, self.done = list(order), set()

    def next(self, count=1):
        for _ in range(count):
            if self.order and self.order[0][2]():
                step, i, _ready = self.order.pop(0)
                step(i)
                self.done.add((step, i))

    def until(self, step, i):
        while (step, i) not in self.done:
            self.next()

    def rest(self):
        while self.order:
            self.next()


def gelu_parts(u):
    square = u * u
    t = jnp.tanh(GELU_C * u * (1.0 + GELU_A * square))
    half = 0.5 * (1.0 + t)
    slope = half + (0.5 * GELU_C) * u * (1.0 - t * t) * (1.0 + (3.0 * GELU_A) * square)
    return u * half, slope


PIECES = 10
RECVS = 11
SENDS = 3
EXTRA = 5
SHIFT_F = (2,)
SHIFT_B = (7,)


SENDS_F = 7
AHEAD = 2


def cut(rows, cols, eighths=1):
    if rows < 128:
        edge = cols - 128 * eighths
        first, second = (pl.ds(0, rows), pl.ds(0, edge)), (pl.ds(0, rows), pl.ds(edge, 128 * eighths))
        halves = (pl.ds(0, rows // 2), first[1]), (pl.ds(rows // 2, rows // 2), first[1])
    else:
        edge = rows - rows * eighths // 8
        half = -(-edge // 32) * 16
        first, second = (pl.ds(0, edge), pl.ds(0, cols)), (pl.ds(edge, rows - edge), pl.ds(0, cols))
        halves = (pl.ds(0, half), first[1]), (pl.ds(half, edge - half), first[1])
    return first, second, halves


def forward_kernel(
    prefix_ref, x_hbm, gy_hbm, wq_hbm, wk_hbm, wv_hbm, g1_ref, g2_ref, wo_hbm, w1_hbm_in, w2_hbm_in,
    out_hbm, w2_hbm, w1_hbm, wa_hbm, wot_hbm, gain_hbm, n1_hbm, q_hbm, kv_hbm, a_hbm, hidden_hbm,
    n2_hbm, slope_hbm, p_hbm, down_hbm,
    wa, wot, w1, w2, x, gy, n1, q, kv, a, hidden, n2, z, slope, p, bias, gain, down_out, down_in, out,
    wq_in, wk_in, wv_in, wo_in, w1_in, w2_in,
    send_sems, recv_sems, local_sems,
):
    me = Place(send_sems, recv_sems, local_sems)
    rows, width = x.shape
    me.greet()
    load_qkv = [me.move(src, dst) for src, dst in ((wq_hbm, wq_in), (wk_hbm, wk_in), (wv_hbm, wv_in))]
    views = [wa, wot] + [w1.at[j] for j in range(4)] + [w2.at[k] for k in range(4)]
    saves = []

    every = slice(None)
    own = (me.z, me.x, me.c, me.y)
    near = me.z + 1 - 2 * lax.rem(me.z, 2)
    upper = lax.div(me.z, 2)
    others = pl.ds(2 - 2 * upper, 2)
    inner = (me.z == 1) | (me.z == 2)
    to_near, to_inner = me.at(near, me.x, me.c, me.y), me.at(2 - upper, me.x, me.c, me.y)

    def shares(i):
        return cut(*views[i].shape[4:], 2)

    def pass_on(i, at, recv, device, group):
        view = views[i].at[at]
        me.send(view, view, i * RECVS + recv, device, i * SENDS_F + group)

    def came(i, at, recv):
        me.arrived(views[i].at[at], i * RECVS + recv)

    def s0(i):
        first, second, _ = shares(i)
        pass_on(i, own + first, 0, to_near, 0)
        pass_on(i, own + first, 1, to_inner, 0)
        pass_on(i, own + first, 3, me.xn, 1)
        pass_on(i, own + first, 4, me.yn, 1)
        pass_on(i, own + second, 5, me.xn, 6)
        pass_on(i, own + second, 6, me.yn, 6)

    def s1(i):
        first, second, _ = shares(i)
        at = (near, me.x, me.c, me.y) + first
        came(i, at, 0)
        pass_on(i, at, 3, me.xn, 1)
        pass_on(i, at, 4, me.yn, 1)
        from_x, from_y = (me.z, 1 - me.x, me.c, me.y) + second, (me.z, me.x, me.c, 1 - me.y) + second
        came(i, from_x, 5)
        came(i, from_y, 6)
        if i % 2:
            pass_on(i, from_y, 7, me.xn, 6)
        else:
            pass_on(i, from_x, 7, me.yn, 6)
        at = (others, me.x, me.c, me.y) + first
        came(i, at, 1)

        @pl.when(inner)
        def _():
            pass_on(i, at, 1, to_near, 3)

        pass_on(i, at, 3, me.xn, 1)
        pass_on(i, at, 4, me.yn, 1)

    def s2(i):
        first, second, (low, high) = shares(i)
        came(i, (every, 1 - me.x, me.c, me.y) + first, 3)
        if i not in SHIFT_F:
            pass_on(i, (every, 1 - me.x, me.c, me.y) + low, 9, me.yn, 1)
        came(i, (every, me.x, me.c, 1 - me.y) + first, 4)
        pass_on(i, (every, me.x, me.c, 1 - me.y) + (first if i in SHIFT_F else high), 9, me.xn, 1)
        came(i, (me.z, 1 - me.x, me.c, 1 - me.y) + second, 7)
        pass_on(i, (me.z, every, me.c, every) + second, 8, to_near, 5)
        pass_on(i, (me.z, every, me.c, every) + second, 2, to_inner, 5)

    def s3(i):
        first, second, _ = shares(i)
        at = (others, every, me.c, every) + second
        came(i, at, 2)

        @pl.when(inner)
        def _():
            pass_on(i, at, 2, to_near, 4)

        came(i, (near, every, me.c, every) + second, 8)
        came(i, (every, 1 - me.x, me.c, 1 - me.y) + first, 9)
        pass_on(i, (every, every, me.c), 10, me.cn, 2)

    def s4(i):
        came(i, (every, every, 1 - me.c), 10)
        if i == 0:
            saves.append(me.move(wa, wa_hbm))
        elif i == 1:
            saves.append(me.move(wot, wot_hbm))
        elif i < 6:
            saves.append(me.move(w1.at[i - 2], w1_hbm.at[i - 2]))
        else:
            k = i - 6
            saves.append(me.move(w2.at[k], w2_hbm.at[:, :, :, :, :, pl.ds(256 * k, 256)]))

    def order():
        for i in range(AHEAD):
            yield s0, i
        for k in range(-1, PIECES + 3):
            for step, i in ((s1, k + 1), (s2, k), (s3, k - 1), (s0, k + 1 + AHEAD), (s4, k - 2)):
                if 0 <= i < PIECES:
                    yield step, i

    steps = Steps((step, i, lambda: True) for step, i in order())

    for kind, ref in ((0, g1_ref), (1, g2_ref)):
        tile = jnp.concatenate([ref[...], jnp.zeros((1, 96), F32)], axis=1)
        for quarter in range(4):
            @pl.when(me.c * 2 + me.y == quarter)
            def _():
                placed = tile if quarter == 0 else pltpu.roll(tile, 32 * quarter, 1)
                wa[(*own, pl.ds(16 * kind, 16), pl.ds(1280, 128))] = jnp.broadcast_to(placed, (16, 128)).astype(BF)
    for load in load_qkv:
        load.wait()
    wa[(*own, every, pl.ds(0, 1024))] = wq_in[...].astype(BF)
    wa[(*own, every, pl.ds(1024, 128))] = wk_in[...].astype(BF)
    wa[(*own, every, pl.ds(1152, 128))] = wv_in[...].astype(BF)
    me.met()
    steps.next()
    load_x = me.move(x_hbm, x)
    load_wo = me.move(wo_hbm, wo_in)
    load_w1 = me.move(w1_hbm_in, w1_in)
    load_w2 = me.move(w2_hbm_in, w2_in)
    load_gy = me.move(gy_hbm, gy)
    load_wo.wait()
    wot[own] = wo_in[...].astype(BF)
    load_w1.wait()
    for j in range(4):
        w1[(j, *own)] = w1_in[:, pl.ds(1024 * j, 1024)].astype(BF)
    load_w2.wait()
    for k in range(4):
        w2[(k, *own)] = w2_in[:, pl.ds(256 * k, 256)].astype(BF)
    steps.next(2)

    first_pos = me.y * rows

    @pl.loop(0, rows // 64)
    def _(t):
        at = pl.multiple_of(t * 64, 64)
        query_pos = first_pos + at + lax.broadcasted_iota(jnp.int32, (64, 2 * rows), 0)
        key_pos = lax.broadcasted_iota(jnp.int32, (64, 2 * rows), 1)
        visible = (key_pos <= query_pos) | (key_pos < prefix_ref[0])
        bias[pl.ds(at, 64), :] = jnp.where(visible, 0.0, -1e30)

    load_x.wait()
    load_gy.wait()
    steps.until(s4, 0)

    for kind in (0, 1):
        for zi in range(4):
            for xi in range(2):
                tile = jnp.zeros((16, 128), F32)
                for ci in range(2):
                    for yi in range(2):
                        tile += wa[zi, xi, ci, yi, pl.ds(16 * kind, 16), pl.ds(1280, 128)].astype(F32)
                gain[kind, :, pl.ds(128 * (2 * zi + xi), 128)] = tile[:8]
    saves.append(me.move(gain, gain_hbm))

    @pl.loop(0, rows // 64)
    def _(t):
        r = pl.ds(pl.multiple_of(t * 64, 64), 64)
        values = x[r, :].astype(F32)
        factor = lax.rsqrt(jnp.mean(values * values, axis=-1, keepdims=True) + epsilon)
        n1[r, :] = (values * factor * gain[0, 0:1, :]).astype(BF)

    kv[me.y] = dot(
        n1[...], wa[:, :, :, :, :, pl.ds(1024, 256)].reshape(width, 256), 1, 0
    ).astype(BF)
    me.send(kv.at[me.y], kv.at[me.y], PIECES * RECVS, me.yn, PIECES * SENDS_F)
    for i in range(2):
        steps.next()
        cols = pl.ds(512 * i, 512)
        q[:, cols] = dot(n1[...], wa[:, :, :, :, :, cols].reshape(width, 512), 1, 0).astype(BF)

    saves.append(me.move(n1, n1_hbm))
    saves.append(me.move(q, q_hbm))
    steps.next()
    me.arrived(kv.at[1 - me.y], PIECES * RECVS)
    saves.append(me.move(kv, kv_hbm))
    length = 2 * rows
    to_log2 = (DH ** -0.5) * 1.4426950408889634

    def head(h):
        cols = pl.ds(h * DH, DH)
        keys = kv[:, :, pl.ds(0, DH)].reshape(length, DH)
        vals = kv[:, :, pl.ds(DH, DH)].reshape(length, DH)
        for t in range(rows // 256):
            r = pl.ds(256 * t, 256)
            s = dot(q[r, cols], keys, 1, 1) * to_log2 + bias[r, :]
            e = jnp.exp2(s - jnp.max(s, axis=-1, keepdims=True))
            chances = (e * (1.0 / jnp.sum(e, axis=-1, keepdims=True))).astype(BF)
            p[(h // 2) % 2, pl.ds((h % 2) * rows + 256 * t, 256), :] = chances
            a[r, cols] = dot(chances, vals, 1, 0).astype(BF)

    p_saves = []
    for h in range(H):
        if h >= 4 and h % 2 == 0:
            p_saves[h // 2 - 2].wait()
        head(h)
        if h % 2:
            p_saves.append(me.move(p.at[(h // 2) % 2], p_hbm.at[h // 2]))
        steps.next()
    saves.extend(p_saves[2:])
    saves.append(me.move(a, a_hbm))
    steps.until(s4, 1)
    for i in range(2):
        cols = pl.ds(512 * i, 512)
        weight = wot[pl.ds(2 * i, 2)].reshape(512, width)
        hidden[:, cols] = x[:, cols].astype(F32) + dot(a[...], weight, 1, 1)
        steps.next()

    @pl.loop(0, rows // 64)
    def _(t):
        r = pl.ds(pl.multiple_of(t * 64, 64), 64)
        values = hidden[r, :]
        factor = lax.rsqrt(jnp.mean(values * values, axis=-1, keepdims=True) + epsilon)
        n2[r, :] = (values * factor * gain[1, 0:1, :]).astype(BF)

    saves.append(me.move(hidden, hidden_hbm))
    saves.append(me.move(n2, n2_hbm))
    steps.next()

    def down_grad_out(j):
        for t in (2 * j, 2 * j + 1):
            cols = pl.ds(pl.multiple_of((2 * t + 1 - me.c) * 256, 256), 256)
            down_out[t] = dot(z[:, cols], gy[...], 0, 0).astype(BF)
        at = pl.ds(2 * j, 2)
        me.send(down_out.at[at], down_in.at[at], PIECES * RECVS + 1 + j, me.cn, PIECES * SENDS_F + 1 + j)

    def down_grad_own(j):
        me.arrived(down_in.at[pl.ds(2 * j, 2)], PIECES * RECVS + 1 + j)
        for t in (2 * j, 2 * j + 1):
            cols = pl.ds(pl.multiple_of((2 * t + me.c) * 256, 256), 256)
            down_in[t] = (dot(z[:, cols], gy[...], 0, 0) + down_in[t].astype(F32)).astype(BF)

    def down(k):
        cols = pl.ds(256 * k, 256)
        for t in range(2):
            r = pl.ds(256 * t, 256)
            y = dot(z[r, :], w2[k].reshape(4096, 256), 1, 0)
            out[r, cols] = (hidden[r, cols] + y).astype(BF)

    for j in range(4):
        steps.until(s4, 2 + j)
        for i in range(2):
            cols, to = pl.ds(512 * i, 512), pl.ds(1024 * j + 512 * i, 512)
            u = dot(n2[...], w1[j, :, :, :, :, :, cols].reshape(width, 512), 1, 0)
            active, steep = gelu_parts(u)
            z[:, to] = active.astype(BF)
            slope[:, to] = steep.astype(BF)
            steps.next()
        down_grad_out(j)
        steps.next()
        if j:
            down_grad_own(j - 1)
            steps.next()
    saves.append(me.move(slope, slope_hbm))
    steps.until(s4, 6)
    down_grad_own(3)
    saves.append(me.move(down_in, down_hbm))
    steps.next()
    down(0)
    for k in (1, 2, 3):
        steps.until(s4, 6 + k)
        down(k)
        if k == 2:
            saves.append(me.move(out.at[:, pl.ds(0, 768)], out_hbm.at[:, pl.ds(0, 768)]))
    steps.rest()
    saves.append(me.move(out.at[:, pl.ds(768, 256)], out_hbm.at[:, pl.ds(768, 256)]))
    for copy in saves:
        copy.wait()
    for i in range(PIECES):
        first, second, _ = shares(i)
        one, four = (0, 0, 0), (every, 0, every)
        for group, at in (
            (0, (pl.ds(0, 2), *one, *first)),
            (1, (pl.ds(0, 3), *four, *first)),
            (2, (every, every, 0)),
            (5, (pl.ds(0, 2), *four, *second)),
            (6, (pl.ds(0, 3), *one, *second)),
        ):
            me.left(views[i].at[at], i * SENDS_F + group)

    @pl.when(inner)
    def _():
        for i in range(PIECES):
            first, second, _ = shares(i)
            me.left(views[i].at[(pl.ds(0, 2), 0, 0, 0) + first], i * SENDS_F + 3)
            me.left(views[i].at[(pl.ds(0, 2), every, 0, every) + second], i * SENDS_F + 4)

    me.left(kv.at[me.y], PIECES * SENDS_F)
    for j in range(4):
        me.left(down_out.at[pl.ds(2 * j, 2)], PIECES * SENDS_F + 1 + j)


def backward_kernel(
    x_hbm, gy_hbm, gain_hbm, w2_hbm, w1_hbm, wa_hbm, wot_hbm, n1_hbm, q_hbm, kv_hbm, a_hbm, hidden_hbm,
    n2_hbm, slope_hbm, p_hbm, down_hbm,
    grad_x_hbm, g2_ref, g1_ref, go_ref, ga_ref,
    gy, n2, hidden, gn, a, q, kv, gain, wbuf, gu, wkv, att, sums, kvsum, kvout, kvin,
    down, pup, pproj, patt, pair_up, pair_att, diag2, diag1, diaga, side2, side1, sidea, line2, line1, linea,
    plane2, plane1, planea,
    send_sems, recv_sems, local_sems,
):
    me = Place(send_sems, recv_sems, local_sems)
    rows, width = gy.shape
    length = 2 * rows
    me.greet()
    load_down = [
        me.move(down_hbm.at[:, :, :, :, pl.ds(256 * k, 256)], down.at[:, :, :, :, pl.ds(256 * k, 256)])
        for k in range(4)
    ]
    load_gy = me.move(gy_hbm, gy)
    load_w2 = [me.move(w2_hbm.at[j], wbuf.at[j]) for j in range(2)]
    load_slope = [me.move(slope_hbm.at[:, pl.ds(1024 * j, 1024)], gu.at[j]) for j in range(2)]
    load_n2 = me.move(n2_hbm, n2)
    load_w1 = [me.move(w1_hbm.at[j], wbuf.at[2 + j]) for j in range(2)]
    load_rest = [
        me.move(src, dst)
        for src, dst in (
            (hidden_hbm, hidden), (gain_hbm, gain), (a_hbm, a), (q_hbm, q), (kv_hbm, kv),
            (wa_hbm.at[:, pl.ds(1024, 256)], wkv),
        )
    ]

    def source(i):
        return pup.at[i - 4] if i < 8 else pproj if i == 8 else patt

    def pair(i):
        return pair_up.at[i - 4] if i < 9 else pair_att

    def part(i, zi, xi, yi, at):
        if i < 4:
            return down.at[zi, xi, yi, at[0], pl.ds(256 * i + at[1].start, at[1].size)]
        return source(i).at[(zi, xi, me.c, yi) + at]

    def group(i, two, one, last):
        return two.at[i] if i < 4 else one.at[i - 4] if i < 9 else last

    def cut_of(i):
        return cut(*((128, 256) if i < 4 else (32, 1024) if i < 9 else (32, 1408)))

    every = slice(None)
    given = set(range(4))

    def send(src, dst, i, recv, device, to):
        me.send(src, dst, i * RECVS + recv, device, i * SENDS + to)

    def came(like, i, recv):
        me.arrived(like, i * RECVS + recv)

    def t0(i):
        send(source(i).at[:, :, 1 - me.c], pair(i), i, 0, me.cn, 2)
        given.add(i)

    def t1(i):
        first, second, (low, high) = cut_of(i)
        diag, plane = group(i, diag2, diag1, diaga), group(i, plane2, plane1, planea)
        if i < 4:
            load_down[i].wait()
        else:
            total, term = source(i), pair(i)
            came(term, i, 0)

            @pl.loop(0, 4)
            def _(zi):
                for xi in range(2):
                    total[zi, xi, me.c] = total[zi, xi, me.c] + term[zi, xi]

        if i not in SHIFT_B:
            send(part(i, every, 1 - me.x, 1 - me.y, low), diag.at[(every,) + low], i, 1, me.yn, 1)
        else:
            high = first
        send(part(i, every, 1 - me.x, 1 - me.y, high), diag.at[(every,) + high], i, 1, me.xn, 1)
        for step in (1, 3, 2):
            send(part(i, me.z_to(step), every, every, second), plane.at[step - 1], i, 2, me.zn(step), 1)

    def t2(i):
        first, second, (low, high) = cut_of(i)
        diag, plane = group(i, diag2, diag1, diaga), group(i, plane2, plane1, planea)
        side = group(i, side2, side1, sidea)
        came(diag.at[(every,) + first], i, 1)
        for step in (1, 3, 2, 0):
            zi = me.z_to(step)
            by_y, by_x = (1 - me.x, me.y, low), (me.x, 1 - me.y, first if i in SHIFT_B else high)
            for xi, yi, half in ((by_x,) if i in SHIFT_B else (by_y, by_x)):
                mine = part(i, zi, xi, yi, half)
                mine[...] = mine[...] + diag[(zi,) + half]
            recv = 2 + step if step else 6
            send(part(i, zi, 1 - me.x, me.y, first), side.at[(0, zi) + first], i, recv, me.xn, 1)
            send(part(i, zi, me.x, 1 - me.y, first), side.at[(1, zi) + first], i, recv, me.yn, 1)
        came(plane, i, 2)
        for xi in range(2):
            for yi in range(2):
                mine = part(i, me.z, xi, yi, second)
                total = mine[...].astype(F32)
                for step in range(3):
                    total += plane[step, xi, yi].astype(F32)
                mine[...] = total.astype(BF)
        send(
            part(i, me.z, 1 - me.x, 1 - me.y, second), diag.at[(me.z,) + second], i, 7,
            me.xn if i % 2 else me.yn, 0,
        )

    def t3(i):
        first, second, _ = cut_of(i)
        diag, side = group(i, diag2, diag1, diaga), group(i, side2, side1, sidea)
        line = group(i, line2, line1, linea)
        for step in (1, 3, 2):
            zi = me.z_to(step)
            came(side.at[(every, zi) + first], i, 2 + step)
            mine = part(i, zi, me.x, me.y, first)
            total = mine[...].astype(F32) + side[(0, zi) + first].astype(F32) + side[(1, zi) + first].astype(F32)
            mine[...] = total.astype(BF)
            send(mine, line.at[(step - 1,) + first], i, 8, me.zn(step), 0)
        came(diag.at[(me.z,) + second], i, 7)
        mine = part(i, me.z, *((me.x, 1 - me.y) if i % 2 else (1 - me.x, me.y)), second)
        mine[...] = mine[...] + diag[(me.z,) + second]
        send(part(i, me.z, 1 - me.x, me.y, second), side.at[(0, me.z) + second], i, 9, me.xn, 0)
        send(part(i, me.z, me.x, 1 - me.y, second), side.at[(1, me.z) + second], i, 9, me.yn, 0)

    def t4(i):
        first, second, _ = cut_of(i)
        side, line = group(i, side2, side1, sidea), group(i, line2, line1, linea)
        came(side.at[(every, me.z) + first], i, 6)
        came(line.at[(every,) + first], i, 8)
        came(side.at[(every, me.z) + second], i, 9)
        out, shift = (
            (g2_ref, 256 * i) if i < 4 else (g1_ref, 1024 * (i - 4)) if i < 8 else (go_ref, 0) if i == 8 else (ga_ref, 0)
        )
        for at in (first, second):
            total = part(i, me.z, me.x, me.y, at)[...].astype(F32)
            total += side[(0, me.z) + at].astype(F32) + side[(1, me.z) + at].astype(F32)
            if at is first:
                for step in range(3):
                    total += line[(step,) + first].astype(F32)
            out[at[0], pl.ds(shift + at[1].start, at[1].size)] = total

    def order():
        yield t1, 0
        for k in range(PIECES + 2):
            for step, i in ((t1, k + 1), (t2, k), (t3, k - 1), (t4, k - 2)):
                if 0 <= i < PIECES:
                    yield step, i

    steps = Steps((step, i, lambda step=step, i=i: step is not t1 or i in given) for step, i in order())
    me.met()
    steps.next()

    def feed_forward(j):
        slot = j % 2
        load_w2[j].wait()
        load_slope[j].wait()
        for i in range(2):
            cols = pl.ds(512 * i, 512)
            grad_active = dot(gy[...], wbuf[slot, cols, :], 1, 1)
            gu[slot, :, cols] = (grad_active * gu[slot, :, cols].astype(F32)).astype(BF)
        steps.next()
        if j < 2:
            load_w2.append(me.move(w2_hbm.at[j + 2], wbuf.at[slot]))
        elif j == 2:
            load_w2.append(me.move(wot_hbm, wbuf.at[0]))
        else:
            load_w2.append(me.move(p_hbm.at[1], wbuf.at[1]))
        for i in range(2):
            term = dot(n2[:, pl.ds(512 * i, 512)], gu[slot], 0, 0)
            pup[j, pl.ds(2 * i, 2)] = term.reshape(2, 2, 2, 2, 32, 1024).astype(BF)
        t0(4 + j)
        steps.next()
        load_w1[j].wait()
        for i in range(2):
            cols = pl.ds(512 * i, 512)
            term = dot(gu[slot], wbuf[2 + slot, cols, :], 1, 1)
            if j == 0:
                gn[:, cols] = term
            else:
                gn[:, cols] = gn[:, cols] + term
        if j < 2:
            load_slope.append(me.move(slope_hbm.at[:, pl.ds(1024 * (j + 2), 1024)], gu.at[slot]))
            load_w1.append(me.move(w1_hbm.at[j + 2], wbuf.at[2 + slot]))
        else:
            load_w1.append(me.move(p_hbm.at[(0, 2)[j - 2]], wbuf.at[2 + slot]))
        steps.next()

    load_gy.wait()
    load_n2.wait()
    for j in range(4):
        feed_forward(j)
    load_x = me.move(x_hbm, n2)
    for copy in load_rest:
        copy.wait()

    sums[...] = jnp.zeros_like(sums)

    @pl.loop(0, rows // 64)
    def _(t):
        r = pl.ds(pl.multiple_of(t * 64, 64), 64)
        grad, values = gn[r, :], hidden[r, :]
        factor = lax.rsqrt(jnp.mean(values * values, axis=-1, keepdims=True) + epsilon)
        scaled = grad * gain[1, 0:1, :]
        middle = jnp.mean(scaled * values, axis=-1, keepdims=True)
        total = gy[r, :].astype(F32) + factor * scaled - values * (factor * factor * factor * middle)
        sums[1] += jnp.sum((grad * values * factor).reshape(8, 8, width), axis=0)
        gn[r, :] = total
        gy[r, :] = total.astype(BF)

    for i in range(2):
        term = dot(gy[:, pl.ds(512 * i, 512)], a[...], 0, 0)
        pproj[pl.ds(2 * i, 2)] = term.reshape(2, 2, 2, 2, 32, width).astype(BF)
    t0(8)
    steps.next()
    load_w2[4].wait()
    for i in range(2):
        cols = pl.ds(512 * i, 512)
        att[:, cols] = dot(gy[...], wbuf[0, :, cols], 1, 0).astype(BF)
    load_p3 = me.move(p_hbm.at[3], wbuf.at[0])
    load_n1 = me.move(n1_hbm, gy)
    steps.next()
    kvsum[...] = jnp.zeros_like(kvsum)
    scale = DH ** -0.5

    def head(h):
        slot = (2, 1, 3, 0)[h // 2]
        cols = pl.ds(h * DH, DH)
        keys = kv[:, :, pl.ds(0, DH)].reshape(length, DH)
        vals = kv[:, :, pl.ds(DH, DH)].reshape(length, DH)
        for t in range(rows // 256):
            r = pl.ds(256 * t, 256)
            grad = att[r, cols]
            chances = wbuf[slot, pl.ds((h % 2) * rows + 256 * t, 256), :]
            grad_chances = dot(grad, vals, 1, 1)
            wide = chances.astype(F32)
            center = jnp.sum(wide * grad_chances, axis=-1, keepdims=True)
            grad_scores = (wide * (grad_chances - center)).astype(BF)
            kvsum[0] += dot(q[r, cols], grad_scores, 0, 0)
            kvsum[1] += dot(grad, chances, 0, 0)
            att[r, cols] = (dot(grad_scores, keys, 1, 0) * scale).astype(BF)

    load_p = (load_w1[4], load_w2[5], load_w1[5], load_p3)
    for h in range(H):
        if h % 2 == 0:
            load_p[h // 2].wait()
        head(h)
        if h == 1:
            load_wq = me.move(wa_hbm.at[:, pl.ds(0, 1024)], wbuf.at[2])
        steps.next()
    for half in (0, 1):
        cols = pl.ds(half * rows, rows)
        kvout[half, :, pl.ds(0, DH)] = (kvsum[0, :, cols] * scale).T.astype(BF)
        kvout[half, :, pl.ds(DH, DH)] = kvsum[1, :, cols].T.astype(BF)
    me.send(kvout.at[1 - me.y], kvin, PIECES * RECVS, me.yn, PIECES * SENDS)
    load_n1.wait()
    for i in range(2):
        term = dot(gy[:, pl.ds(512 * i, 512)], att[...], 0, 0)
        patt[pl.ds(2 * i, 2), :, :, :, :, pl.ds(0, 1024)] = term.reshape(2, 2, 2, 2, 32, width).astype(BF)
    steps.next()
    me.arrived(kvin, PIECES * RECVS)
    kvin[...] = kvin[...] + kvout[me.y]
    for i in range(2):
        term = dot(gy[:, pl.ds(512 * i, 512)], kvin[...], 0, 0)
        patt[pl.ds(2 * i, 2), :, :, :, :, pl.ds(1024, 256)] = term.reshape(2, 2, 2, 2, 32, 256).astype(BF)
    load_wq.wait()
    for i in range(2):
        cols = pl.ds(512 * i, 512)
        hidden[:, cols] = dot(att[...], wbuf[2, cols, :], 1, 1) + dot(kvin[...], wkv[cols, :], 1, 1)
        steps.next()
    load_x.wait()

    @pl.loop(0, rows // 64)
    def _(t):
        r = pl.ds(pl.multiple_of(t * 64, 64), 64)
        grad, values = hidden[r, :], n2[r, :].astype(F32)
        factor = lax.rsqrt(jnp.mean(values * values, axis=-1, keepdims=True) + epsilon)
        scaled = grad * gain[0, 0:1, :]
        middle = jnp.mean(scaled * values, axis=-1, keepdims=True)
        sums[0] += jnp.sum((grad * values * factor).reshape(8, 8, width), axis=0)
        gn[r, :] = gn[r, :] + factor * scaled - values * (factor * factor * factor * middle)

    save_x = me.move(gn, grad_x_hbm)
    for kind in (0, 1):
        row = jnp.sum(sums[kind], axis=0, keepdims=True)
        for zi in range(4):
            for xi in range(2):
                lanes = slice(128 * (2 * zi + xi), 128 * (2 * zi + xi) + 128)
                tile = jnp.broadcast_to(row[:, lanes], (16, 128)).astype(BF)
                for ci in range(2):
                    for yi in range(2):
                        patt[zi, xi, ci, yi, pl.ds(16 * kind, 16), pl.ds(1280, 128)] = tile
    t0(9)
    steps.rest()
    save_x.wait()
    for i in range(PIECES):
        if i < 4:
            at = (every, pl.ds(256 * i, 256))
            me.left(down.at[(pl.ds(0, 3), 0, 0) + at], i * SENDS)
            me.left(down.at[(pl.ds(0, 3), every, every) + at], i * SENDS + 1)
        else:
            me.left(source(i).at[pl.ds(0, 3), 0, 0, 0], i * SENDS)
            me.left(source(i).at[pl.ds(0, 3), :, 0], i * SENDS + 1)
            me.left(source(i).at[:, :, 0], i * SENDS + 2)
    me.left(kvin, PIECES * SENDS)


def on_grid(
    tokens, cotangent, prefix, attention_gain, query_weight, key_weight, value_weight, projection_weight,
    feedforward_gain, up_weight, down_weight,
):
    rows, width = tokens.shape[1:]
    vmem, hbm = pl.BlockSpec(memory_space=pltpu.VMEM), pl.BlockSpec(memory_space=pl.ANY)
    smem = pl.BlockSpec(memory_space=pltpu.SMEM)
    x, gy = tokens.reshape(rows, width), cotangent.reshape(rows, width)
    sds = jax.ShapeDtypeStruct
    grid = (4, 2, 2, 2)
    send_sems_f, send_sems, recv_sems = (
        pltpu.SemaphoreType.DMA((PIECES * n + EXTRA,)) for n in (SENDS_F, SENDS, RECVS)
    )
    length = 2 * rows
    out = pl.pallas_call(
        forward_kernel,
        out_shape=(
            sds((rows, width), BF),
            sds((*grid, 128, 1024), BF),
            sds((4, *grid, 32, 1024), BF),
            sds((*grid, 32, 1408), BF),
            sds((*grid, 32, 1024), BF),
            sds((2, 8, width), F32),
            sds((rows, width), BF),
            sds((rows, width), BF),
            sds((2, rows, 256), BF),
            sds((rows, width), BF),
            sds((rows, width), F32),
            sds((rows, width), BF),
            sds((rows, 4096), BF),
            sds((4, 2 * rows, length), BF),
            sds((8, 256, width), BF),
        ),
        in_specs=[smem] + [hbm] * 5 + [vmem] * 2 + [hbm] * 3,
        out_specs=[hbm] * 15,
        scratch_shapes=[
            pltpu.VMEM((*grid, 32, 1408), BF),
            pltpu.VMEM((*grid, 32, 1024), BF),
            pltpu.VMEM((4, *grid, 32, 1024), BF),
            pltpu.VMEM((4, *grid, 128, 256), BF),
            pltpu.VMEM((rows, width), BF),
            pltpu.VMEM((rows, width), BF),
            pltpu.VMEM((rows, width), BF),
            pltpu.VMEM((rows, width), BF),
            pltpu.VMEM((2, rows, 256), BF),
            pltpu.VMEM((rows, width), BF),
            pltpu.VMEM((rows, width), F32),
            pltpu.VMEM((rows, width), BF),
            pltpu.VMEM((rows, 4096), BF),
            pltpu.VMEM((rows, 4096), BF),
            pltpu.VMEM((2, 2 * rows, length), BF),
            pltpu.VMEM((rows, length), F32),
            pltpu.VMEM((2, 8, width), F32),
            pltpu.VMEM((8, 256, width), BF),
            pltpu.VMEM((8, 256, width), BF),
            pltpu.VMEM((rows, width), BF),
            pltpu.VMEM(query_weight.shape, F32),
            pltpu.VMEM(key_weight.shape, F32),
            pltpu.VMEM(value_weight.shape, F32),
            pltpu.VMEM((32, width), F32),
            pltpu.VMEM(up_weight.shape, F32),
            pltpu.VMEM(down_weight.shape, F32),
            send_sems_f,
            recv_sems,
            pltpu.SemaphoreType.DMA((40,)),
        ],
        compiler_params=pltpu.CompilerParams(
            collective_id=0, has_side_effects=True, vmem_limit_bytes=VMEM_LIMIT
        ),
    )(
        prefix, x, gy, query_weight, key_weight, value_weight, attention_gain.reshape(1, 32),
        feedforward_gain.reshape(1, 32), projection_weight.T, up_weight, down_weight,
    )
    layer_output, w2, w1, wa, wot, gain, n1, q, kv, a, hidden, n2, slope, p, down = out
    grad_x, g2, g1, go, ga = pl.pallas_call(
        backward_kernel,
        out_shape=(
            sds((rows, width), F32),
            sds((128, 1024), F32),
            sds((32, 4096), F32),
            sds((32, 1024), F32),
            sds((32, 1408), F32),
        ),
        in_specs=[hbm] * 16,
        out_specs=[hbm] + [vmem] * 4,
        scratch_shapes=[
            pltpu.VMEM((rows, width), BF),
            pltpu.VMEM((rows, width), BF),
            pltpu.VMEM((rows, width), F32),
            pltpu.VMEM((rows, width), F32),
            pltpu.VMEM((rows, width), BF),
            pltpu.VMEM((rows, width), BF),
            pltpu.VMEM((2, rows, 256), BF),
            pltpu.VMEM((2, 8, width), F32),
            pltpu.VMEM((4, 1024, 1024), BF),
            pltpu.VMEM((2, rows, 1024), BF),
            pltpu.VMEM((width, 256), BF),
            pltpu.VMEM((rows, width), BF),
            pltpu.VMEM((2, 8, width), F32),
            pltpu.VMEM((2, DH, length), F32),
            pltpu.VMEM((2, rows, 256), BF),
            pltpu.VMEM((rows, 256), BF),
            pltpu.VMEM((4, 2, 2, 128, 1024), BF),
            pltpu.VMEM((4, *grid, 32, 1024), BF),
            pltpu.VMEM((*grid, 32, 1024), BF),
            pltpu.VMEM((*grid, 32, 1408), BF),
            pltpu.VMEM((5, 4, 2, 2, 32, 1024), BF),
            pltpu.VMEM((4, 2, 2, 32, 1408), BF),
            pltpu.VMEM((4, 4, 128, 256), BF), pltpu.VMEM((5, 4, 32, 1024), BF), pltpu.VMEM((4, 32, 1408), BF),
            pltpu.VMEM((4, 2, 4, 128, 256), BF), pltpu.VMEM((5, 2, 4, 32, 1024), BF), pltpu.VMEM((2, 4, 32, 1408), BF),
            pltpu.VMEM((4, 3, 128, 256), BF), pltpu.VMEM((5, 3, 32, 1024), BF), pltpu.VMEM((3, 32, 1408), BF),
            pltpu.VMEM((4, 3, 2, 2, 16, 256), BF), pltpu.VMEM((5, 3, 2, 2, 32, 128), BF), pltpu.VMEM((3, 2, 2, 32, 128), BF),
            send_sems,
            recv_sems,
            pltpu.SemaphoreType.DMA((40,)),
        ],
        compiler_params=pltpu.CompilerParams(
            collective_id=1, has_side_effects=True, vmem_limit_bytes=VMEM_LIMIT
        ),
    )(
        x, gy, gain, w2.reshape(4, 1024, 1024), w1.reshape(4, 1024, 1024), wa.reshape(1024, 1408), wot.reshape(1024, 1024),
        n1, q, kv, a, hidden, n2, slope, p, down.reshape(4, 2, 2, 128, 1024),
    )
    layer_output, grad_x, g1_gain, gq, gk, gv, gp, g2_gain, g1, g2 = pl.pallas_call(
        hand_out,
        out_shape=(
            sds((rows, width), BF),
            sds((rows, width), F32),
            sds((1, 32), F32),
            sds((32, 1024), F32),
            sds((32, 128), F32),
            sds((32, 128), F32),
            sds((32, 1024), F32),
            sds((1, 32), F32),
            sds((32, 4096), F32),
            sds((128, 1024), F32),
        ),
        in_specs=[hbm] * 6,
        out_specs=[hbm, hbm, vmem, hbm, hbm, hbm, hbm, vmem, hbm, hbm],
        scratch_shapes=[
            pltpu.VMEM((rows, width), BF),
            pltpu.VMEM((rows, width), F32),
            pltpu.VMEM((32, 1408), F32),
            pltpu.VMEM((32, 1024), F32),
            pltpu.VMEM((32, 4096), F32),
            pltpu.VMEM((128, 1024), F32),
            pltpu.SemaphoreType.DMA((24,)),
        ],
        compiler_params=pltpu.CompilerParams(vmem_limit_bytes=VMEM_LIMIT),
    )(layer_output, grad_x, ga, go, g1, g2)
    return (
        layer_output.reshape(tokens.shape),
        grad_x.reshape(tokens.shape),
        g1_gain.reshape(32),
        gq,
        gk,
        gv,
        gp.T,
        g2_gain.reshape(32),
        g1,
        g2,
    )


def hand_out(
    y_in, x_in, a_in, p_in, up_in, down_in,
    y_out, x_out, g1_out, q_out, k_out, v_out, p_out, g2_out, up_out, down_out,
    y, x, a, p, up, down, sems,
):
    started = 0

    def move(src, dst):
        nonlocal started
        copy = pltpu.make_async_copy(src, dst, sems.at[started])
        started += 1
        copy.start()
        return copy

    quarters = [pl.ds(i * (x.shape[0] // 4), x.shape[0] // 4) for i in range(4)]
    moves = [(x_in.at[r], x.at[r], x_out.at[r]) for r in quarters]
    moves += [(y_in, y, y_out), (up_in, up, up_out), (down_in, down, down_out), (p_in, p, p_out)]
    loads = [move(a_in, a)] + [move(src, by) for src, by, _ in moves]
    stores = []
    loads[0].wait()
    for cols, out in ((pl.ds(0, 1024), q_out), (pl.ds(1024, 128), k_out), (pl.ds(1152, 128), v_out)):
        stores.append(move(a.at[:, cols], out))
    for load, (_, by, dst) in zip(loads[1:], moves):
        load.wait()
        stores.append(move(by, dst))
    quarter = lax.rem(lax.axis_index("dp"), 2) * 2 + lax.axis_index("seq")
    for row, out in ((0, g1_out), (16, g2_out)):
        for k in range(4):
            @pl.when(quarter == k)
            def _():
                out[...] = a[row : row + 1, 1280 + 32 * k : 1312 + 32 * k]
    for copy in stores:
        copy.wait()


def root_norm(values, gain):
    factor = lax.rsqrt(jnp.mean(values * values, axis=-1, keepdims=True) + epsilon)
    return values * factor * gain


def smooth_gate(values):
    return jax.nn.gelu(values, approximate=True)


def product(left, right):
    return jnp.dot(left, right, preferred_element_type=jnp.float32)


def inner_rows(left, right):
    return lax.dot_general(
        left, right, (((0,), (0,)), ((), ())), preferred_element_type=jnp.float32
    )


def outer_rows(left, right):
    return lax.dot_general(
        left, right, (((1,), (1,)), ((), ())), preferred_element_type=jnp.float32
    )


def local(
    tokens,
    cotangent,
    prefix,
    attention_gain,
    query_weight,
    key_weight,
    value_weight,
    projection_weight,
    feedforward_gain,
    up_weight,
    down_weight,
):
    seqs_here, span_len, model_width = tokens.shape
    length = span_len * lax.axis_size("seq")
    row_count = seqs_here * span_len
    block_len = min(64, span_len)
    block_count = span_len // block_len
    score_scale = DH ** (-0.5)
    gain_low = attention_gain.astype(jnp.bfloat16)
    query_low = query_weight.astype(jnp.bfloat16)
    key_low = key_weight.astype(jnp.bfloat16)
    value_low = value_weight.astype(jnp.bfloat16)
    projection_low = projection_weight.astype(jnp.bfloat16)
    second_low = feedforward_gain.astype(jnp.bfloat16)
    up_low = up_weight.astype(jnp.bfloat16)
    down_low = down_weight.astype(jnp.bfloat16)
    gathered = (
        lax.all_gather(gain_low, ("dp", "seq"), axis=0, tiled=True),
        lax.all_gather(query_low, ("dp", "seq"), axis=0, tiled=True),
        lax.all_gather(key_low, ("dp", "seq"), axis=0, tiled=True),
        lax.all_gather(value_low, ("dp", "seq"), axis=0, tiled=True),
        lax.all_gather(projection_low, ("dp", "seq"), axis=1, tiled=True),
        lax.all_gather(second_low, ("dp", "seq"), axis=0, tiled=True),
        lax.all_gather(up_low, ("dp", "seq"), axis=0, tiled=True),
        lax.all_gather(down_low, ("dp", "seq"), axis=0, tiled=True),
    )
    gain_one, query_full, key_full, value_full, projection_full, gain_two, up_full, down_full = (
        gathered
    )
    inputs = tokens.reshape(row_count, model_width).astype(jnp.float32)
    gain_first = gain_one.astype(jnp.float32)
    normed = root_norm(inputs, gain_first).astype(jnp.bfloat16)
    queries = product(normed, query_full).astype(jnp.bfloat16)
    pair_weight = jnp.concatenate([key_full, value_full], axis=1)
    pair_rows = product(normed, pair_weight).astype(jnp.bfloat16)
    key_own = pair_rows[:, :DH].reshape(seqs_here, span_len, DH)
    value_own = pair_rows[:, DH:].reshape(seqs_here, span_len, DH)
    key_all, value_all = (
        lax.all_gather(key_own, "seq", axis=1, tiled=True),
        lax.all_gather(value_own, "seq", axis=1, tiled=True),
    )
    query_pos = lax.axis_index("seq") * span_len + jnp.arange(span_len, dtype=jnp.int32)
    pos_blocks = query_pos.reshape(block_count, block_len)
    key_pos = jnp.arange(length, dtype=jnp.int32)

    def masked_scores(query_block, key_rows, positions, prefix_len):
        flat = query_block.reshape(block_len * H, DH)
        scores = (outer_rows(flat, key_rows) * score_scale).reshape(block_len, H, length)
        visible = (key_pos[None, :] <= positions[:, None]) | (key_pos[None, :] < prefix_len)
        return jnp.where(visible[:, None, :], scores, masked_score)

    def forward_sequence(members):
        query_blocks, key_rows, value_rows, prefix_len = members

        def forward_block(pieces):
            query_block, positions = pieces
            scores = masked_scores(query_block, key_rows, positions, prefix_len)
            maxima = jnp.max(scores, axis=-1, keepdims=True)
            exponent = jnp.exp(scores - maxima)
            totals = jnp.sum(exponent, axis=-1, keepdims=True)
            chances = (exponent / totals).astype(jnp.bfloat16)
            mixed = product(chances.reshape(block_len * H, length), value_rows)
            return (
                mixed.reshape(block_len, H * DH).astype(jnp.bfloat16),
                (maxima + jnp.log(totals))[..., 0],
            )

        return lax.map(forward_block, (query_blocks, pos_blocks))

    query_seq = queries.reshape(seqs_here, block_count, block_len, H, DH)
    attended, log_totals = lax.map(forward_sequence, (query_seq, key_all, value_all, prefix))
    attended = attended.reshape(row_count, H * DH)
    hidden = inputs + product(attended, projection_full)
    gain_second = gain_two.astype(jnp.float32)
    normed_two = root_norm(hidden, gain_second).astype(jnp.bfloat16)
    before = product(normed_two, up_full)
    active = smooth_gate(before).astype(jnp.bfloat16)
    layer_output = (hidden + product(active, down_full)).astype(jnp.bfloat16)
    gathered = (
        lax.all_gather(gain_low, ("dp", "seq"), axis=0, tiled=True),
        lax.all_gather(query_low, ("dp", "seq"), axis=0, tiled=True),
        lax.all_gather(key_low, ("dp", "seq"), axis=0, tiled=True),
        lax.all_gather(value_low, ("dp", "seq"), axis=0, tiled=True),
        lax.all_gather(projection_low, ("dp", "seq"), axis=1, tiled=True),
        lax.all_gather(second_low, ("dp", "seq"), axis=0, tiled=True),
        lax.all_gather(up_low, ("dp", "seq"), axis=0, tiled=True),
        lax.all_gather(down_low, ("dp", "seq"), axis=0, tiled=True),
    )
    gain_one, query_full, key_full, value_full, projection_full, gain_two, up_full, down_full = (
        gathered
    )
    gain_first = gain_one.astype(jnp.float32)
    gain_second = gain_two.astype(jnp.float32)
    pair_weight = jnp.concatenate([key_full, value_full], axis=1)
    grad_out = cotangent.reshape(row_count, model_width)
    grad_start = grad_out.astype(jnp.float32)
    down_grad = inner_rows(active, grad_out)
    grad_active = outer_rows(grad_out, down_full)
    _, gate_pull = jax.vjp(smooth_gate, before)
    grad_before = gate_pull(grad_active)[0].astype(jnp.bfloat16)
    up_grad = inner_rows(normed_two, grad_before)
    grad_normed_two = outer_rows(grad_before, up_full)
    _, second_pull = jax.vjp(root_norm, hidden, gain_second)
    grad_hidden_norm, feedforward_gain_grad = second_pull(grad_normed_two)
    grad_hidden = grad_start + grad_hidden_norm
    grad_branch = grad_hidden.astype(jnp.bfloat16)
    projection_grad = inner_rows(attended, grad_branch)
    grad_attended = outer_rows(grad_branch, projection_full).astype(jnp.bfloat16)
    key_all, value_all = (
        lax.all_gather(key_own, "seq", axis=1, tiled=True),
        lax.all_gather(value_own, "seq", axis=1, tiled=True),
    )
    grad_seq = grad_attended.reshape(seqs_here, block_count, block_len, H, DH)

    def backward_sequence(members):
        query_blocks, grad_blocks, total_blocks, key_rows, value_rows, prefix_len = members

        def backward_block(carry, pieces):
            key_sum, value_sum = carry
            query_block, grad_block, total_block, positions = pieces
            scores = masked_scores(query_block, key_rows, positions, prefix_len)
            chances = jnp.exp(scores - total_block[..., None])
            chance_low = chances.astype(jnp.bfloat16).reshape(block_len * H, length)
            grad_rows = grad_block.reshape(block_len * H, DH)
            query_rows = query_block.reshape(block_len * H, DH)
            grad_chances = outer_rows(grad_rows, value_rows).reshape(block_len, H, length)
            center = jnp.sum(chances * grad_chances, axis=-1, keepdims=True)
            grad_scores = (
                (chances * (grad_chances - center))
                .astype(jnp.bfloat16)
                .reshape(block_len * H, length)
            )
            grad_query = (product(grad_scores, key_rows) * score_scale).astype(jnp.bfloat16)
            key_sum = key_sum + inner_rows(grad_scores, query_rows) * score_scale
            value_sum = value_sum + inner_rows(chance_low, grad_rows)
            return ((key_sum, value_sum), grad_query.reshape(block_len, H * DH))

        empty_sum = jnp.zeros((length, DH), jnp.float32)
        (key_sum, value_sum), grad_queries = lax.scan(
            backward_block,
            (empty_sum, empty_sum),
            (query_blocks, grad_blocks, total_blocks, pos_blocks),
        )
        return (key_sum, value_sum, grad_queries)

    key_terms, value_terms, grad_queries = lax.map(
        backward_sequence, (query_seq, grad_seq, log_totals, key_all, value_all, prefix)
    )
    grad_keys, grad_values = (
        lax.psum_scatter(
            key_terms.astype(jnp.bfloat16), "seq", scatter_dimension=1, tiled=True
        ).astype(jnp.float32),
        lax.psum_scatter(
            value_terms.astype(jnp.bfloat16), "seq", scatter_dimension=1, tiled=True
        ).astype(jnp.float32),
    )
    grad_pair = jnp.concatenate(
        [grad_keys.reshape(row_count, DH), grad_values.reshape(row_count, DH)], axis=1
    ).astype(jnp.bfloat16)
    grad_query_rows = grad_queries.reshape(row_count, H * DH)
    query_grad = inner_rows(normed, grad_query_rows)
    pair_grad = inner_rows(normed, grad_pair)
    key_grad = pair_grad[:, :DH]
    value_grad = pair_grad[:, DH:]
    grad_normed = outer_rows(grad_query_rows, query_full) + outer_rows(grad_pair, pair_weight)
    _, first_pull = jax.vjp(root_norm, inputs, gain_first)
    grad_inputs_norm, attention_gain_grad = first_pull(grad_normed)
    input_grad = (grad_hidden + grad_inputs_norm).reshape(seqs_here, span_len, model_width)
    layer_output = layer_output.reshape(seqs_here, span_len, model_width)
    summed = (
        lax.psum_scatter(attention_gain_grad, ("dp", "seq"), scatter_dimension=0, tiled=True),
        lax.psum_scatter(query_grad, ("dp", "seq"), scatter_dimension=0, tiled=True),
        lax.psum_scatter(key_grad, ("dp", "seq"), scatter_dimension=0, tiled=True),
        lax.psum_scatter(value_grad, ("dp", "seq"), scatter_dimension=0, tiled=True),
        lax.psum_scatter(projection_grad, ("dp", "seq"), scatter_dimension=1, tiled=True),
        lax.psum_scatter(feedforward_gain_grad, ("dp", "seq"), scatter_dimension=0, tiled=True),
        lax.psum_scatter(up_grad, ("dp", "seq"), scatter_dimension=0, tiled=True),
        lax.psum_scatter(down_grad, ("dp", "seq"), scatter_dimension=0, tiled=True),
    )
    return (
        layer_output,
        input_grad,
        summed[0],
        summed[1],
        summed[2],
        summed[3],
        summed[4],
        summed[5],
        summed[6],
        summed[7],
    )


def fits(mesh, tokens, up_weight):
    return (
        mesh.shape["dp"] == 16
        and mesh.shape["seq"] == 2
        and tokens.shape == (16, 1024, 1024)
        and up_weight.shape == (1024, 4096)
    )


def solution(mesh):
    def layer(*args):
        return sharded(mesh, on_grid if fits(mesh, args[0], args[9]) else local)(*args)

    return layer


def sharded(mesh, part):
    return jax.shard_map(
        part,
        mesh=mesh,
        in_specs=(
            P("dp", "seq", None),
            P("dp", "seq", None),
            P("dp"),
            P(("dp", "seq")),
            P(("dp", "seq"), None),
            P(("dp", "seq"), None),
            P(("dp", "seq"), None),
            P(None, ("dp", "seq")),
            P(("dp", "seq")),
            P(("dp", "seq"), None),
            P(("dp", "seq"), None),
        ),
        out_specs=(
            P("dp", "seq", None),
            P("dp", "seq", None),
            P(("dp", "seq")),
            P(("dp", "seq"), None),
            P(("dp", "seq"), None),
            P(("dp", "seq"), None),
            P(None, ("dp", "seq")),
            P(("dp", "seq")),
            P(("dp", "seq"), None),
            P(("dp", "seq"), None),
        ),
        check_vma=False,
    )
```
